32 devices in a mesh: dp: 8 (over z, y), mp: 4 (over x, core).
Axes of the slice: x: 2, y: 2, z: 4, core: 2. Of those that a mesh axis runs over, the one named last changes fastest.
Arguments:
- pixels: bfloat16 [32, 588, 1536], P('dp'), may hold values from -6 to 6
- visible: int32 [32, 147], P('dp'), may hold values from 0 to 587, as said below
- valid: int32 [32, 588, 256], P('dp'), may hold values 0 or 1
- row_dest: int32 [32, 147], P('dp'), may hold values from 0 to 592, as said below
- encoder_in: float32 [768, 7, 768], P('dp', None, 'mp'), may hold values from -0.21875 to 0.21875
- encoder_in_moment: float32 [768, 7, 768], P('dp', None, 'mp'), may hold values from -3.7252903e-08 to 3.7252903e-08
- encoder_in_second: float32 [768, 7, 768], P('dp', None, 'mp'), may hold values from 1.6837284e-16 to 6.671377e-16
- encoder_out: float32 [5, 768, 768], P(None, 'mp', 'dp'), may hold values from -0.15625 to 0.15625
- encoder_out_moment: float32 [5, 768, 768], P(None, 'mp', 'dp'), may hold values from -3.7252903e-08 to 3.7252903e-08
- encoder_out_second: float32 [5, 768, 768], P(None, 'mp', 'dp'), may hold values from 1.6837284e-16 to 6.671377e-16
- decoder_in: float32 [512, 7, 512], P('dp', None, 'mp'), may hold values from -0.25 to 0.25
- decoder_in_moment: float32 [512, 7, 512], P('dp', None, 'mp'), may hold values from -3.7252903e-08 to 3.7252903e-08
- decoder_in_second: float32 [512, 7, 512], P('dp', None, 'mp'), may hold values from 1.6837284e-16 to 6.671377e-16
- decoder_out: float32 [5, 512, 512], P(None, 'mp', 'dp'), may hold values from -0.1875 to 0.1875
- decoder_out_moment: float32 [5, 512, 512], P(None, 'mp', 'dp'), may hold values from -3.7252903e-08 to 3.7252903e-08
- decoder_out_second: float32 [5, 512, 512], P(None, 'mp', 'dp'), may hold values from 1.6837284e-16 to 6.671377e-16
- patch_embed: float32 [1536, 768], P('dp'), may hold values from -0.15625 to 0.15625
- patch_embed_moment: float32 [1536, 768], P('dp'), may hold values from -7.450581e-09 to 7.450581e-09
- patch_embed_second: float32 [1536, 768], P('dp'), may hold values from 6.671377e-18 to 2.6685508e-17
- decoder_embed: float32 [768, 512], P('dp'), may hold values from -0.21875 to 0.21875
- decoder_embed_moment: float32 [768, 512], P('dp'), may hold values from -3.7252903e-08 to 3.7252903e-08
- decoder_embed_second: float32 [768, 512], P('dp'), may hold values from 1.6837284e-16 to 6.671377e-16
- pixel_head: float32 [512, 1536], P('dp', 'mp'), may hold values from -0.25 to 0.25
- pixel_head_moment: float32 [512, 1536], P('dp', 'mp'), may hold values from -3.7252903e-08 to 3.7252903e-08
- pixel_head_second: float32 [512, 1536], P('dp', 'mp'), may hold values from 1.6837284e-16 to 6.671377e-16
- norm_params: float32 [8192], P('dp'), may hold values from -3 to 3
- norm_params_moment: float32 [8192], P('dp'), may hold values from -3.5762787e-07 to 3.5762787e-07
- norm_params_second: float32 [8192], P('dp'), may hold values from 1.2707385e-14 to 5.082954e-14
Outputs:
- loss_sum: float32 [], replicated
- valid_count: float32 [], replicated
- grad_norm: float32 [], replicated
- new_encoder_in: float32 [768, 7, 768], P('dp', None, 'mp')
- new_encoder_in_moment: float32 [768, 7, 768], P('dp', None, 'mp')
- new_encoder_in_second: float32 [768, 7, 768], P('dp', None, 'mp')
- new_encoder_out: float32 [5, 768, 768], P(None, 'mp', 'dp')
- new_encoder_out_moment: float32 [5, 768, 768], P(None, 'mp', 'dp')
- new_encoder_out_second: float32 [5, 768, 768], P(None, 'mp', 'dp')
- new_decoder_in: float32 [512, 7, 512], P('dp', None, 'mp')
- new_decoder_in_moment: float32 [512, 7, 512], P('dp', None, 'mp')
- new_decoder_in_second: float32 [512, 7, 512], P('dp', None, 'mp')
- new_decoder_out: float32 [5, 512, 512], P(None, 'mp', 'dp')
- new_decoder_out_moment: float32 [5, 512, 512], P(None, 'mp', 'dp')
- new_decoder_out_second: float32 [5, 512, 512], P(None, 'mp', 'dp')
- new_patch_embed: float32 [1536, 768], P('dp')
- new_patch_embed_moment: float32 [1536, 768], P('dp')
- new_patch_embed_second: float32 [1536, 768], P('dp')
- new_decoder_embed: float32 [768, 512], P('dp')
- new_decoder_embed_moment: float32 [768, 512], P('dp')
- new_decoder_embed_second: float32 [768, 512], P('dp')
- new_pixel_head: float32 [512, 1536], P('dp', 'mp')
- new_pixel_head_moment: float32 [512, 1536], P('dp', 'mp')
- new_pixel_head_second: float32 [512, 1536], P('dp', 'mp')
- new_norm_params: float32 [8192], P('dp')
- new_norm_params_moment: float32 [8192], P('dp')
- new_norm_params_second: float32 [8192], P('dp')
The draws below stay inside these ranges and needn't reach their ends.
Inputs may be any that keep to these rules, and one draw needn't show every extreme that they name: `visible`: each row holds 147 different token numbers in rising order. `row_dest`: let N be the number of dp indices, 74 = ceil(4 * 147 / N) and 592 = N * 74. All entries of an item slot equal 592 when the slot is empty, and a device's live slots come first. The live slots of a device and of the device half the dp axis away number 4 together. A live entry is owner * 74 + k: owner is the dp index of the device that processes this visible row, k counts the earlier rows of the same device sent to that owner. Entries of one device differ; each owner receives exactly 294 = 294 rows; some device sends 74 rows to one owner and some device has no live slot.
All inputs are finite; a program needn't handle non-finite values. No bound on the sum of `valid` on one device may be relied on, other than what follows from the above.
Results may differ from the reference program's by a relative error of at most 0.0075.
Values may be sent and summed in bfloat16 or wider, within the bound.
No kernel may reach another device: no remote copies, remote signals or barrier semaphores. Data moves between devices by JAX's collectives and lax.ppermute only.
A program may use at most 256 MiB of HBM per device.

```python
import math
import jax
import jax.numpy as jnp
from jax import lax

D_ENC = 768
HEADS_ENC = 12
D_DEC = 512
HEADS_DEC = 16
BANDS = 6
PATCH_PIX = 256
TOK = 588
VIS = 147
ITEM_CAP = 4
STEP = 10
PIX = 1536
SLOTS = 32
CAP = 74
ENC_BLOCKS = 7
ENC_OUTS = 5
DEC_BLOCKS = 7
DEC_OUTS = 5
NORM_LEN = 8192
PARAMS = 12591104
N_DP = 8


def draw_visible(key, part):
    key = jax.random.fold_in(key, 3)
    slot_keys = jax.random.split(key, SLOTS)

    def choose(one_key):
        return jnp.sort(jax.random.permutation(one_key, TOK)[:VIS])
    return jax.vmap(choose)(slot_keys).astype(jnp.int32)


def draw_row_dest(key, part):
    key = jax.random.fold_in(key, 5)
    devices = SLOTS // ITEM_CAP
    half_count = devices // 2
    key_share, key_full, key_offset = jax.random.split(key, 3)
    shares = jax.random.randint(key_share, (half_count,), 0, ITEM_CAP + 1)
    full_pair = jax.random.randint(key_full, (), 0, half_count)
    shares = jnp.where(jnp.arange(half_count) == full_pair, ITEM_CAP, shares)
    live_items = jnp.concatenate([shares, ITEM_CAP - shares])
    live_rows = live_items * VIS
    first_row = jnp.cumsum(live_rows) - live_rows
    offset = jax.random.randint(key_offset, (), 0, devices)
    slot_index = jnp.arange(ITEM_CAP)[:, None]
    local_row = slot_index * VIS + jnp.arange(VIS)[None, :]
    global_row = first_row[:, None, None] + local_row[None]
    owner = (global_row + offset) % devices
    position = owner * CAP + local_row[None] // devices
    alive_slot = slot_index[None] < live_items[:, None, None]
    return jnp.where(alive_slot, position, devices * CAP).reshape(SLOTS, VIS).astype(jnp.int32)


def draw_norm_params(key, part):
    key = jax.random.fold_in(key, 7)
    key_gain, key_small, key_mask = jax.random.split(key, 3)
    number = jnp.arange(NORM_LEN)
    encoder_part = number < 6 * D_ENC
    row_kind = jnp.where(encoder_part, number // D_ENC, (number - 6 * D_ENC) // D_DEC)
    is_gain = (row_kind % 2 == 0) & (row_kind < 6)
    is_mask = jnp.logical_not(encoder_part) & (row_kind == 6)
    gain_values = jnp.clip(1.0 + 0.15 * jax.random.normal(key_gain, (NORM_LEN,), jnp.float32), 0.5, 1.5)
    small_values = jnp.clip(0.3 * jax.random.normal(key_small, (NORM_LEN,), jnp.float32), -3.0, 3.0)
    mask_values = jnp.clip(jax.random.normal(key_mask, (NORM_LEN,), jnp.float32), -3.0, 3.0)
    return jnp.where(is_gain, gain_values, jnp.where(is_mask, mask_values, small_values)).astype(jnp.float32)


def plant(entries, key, smallest, largest):
    longest = entries.shape.index(max(entries.shape))
    spots = []
    for shift in (0, 1):
        where = [jax.random.randint(jax.random.fold_in(key, axis), (), 0, length) for axis, length in enumerate(entries.shape)]
        where[longest] = (where[longest] + shift) % entries.shape[longest]
        spots.append(tuple(where))
    return entries.at[spots[0]].set(smallest).at[spots[1]].set(largest)


def block_scale(rng, dims, pieces, least, high):
    def one(dim, blocks):
        draws = jax.random.uniform(jax.random.fold_in(jax.random.fold_in(rng, 6), dim), (blocks,), jnp.float32, least / len(pieces), high / len(pieces))
        return jnp.repeat(jnp.exp(draws), dims[dim] // blocks).reshape((-1,) + (1,) * (len(dims) - dim - 1))

    factor_of = one(*pieces[0])
    for cut in pieces[1:]:
        factor_of = factor_of * one(*cut)
    return factor_of


def scatter_about(key, dims, spread, reach, shards=(), kind=jnp.bfloat16):
    factor_of = block_scale(key, dims, shards, -0.22, 0.18) if shards else 1.0
    array = jax.random.normal(key, dims, jnp.float32) * spread * factor_of
    return jnp.minimum(jnp.maximum(array, -reach), reach).astype(kind)


def setup_inputs(seed: int = 0) -> dict:
    arg_keys = jax.random.split(jax.random.key(seed), 29)
    return {
        "pixels": scatter_about(arg_keys[0], (SLOTS, TOK, PIX), 1.0, 6.0, ((0, 8),)),
        "visible": draw_visible(jax.random.fold_in(arg_keys[28], 71), 0),
        "valid": plant((jax.random.randint(arg_keys[2], (SLOTS, TOK, PATCH_PIX), 0, 8) < 7).astype(jnp.int32), jax.random.fold_in(arg_keys[2], 1), 0, 1),
        "row_dest": draw_row_dest(jax.random.fold_in(arg_keys[28], 71), 0),
        "encoder_in": scatter_about(arg_keys[4], (D_ENC, ENC_BLOCKS, D_ENC), D_ENC ** -0.5, 0.21875, ((0, 8), (2, 4)), jnp.float32),
        "encoder_in_moment": scatter_about(arg_keys[5], (D_ENC, ENC_BLOCKS, D_ENC), (0.11 * 0.0002 / PARAMS ** 0.5), 3.725290298461914e-08, ((0, 8), (2, 4)), jnp.float32),
        "encoder_in_second": jnp.clip(jnp.exp(math.log(6.671377076362679e-16) - 1.3768157 * jax.random.uniform(arg_keys[6], (D_ENC, ENC_BLOCKS, D_ENC), jnp.float32) ** block_scale(arg_keys[6], (D_ENC, ENC_BLOCKS, D_ENC), ((0, 8), (2, 4)), -0.2, 0.2)), 1.683728386782954e-16, 6.671377076362679e-16),
        "encoder_out": scatter_about(arg_keys[7], (ENC_OUTS, D_ENC, D_ENC), (2 * D_ENC) ** -0.5, 0.15625, ((1, 4), (2, 8)), jnp.float32),
        "encoder_out_moment": scatter_about(arg_keys[8], (ENC_OUTS, D_ENC, D_ENC), (0.11 * 0.0002 / PARAMS ** 0.5), 3.725290298461914e-08, ((1, 4), (2, 8)), jnp.float32),
        "encoder_out_second": jnp.clip(jnp.exp(math.log(6.671377076362679e-16) - 1.3768157 * jax.random.uniform(arg_keys[9], (ENC_OUTS, D_ENC, D_ENC), jnp.float32) ** block_scale(arg_keys[9], (ENC_OUTS, D_ENC, D_ENC), ((1, 4), (2, 8)), -0.2, 0.2)), 1.683728386782954e-16, 6.671377076362679e-16),
        "decoder_in": scatter_about(arg_keys[10], (D_DEC, DEC_BLOCKS, D_DEC), D_DEC ** -0.5, 0.25, ((0, 8), (2, 4)), jnp.float32),
        "decoder_in_moment": scatter_about(arg_keys[11], (D_DEC, DEC_BLOCKS, D_DEC), (0.11 * 0.0002 / PARAMS ** 0.5), 3.725290298461914e-08, ((0, 8), (2, 4)), jnp.float32),
        "decoder_in_second": jnp.clip(jnp.exp(math.log(6.671377076362679e-16) - 1.3768157 * jax.random.uniform(arg_keys[12], (D_DEC, DEC_BLOCKS, D_DEC), jnp.float32) ** block_scale(arg_keys[12], (D_DEC, DEC_BLOCKS, D_DEC), ((0, 8), (2, 4)), -0.2, 0.2)), 1.683728386782954e-16, 6.671377076362679e-16),
        "decoder_out": scatter_about(arg_keys[13], (DEC_OUTS, D_DEC, D_DEC), (2 * D_DEC) ** -0.5, 0.1875, ((1, 4), (2, 8)), jnp.float32),
        "decoder_out_moment": scatter_about(arg_keys[14], (DEC_OUTS, D_DEC, D_DEC), (0.11 * 0.0002 / PARAMS ** 0.5), 3.725290298461914e-08, ((1, 4), (2, 8)), jnp.float32),
        "decoder_out_second": jnp.clip(jnp.exp(math.log(6.671377076362679e-16) - 1.3768157 * jax.random.uniform(arg_keys[15], (DEC_OUTS, D_DEC, D_DEC), jnp.float32) ** block_scale(arg_keys[15], (DEC_OUTS, D_DEC, D_DEC), ((1, 4), (2, 8)), -0.2, 0.2)), 1.683728386782954e-16, 6.671377076362679e-16),
        "patch_embed": scatter_about(arg_keys[16], (PIX, D_ENC), PIX ** -0.5, 0.15625, ((0, 8),), jnp.float32),
        "patch_embed_moment": scatter_about(arg_keys[17], (PIX, D_ENC), (0.022 * 0.0002 / PARAMS ** 0.5), 7.450580596923828e-09, ((0, 8),), jnp.float32),
        "patch_embed_second": jnp.clip(jnp.exp(math.log(2.6685508305450715e-17) - 1.3862944 * jax.random.uniform(arg_keys[18], (PIX, D_ENC), jnp.float32) ** block_scale(arg_keys[18], (PIX, D_ENC), ((0, 8),), -0.2, 0.2)), 6.671377076362679e-18, 2.6685508305450715e-17),
        "decoder_embed": scatter_about(arg_keys[19], (D_ENC, D_DEC), D_ENC ** -0.5, 0.21875, ((0, 8),), jnp.float32),
        "decoder_embed_moment": scatter_about(arg_keys[20], (D_ENC, D_DEC), (0.11 * 0.0002 / PARAMS ** 0.5), 3.725290298461914e-08, ((0, 8),), jnp.float32),
        "decoder_embed_second": jnp.clip(jnp.exp(math.log(6.671377076362679e-16) - 1.3768157 * jax.random.uniform(arg_keys[21], (D_ENC, D_DEC), jnp.float32) ** block_scale(arg_keys[21], (D_ENC, D_DEC), ((0, 8),), -0.2, 0.2)), 1.683728386782954e-16, 6.671377076362679e-16),
        "pixel_head": scatter_about(arg_keys[22], (D_DEC, PIX), D_DEC ** -0.5, 0.25, ((0, 8), (1, 4)), jnp.float32),
        "pixel_head_moment": scatter_about(arg_keys[23], (D_DEC, PIX), (0.11 * 0.0002 / PARAMS ** 0.5), 3.725290298461914e-08, ((0, 8), (1, 4)), jnp.float32),
        "pixel_head_second": jnp.clip(jnp.exp(math.log(6.671377076362679e-16) - 1.3768157 * jax.random.uniform(arg_keys[24], (D_DEC, PIX), jnp.float32) ** block_scale(arg_keys[24], (D_DEC, PIX), ((0, 8), (1, 4)), -0.2, 0.2)), 1.683728386782954e-16, 6.671377076362679e-16),
        "norm_params": draw_norm_params(jax.random.fold_in(arg_keys[28], 71), 0),
        "norm_params_moment": scatter_about(arg_keys[26], (NORM_LEN,), (1.0 * 0.0002 / PARAMS ** 0.5), 3.5762786865234375e-07, ((0, 8),), jnp.float32),
        "norm_params_second": jnp.clip(jnp.exp(math.log(5.0829539145411107e-14) - 1.3862944 * jax.random.uniform(arg_keys[27], (NORM_LEN,), jnp.float32) ** block_scale(arg_keys[27], (NORM_LEN,), ((0, 8),), -0.2, 0.2)), 1.2707384786352777e-14, 5.0829539145411107e-14),
    }


EPS_NORM = 1e-05
EPS_PIX = 1e-06
CLIP = 0.0002
LR_MATRIX = 0.03
LR_NORM = 0.5
BETA_ONE = 0.9
BETA_TWO = 0.95
ADAM_EPS = 1e-10
DECAY = 0.05

@jax.custom_vjp
def low(v):
    return lax.optimization_barrier(v.astype(jnp.bfloat16)).astype(jnp.float32)

@jax.custom_vjp
def low_back(v):
    return v

def low_keep(v):
    return (low(v), None)

def low_pass(kept, grad):
    return (grad,)

def back_keep(v):
    return (v, None)

def back_low(kept, grad):
    return (low(grad),)
low.defvjp(low_keep, low_pass)
low_back.defvjp(back_keep, back_low)

def round_both(value):
    return low(low_back(value))

def matmul(left, right):
    return jnp.dot(left, right, precision=lax.Precision.HIGHEST, preferred_element_type=jnp.float32)

def sincos(count_rows, features):
    places = jnp.arange(count_rows, dtype=jnp.float32)[:, None]
    half_width = features // 2
    freqs = jnp.exp(-jnp.log(10000.0) * jnp.arange(half_width, dtype=jnp.float32) / half_width)
    angles = places * freqs[None, :]
    return jnp.concatenate([jnp.sin(angles), jnp.cos(angles)], axis=1)

def layer_norm(stream, gain_row, shift_row):
    centred = stream - lax.optimization_barrier(jnp.mean(stream, -1, keepdims=True))
    return centred * lax.rsqrt(lax.optimization_barrier(jnp.mean(centred * centred, -1, keepdims=True)) + EPS_NORM) * gain_row + shift_row

def attend(normed, w_qkv, w_proj, head_count):
    length, features = normed.shape
    head_size = features // head_count
    projected = [round_both(matmul(normed, w_qkv[:, number])).reshape(length, head_count, head_size) for number in range(3)]
    scores = jnp.einsum('qhd,khd->hqk', projected[0], projected[1], precision=lax.Precision.HIGHEST) * head_size ** (-0.5)
    scores = low_back(scores)
    attend_low = low(jax.nn.softmax(scores, axis=-1))
    mixture = jnp.einsum('hqk,khd->qhd', attend_low, projected[2], precision=lax.Precision.HIGHEST)
    mixture = round_both(mixture.reshape(length, features))
    return low_back(matmul(mixture, w_proj))

def layer_block(stream, w_in, w_out, gains, head_count):
    features = stream.shape[-1]
    normed = low(layer_norm(stream, gains[0], gains[1]))
    stream = stream + attend(normed, w_in[:, 0:3], w_out[0], head_count)
    normed = low(layer_norm(stream, gains[2], gains[3]))
    upward = low_back(matmul(normed, w_in[:, 3:].reshape(features, -1)))
    hidden = low(jax.nn.gelu(upward, approximate=False))
    return stream + low_back(matmul(hidden, w_out[1:].reshape(-1, features)))

def split_norms(norm_vector):
    enc_gains = norm_vector[:6 * D_ENC].reshape(6, D_ENC)
    dec_gains = norm_vector[6 * D_ENC:6 * D_ENC + 6 * D_DEC].reshape(6, D_DEC)
    mask_token = norm_vector[6 * D_ENC + 6 * D_DEC:6 * D_ENC + 7 * D_DEC]
    return (enc_gains, dec_gains, mask_token)

def loss_weight(shown_row, valid_row, alive_slot):
    return (1.0 - shown_row)[:, None] * jnp.tile(valid_row, (1, BANDS)) * alive_slot

def slot_loss(weights, pixel_rows, chosen, valid_row, alive_slot):
    enc_in, enc_out, dec_in, dec_out, patch_matrix, embed_matrix, head_matrix, norm_vector = weights
    enc_gains, dec_gains, mask_token = split_norms(norm_vector)
    centred = pixel_rows - lax.optimization_barrier(jnp.mean(pixel_rows, -1, keepdims=True))
    target = centred * lax.rsqrt(lax.optimization_barrier(jnp.mean(centred * centred, -1, keepdims=True)) + EPS_PIX)
    stream = low_back(matmul(pixel_rows[chosen], patch_matrix)) + sincos(TOK, D_ENC)[chosen]
    stream = layer_block(stream, enc_in, enc_out, enc_gains, HEADS_ENC)
    normed = low(layer_norm(stream, enc_gains[4], enc_gains[5]))
    embedded = low_back(matmul(normed, embed_matrix))
    shown_row = jnp.zeros((TOK,), jnp.float32).at[chosen].set(1.0)
    stream = jnp.zeros((TOK, D_DEC), jnp.float32).at[chosen].set(embedded)
    stream = stream + (1.0 - shown_row)[:, None] * mask_token[None, :] + sincos(TOK, D_DEC)
    stream = layer_block(stream, dec_in, dec_out, dec_gains, HEADS_DEC)
    normed = low(layer_norm(stream, dec_gains[4], dec_gains[5]))
    predicted = low_back(matmul(normed, head_matrix))
    errors = predicted - target
    return jnp.sum(loss_weight(shown_row, valid_row, alive_slot) * errors * errors)

def adam_update(weight, moment, second, gradient, step_rate, decay_rate):
    moment = BETA_ONE * moment + (1.0 - BETA_ONE) * gradient
    second = BETA_TWO * second + (1.0 - BETA_TWO) * gradient * gradient
    fixed_one = moment / (1.0 - BETA_ONE ** STEP)
    fixed_two = second / (1.0 - BETA_TWO ** STEP)
    weight = weight - step_rate * (fixed_one / (jnp.sqrt(fixed_two) + ADAM_EPS) + decay_rate * weight)
    return [weight, moment, second]

def reference(pixels, visible, valid, row_dest, encoder_in, encoder_in_moment, encoder_in_second, encoder_out, encoder_out_moment, encoder_out_second, decoder_in, decoder_in_moment, decoder_in_second, decoder_out, decoder_out_moment, decoder_out_second, patch_embed, patch_embed_moment, patch_embed_second, decoder_embed, decoder_embed_moment, decoder_embed_second, pixel_head, pixel_head_moment, pixel_head_second, norm_params, norm_params_moment, norm_params_second):
    masters = [encoder_in, encoder_out, decoder_in, decoder_out, patch_embed, decoder_embed, pixel_head, norm_params]
    moments = [encoder_in_moment, encoder_out_moment, decoder_in_moment, decoder_out_moment, patch_embed_moment, decoder_embed_moment, pixel_head_moment, norm_params_moment]
    seconds = [encoder_in_second, encoder_out_second, decoder_in_second, decoder_out_second, patch_embed_second, decoder_embed_second, pixel_head_second, norm_params_second]
    alive = (row_dest[:, 0] < N_DP * CAP).astype(jnp.float32)
    pixel_float = pixels.astype(jnp.float32)
    valid_float = valid.astype(jnp.float32)
    shown = jnp.zeros((SLOTS, TOK), jnp.float32).at[jnp.arange(SLOTS)[:, None], visible].set(1.0)
    valid_count = BANDS * jnp.sum((1.0 - shown) * alive[:, None] * lax.optimization_barrier(jnp.sum(valid_float, -1)))

    def total_loss(params):
        rounded = [low(weight) for weight in params]

        def scan_step(running, slot_data):
            return (running + jax.checkpoint(slot_loss)(rounded, *slot_data), None)
        running, unused = lax.scan(scan_step, jnp.zeros((), jnp.float32), (pixel_float, visible, valid_float, alive))
        return running
    loss_sum, pullback = jax.vjp(total_loss, masters)
    gradients = pullback(1.0 / valid_count)[0]
    grad_norm = jnp.sqrt(sum((jnp.sum(gradient * gradient) for gradient in gradients)))
    clip_scale = CLIP / jnp.maximum(grad_norm, CLIP)
    updated = []
    for number in range(8):
        step_rate = LR_NORM if number == 7 else LR_MATRIX
        decay_rate = 0.0 if number == 7 else DECAY
        updated.extend(adam_update(masters[number], moments[number], seconds[number], gradients[number] * clip_scale, step_rate, decay_rate))
    return (loss_sum, valid_count, grad_norm, updated[0], updated[1], updated[2], updated[3], updated[4], updated[5], updated[6], updated[7], updated[8], updated[9], updated[10], updated[11], updated[12], updated[13], updated[14], updated[15], updated[16], updated[17], updated[18], updated[19], updated[20], updated[21], updated[22], updated[23])
```

```python
import math

import jax
import jax.numpy as jnp
from jax import lax
from jax.sharding import Mesh
from jax.sharding import PartitionSpec as P

HEADS_ENC = 12
HEADS_DEC = 16
STEP = 10


EPS_NORM = 1e-05
EPS_PIX = 1e-06
CLIP = 0.0002
LR_MATRIX = 0.03
LR_NORM = 0.5
BETA_ONE = 0.9
BETA_TWO = 0.95
ADAM_EPS = 1e-10
DECAY = 0.05
FLOAT_TYPE = jnp.float32
NARROW_TYPE = jnp.bfloat16
SWAP = [(0, 1), (1, 0)]
LANES = 128
DATA = ("z", "y")


def product(spec, left, right):
    return jnp.einsum(spec, left, right, preferred_element_type=FLOAT_TYPE)


def low(values):
    return values.astype(NARROW_TYPE)


def swap(values, axis="c"):
    return lax.ppermute(values, axis, SWAP)


def join(partial):
    return partial + swap(partial)


def join_low(partial):
    mine = low(partial)
    other = swap(mine)
    return mine.astype(FLOAT_TYPE) + other.astype(FLOAT_TYPE)


def shift(values, axis, step):
    size = lax.axis_size(axis)
    return lax.ppermute(values, axis, [(i, (i + step) % size) for i in range(size)])


def total_over(values, axes):
    for axis in axes:
        size = lax.axis_size(axis)
        if size & (size - 1):
            values = lax.psum(values, axis)
            continue
        step = 1
        while step < size:
            values = values + lax.ppermute(values, axis, [(i, i ^ step) for i in range(size)])
            step *= 2
    return values


def spread(blob):
    sizes = tuple(lax.axis_size(axis) for axis in ("x", "z", "y"))
    if sizes != (2, 4, 2):
        return lax.all_gather(blob, ("x", "z", "y")).reshape(sizes + blob.shape)
    x, z, y = (lax.axis_index(axis) for axis in ("x", "z", "y"))
    column = jnp.zeros((4,) + blob.shape, blob.dtype)
    moving = blob
    for step in range(4):
        column = lax.dynamic_update_index_in_dim(column, moving, (z - step) % 4, 0)
        if step < 3:
            moving = shift(moving, "z", 1)
    from_x = swap(column, "x")
    from_y = swap(column, "y")
    corner = jnp.concatenate([swap(from_x[:2], "y"), swap(from_y[2:], "x")])
    whole = jnp.zeros((2, 4, 2) + blob.shape, blob.dtype)
    for part, at_x, at_y in (
        (column, x, y),
        (from_x, 1 - x, y),
        (from_y, x, 1 - y),
        (corner, 1 - x, 1 - y),
    ):
        whole = lax.dynamic_update_slice(whole, part[None, :, None], (at_x, 0, at_y, 0, 0))
    return whole


def collect(grads):
    sizes = tuple(lax.axis_size(axis) for axis in ("x", "z", "y"))
    shape = grads.shape[3:]
    if sizes != (2, 4, 2):
        flat = grads.reshape((-1,) + shape)
        return lax.psum_scatter(flat, ("x", "z", "y"), scatter_dimension=0).astype(FLOAT_TYPE)
    x, z, y = (lax.axis_index(axis) for axis in ("x", "z", "y"))

    def part(at_x, at_y):
        cut = lax.dynamic_slice(grads, (at_x, 0, at_y, 0, 0), (1, 4, 1) + shape)
        return cut.reshape((4,) + shape)

    def add(*terms):
        return sum(term.astype(FLOAT_TYPE) for term in terms)

    corner = part(1 - x, 1 - y)
    by_x = swap(corner[:2], "x")
    by_y = swap(corner[2:], "y")
    to_y = part(x, 1 - y)
    to_x = part(1 - x, y)
    to_y = jnp.concatenate([low(add(to_y[:2], by_x)), to_y[2:]])
    to_x = jnp.concatenate([to_x[:2], low(add(to_x[2:], by_y))])
    column = low(add(part(x, y), swap(to_y, "y"), swap(to_x, "x")))

    def at(index):
        return lax.dynamic_index_in_dim(column, index % 4, 0, keepdims=False)

    moving = at(z - 1)
    for step in range(1, 4):
        moving = add(shift(moving, "z", 1), at(z - 1 - step))
        if step < 3:
            moving = low(moving)
    return moving


def exact_gelu(values):
    return jax.nn.gelu(values, approximate=False)


def angles_of(places, features):
    half_width = features // 2
    freqs = jnp.exp(-jnp.log(10000.0) * jnp.arange(half_width, dtype=FLOAT_TYPE) / half_width)
    angles = places.astype(FLOAT_TYPE)[:, None] * freqs[None, :]
    return jnp.concatenate([jnp.sin(angles), jnp.cos(angles)], axis=1)


def norm_fwd(stream, gain_row, shift_row):
    centred = stream - jnp.mean(stream, -1, keepdims=True)
    inverse = lax.rsqrt(jnp.mean(centred * centred, -1, keepdims=True) + EPS_NORM)
    scaled = centred * inverse
    return (scaled * gain_row + shift_row, (scaled, inverse))


def norm_back(upstream, kept_state, gain_row):
    scaled, inverse = kept_state
    weighted = upstream * gain_row
    input_grad = inverse * (
        weighted
        - jnp.mean(weighted, -1, keepdims=True)
        - scaled * jnp.mean(weighted * scaled, -1, keepdims=True)
    )
    return (input_grad, jnp.sum(upstream * scaled, 0), jnp.sum(upstream, 0))


def attn_fwd(stream, w_qkv, w_proj, gain_row, shift_row, head_count):
    normed, norm_kept = norm_fwd(stream, gain_row, shift_row)
    normed_low = low(normed)
    length = stream.shape[0]
    width = w_proj.shape[2]
    head_size = width // head_count
    triple = low(product("ld,xdc->xlc", normed_low, w_qkv))
    split_heads = triple.reshape(2, length, 3, head_count, head_size).transpose(2, 0, 3, 1, 4)
    scores = product("xhqe,xhke->xhqk", split_heads[0], split_heads[1]) * head_size ** (-0.5)
    log_total = jax.nn.logsumexp(scores, axis=-1, keepdims=True)
    attend_low = low(jnp.exp(scores - log_total))
    mixture = low(product("xhqk,xhke->xqhe", attend_low, split_heads[2]))
    mixture = mixture.reshape(2, length, width)
    partial = product("lc,dc->ld", mixture[0], w_proj[0]) + product("lc,dc->ld", mixture[1], w_proj[1])
    return (stream + join(partial), (normed_low, norm_kept, split_heads, mixture, log_total))


def attn_back(upstream, kept_state, w_qkv, w_proj, gain_row, head_count):
    normed_low, norm_kept, split_heads, mixture, log_total = kept_state
    _, length, width = mixture.shape
    head_size = width // head_count
    factor = head_size ** (-0.5)
    upstream_low = low(upstream)
    proj_grad = low(product("ld,xlc->xdc", upstream_low, mixture))
    mix_grad = low(product("ld,xdc->xlc", upstream_low, w_proj))
    mix_grad = mix_grad.reshape(2, length, head_count, head_size).transpose(0, 2, 1, 3)
    scores = product("xhqe,xhke->xhqk", split_heads[0], split_heads[1]) * factor
    attend_full = jnp.exp(scores - log_total)
    value_grad = low(product("xhqk,xhqe->xkhe", low(attend_full), mix_grad))
    attend_grad = product("xhqe,xhke->xhqk", mix_grad, split_heads[2])
    score_grad = attend_full * (attend_grad - jnp.sum(attend_full * attend_grad, -1, keepdims=True))
    score_grad = low(score_grad)
    query_grad = low(product("xhqk,xhke->xqhe", score_grad, split_heads[1]) * factor)
    key_grad = low(product("xhqk,xhqe->xkhe", score_grad, split_heads[0]) * factor)
    triple_grad = jnp.stack([query_grad, key_grad, value_grad], axis=2).reshape(2, length, 3 * width)
    qkv_grad = low(product("ld,xlc->xdc", normed_low, triple_grad))
    normed_grad = join_low(
        product("lc,dc->ld", triple_grad[0], w_qkv[0]) + product("lc,dc->ld", triple_grad[1], w_qkv[1])
    )
    input_grad, gain_grad, shift_grad = norm_back(normed_grad, norm_kept, gain_row)
    return (upstream + input_grad, qkv_grad, proj_grad, gain_grad, shift_grad)


def mlp_fwd(stream, w_up, w_down, gain_row, shift_row):
    normed, norm_kept = norm_fwd(stream, gain_row, shift_row)
    normed_low = low(normed)
    upward = product("ld,xdc->xlc", normed_low, w_up)
    hidden = low(exact_gelu(upward))
    partial = product("lc,dc->ld", hidden[0], w_down[0]) + product("lc,dc->ld", hidden[1], w_down[1])
    return (stream + join(partial), (normed_low, norm_kept, upward, hidden))


def mlp_back(upstream, kept_state, w_up, w_down, gain_row):
    normed_low, norm_kept, upward, hidden = kept_state
    upstream_low = low(upstream)
    down_grad = low(product("ld,xlc->xdc", upstream_low, hidden))
    hidden_grad = product("ld,xdc->xlc", upstream_low, w_down)
    upward_grad = low(jax.vjp(exact_gelu, upward)[1](hidden_grad)[0])
    up_grad = low(product("ld,xlc->xdc", normed_low, upward_grad))
    normed_grad = join_low(
        product("lc,dc->ld", upward_grad[0], w_up[0]) + product("lc,dc->ld", upward_grad[1], w_up[1])
    )
    input_grad, gain_grad, shift_grad = norm_back(normed_grad, norm_kept, gain_row)
    return (upstream + input_grad, up_grad, down_grad, gain_grad, shift_grad)


def adam_update(weight, moment, second, gradient, step_rate, decay_rate):
    moment = BETA_ONE * moment + (1.0 - BETA_ONE) * gradient
    second = BETA_TWO * second + (1.0 - BETA_TWO) * gradient * gradient
    fixed_one = moment / (1.0 - BETA_ONE**STEP)
    fixed_two = second / (1.0 - BETA_TWO**STEP)
    weight = weight - step_rate * (
        fixed_one / (jnp.sqrt(fixed_two) + ADAM_EPS) + decay_rate * weight
    )
    return [weight, moment, second]


def one_hot(visible_row, tokens):
    return visible_row[:, None] == jnp.arange(tokens)[None, :]


def pick(array, index, axis=0):
    return lax.dynamic_index_in_dim(array, index, axis, keepdims=False)


def columns_of(blob, widths):
    pieces, start = [], 0
    for width in widths:
        pieces.append(blob[..., start : start + width])
        start += width
    return pieces


def on_device(
    pixels,
    visible,
    valid,
    row_dest,
    encoder_in,
    encoder_in_moment,
    encoder_in_second,
    encoder_out,
    encoder_out_moment,
    encoder_out_second,
    decoder_in,
    decoder_in_moment,
    decoder_in_second,
    decoder_out,
    decoder_out_moment,
    decoder_out_second,
    patch_embed,
    patch_embed_moment,
    patch_embed_second,
    decoder_embed,
    decoder_embed_moment,
    decoder_embed_second,
    pixel_head,
    pixel_head_moment,
    pixel_head_second,
    norm_params,
    norm_params_moment,
    norm_params_second,
):
    masters = [
        encoder_in,
        encoder_out,
        decoder_in,
        decoder_out,
        patch_embed,
        decoder_embed,
        pixel_head,
        norm_params,
    ]
    moments = [
        encoder_in_moment,
        encoder_out_moment,
        decoder_in_moment,
        decoder_out_moment,
        patch_embed_moment,
        decoder_embed_moment,
        pixel_head_moment,
        norm_params_moment,
    ]
    seconds = [
        encoder_in_second,
        encoder_out_second,
        decoder_in_second,
        decoder_out_second,
        patch_embed_second,
        decoder_embed_second,
        pixel_head_second,
        norm_params_second,
    ]
    x, c = lax.axis_index("x"), lax.axis_index("c")
    data_size = lax.axis_size("z") * lax.axis_size("y")
    slot_total, tokens, pix_width = pixels.shape
    vis_count = visible.shape[1]
    patch_positions = valid.shape[2]
    rows_enc, _, part_enc = encoder_in.shape
    rows_dec, _, part_dec = decoder_in.shape
    width_enc, width_dec = patch_embed.shape[1], decoder_embed.shape[1]
    enc_heads = HEADS_ENC // 4
    dec_heads = HEADS_DEC // 4

    patch_rows = patch_embed.shape[0] // 2
    half_enc, quarter_dec = width_enc // 2, width_dec // 4
    patch_piece = lax.dynamic_slice(
        low(patch_embed), (c * patch_rows, x * half_enc), (patch_rows, half_enc)
    ).reshape(rows_enc, -1)
    embed_piece = lax.dynamic_slice(
        low(decoder_embed), (0, (2 * x + c) * quarter_dec), (rows_enc, quarter_dec)
    )
    norm_share, norm_room = norm_params.shape[0], rows_enc * LANES
    norm_piece = jnp.pad(low(norm_params), (0, norm_room - norm_share)).reshape(rows_enc, LANES)
    enc_in_low = low(encoder_in).reshape(rows_enc, -1)
    enc_out_low = low(encoder_out).transpose(2, 0, 1).reshape(rows_enc, -1)
    dec_in_low = low(decoder_in).reshape(rows_dec, -1)
    dec_out_low = low(decoder_out).transpose(2, 0, 1).reshape(rows_dec, -1)
    head_low = low(pixel_head)
    first_widths = (3 * part_enc, part_enc, patch_piece.shape[1], LANES)
    second_widths = (4 * part_enc, 4 * part_enc, quarter_dec)
    third_widths = (7 * part_dec, 5 * part_dec, head_low.shape[1])
    first_blob = jnp.concatenate(
        [enc_in_low[:, : 3 * part_enc], enc_out_low[:, :part_enc], patch_piece, norm_piece], 1
    )
    second_blob = jnp.concatenate(
        [enc_in_low[:, 3 * part_enc :], enc_out_low[:, part_enc:], embed_piece], 1
    )
    third_blob = jnp.concatenate([dec_in_low, dec_out_low, head_low], 1)
    first_all = spread(first_blob)
    second_all = spread(second_blob)
    third_all = spread(third_blob)

    def flat(array):
        return array.reshape(2, -1, array.shape[-1])

    enc_qkv, enc_proj, patch_all, norm_all = columns_of(flat(first_all), first_widths)
    enc_up, enc_down, embed_all = columns_of(flat(second_all), second_widths)
    dec_in_all, dec_out_all, head_all = columns_of(flat(third_all), third_widths)
    dec_qkv, dec_up = dec_in_all[..., : 3 * part_dec], dec_in_all[..., 3 * part_dec :]
    dec_proj, dec_down = dec_out_all[..., :part_dec], dec_out_all[..., part_dec:]
    patch_all = patch_all.reshape(2, -1, half_enc)
    embed_other = swap(embed_all)
    embed_even = jnp.where(c == 0, embed_all, embed_other)
    embed_odd = jnp.where(c == 0, embed_other, embed_all)
    full_embed = jnp.concatenate([embed_even[0], embed_odd[0], embed_even[1], embed_odd[1]], 1)
    norm_full = norm_all[0].reshape(data_size, norm_room)[:, :norm_share].reshape(-1)
    norm_full = norm_full.astype(FLOAT_TYPE)
    enc_gains = norm_full[: 6 * width_enc].reshape(6, width_enc)
    dec_gains = norm_full[6 * width_enc : 6 * width_enc + 6 * width_dec].reshape(6, width_dec)
    mask_token = norm_full[6 * width_enc + 6 * width_dec : 6 * width_enc + 7 * width_dec]

    buf_rows = data_size * -(-(slot_total * vis_count) // data_size)
    alive = row_dest[:, 0] < buf_rows
    use_own = pick(alive, x)
    half_step = lax.axis_size("z") // 2

    def shown_of(visible_row):
        return jnp.any(one_hot(visible_row, tokens), axis=0).astype(FLOAT_TYPE)

    shown_slots = jnp.stack([shown_of(visible[slot]) for slot in range(slot_total)])
    per_token = jnp.sum(valid, -1).astype(FLOAT_TYPE)
    valid_count = jnp.sum((1.0 - shown_slots) * alive.astype(FLOAT_TYPE)[:, None] * per_token)
    valid_count = total_over(valid_count * (pix_width // patch_positions), DATA)

    def seen_of(slot):
        chosen = low(one_hot(pick(visible, slot), tokens))
        rows = low(product("vt,tp->vp", chosen, pick(pixels, slot)))
        rows = rows.reshape(vis_count, data_size, 2, patch_rows)
        return pick(rows, c, 2).reshape(vis_count, data_size * patch_rows)

    def pixels_of(slot):
        rows = pick(pixels, slot).reshape(tokens, 2, 2, pix_width // 4)
        rows = pick(rows, c, 2).reshape(tokens, pix_width // 2)
        return jnp.concatenate([rows, low(pick(valid, slot))], 1)

    away = slot_total - 1 - x
    visible_row = jnp.where(use_own, pick(visible, x), shift(pick(visible, away), "z", half_step))
    seen_rows = jnp.where(use_own, seen_of(x), shift(seen_of(away), "z", half_step))
    chosen = low(one_hot(visible_row, tokens))
    hidden_row = 1.0 - shown_of(visible_row)

    stream = product("lp,xpd->xld", seen_rows, patch_all)
    stream = join(jnp.concatenate([stream[0], stream[1]], 1)) + angles_of(visible_row, width_enc)
    stream, enc_attn_kept = attn_fwd(
        stream, enc_qkv, enc_proj, enc_gains[0], enc_gains[1], enc_heads
    )
    stream, enc_mlp_kept = mlp_fwd(stream, enc_up, enc_down, enc_gains[2], enc_gains[3])
    normed, enc_norm_kept = norm_fwd(stream, enc_gains[4], enc_gains[5])
    enc_normed_low = low(normed)
    embedded = product("ld,dc->lc", enc_normed_low, full_embed)

    own_pixels = pixels_of(x)
    sent_pixels, embedded = lax.optimization_barrier((pixels_of(away), embedded))
    pixel_pack = jnp.where(use_own, own_pixels, shift(sent_pixels, "z", half_step))

    embedded_high = low(embedded)
    embedded_rest = low(embedded - embedded_high.astype(FLOAT_TYPE))
    placed = product("vt,vc->tc", chosen, jnp.concatenate([embedded_high, embedded_rest], 1))
    placed = placed[:, :width_dec] + placed[:, width_dec:]
    stream = placed + hidden_row[:, None] * mask_token + angles_of(jnp.arange(tokens), width_dec)
    stream, dec_attn_kept = attn_fwd(
        stream, dec_qkv, dec_proj, dec_gains[0], dec_gains[1], dec_heads
    )
    stream, dec_mlp_kept = mlp_fwd(stream, dec_up, dec_down, dec_gains[2], dec_gains[3])
    normed, dec_norm_kept = norm_fwd(stream, dec_gains[4], dec_gains[5])
    dec_normed_low = low(normed)
    predicted = product("ld,xdp->xlp", dec_normed_low, head_all)

    pixel_cols = pixel_pack[:, : pix_width // 2].astype(FLOAT_TYPE)
    valid_cols = pixel_pack[:, pix_width // 2 :].astype(FLOAT_TYPE)
    half_mean = jnp.mean(pixel_cols, -1, keepdims=True)
    half_square = jnp.sum((pixel_cols - half_mean) ** 2, -1, keepdims=True)
    half_both = jnp.concatenate([half_mean, half_square], 1)
    other_both = swap(half_both)
    mean = 0.5 * (half_both[:, :1] + other_both[:, :1])
    gap = half_both[:, :1] - other_both[:, :1]
    variance = (half_both[:, 1:] + other_both[:, 1:]) / pix_width + 0.25 * gap * gap
    target = (pixel_cols - mean) * lax.rsqrt(variance + EPS_PIX)
    half_positions = patch_positions // 2
    front = jnp.where(c == 0, valid_cols[:, :half_positions], valid_cols[:, half_positions:])
    back = jnp.where(c == 0, valid_cols[:, half_positions:], valid_cols[:, :half_positions])
    part_mask = jnp.concatenate([front, back, front], 1) * hidden_row[:, None]
    loss_weights = part_mask[None]
    goal = jnp.stack([target[:, : pix_width // 4], target[:, pix_width // 4 :]])
    errors = predicted - goal
    loss_part = jnp.sum(loss_weights * errors * errors)
    pred_grad = low(loss_weights * (2.0 * errors) * (1.0 / valid_count))
    head_grad = low(product("ld,xlp->xdp", dec_normed_low, pred_grad))
    normed_grad = join_low(
        product("lp,dp->ld", pred_grad[0], head_all[0]) + product("lp,dp->ld", pred_grad[1], head_all[1])
    )
    stream_grad, dec_gain_five, dec_shift_five = norm_back(
        normed_grad, dec_norm_kept, dec_gains[4]
    )
    stream_grad, dec_up_grad, dec_down_grad, dec_gain_three, dec_shift_three = mlp_back(
        stream_grad, dec_mlp_kept, dec_up, dec_down, dec_gains[2]
    )
    stream_grad, dec_qkv_grad, dec_proj_grad, dec_gain_one, dec_shift_one = attn_back(
        stream_grad, dec_attn_kept, dec_qkv, dec_proj, dec_gains[0], dec_heads
    )
    third_grads = jnp.concatenate(
        [dec_qkv_grad, dec_up_grad, dec_proj_grad, dec_down_grad, head_grad], 2
    )
    third_sum = collect(third_grads.reshape(third_all.shape))
    mask_grad = jnp.sum(hidden_row[:, None] * stream_grad, axis=0)
    embedded_grad = low(product("vt,tc->vc", chosen, low(stream_grad)))
    embed_mine = jnp.stack(
        [pick(embedded_grad.reshape(vis_count, 4, quarter_dec), 2 * part + c, 1) for part in (0, 1)]
    )
    embed_grad = low(product("ld,xlc->xdc", enc_normed_low, embed_mine))
    normed_grad = product("lc,dc->ld", embedded_grad, full_embed)
    stream_grad, enc_gain_five, enc_shift_five = norm_back(
        normed_grad, enc_norm_kept, enc_gains[4]
    )
    stream_grad, enc_up_grad, enc_down_grad, enc_gain_three, enc_shift_three = mlp_back(
        stream_grad, enc_mlp_kept, enc_up, enc_down, enc_gains[2]
    )
    second_grads = jnp.concatenate([enc_up_grad, enc_down_grad, embed_grad], 2)
    second_sum = collect(second_grads.reshape(second_all.shape))
    stream_grad, enc_qkv_grad, enc_proj_grad, enc_gain_one, enc_shift_one = attn_back(
        stream_grad, enc_attn_kept, enc_qkv, enc_proj, enc_gains[0], enc_heads
    )
    stream_low = low(stream_grad)
    patch_grad = low(
        product("lp,xld->xpd", seen_rows, jnp.stack([stream_low[:, :half_enc], stream_low[:, half_enc:]]))
    )
    norm_pieces = jnp.concatenate(
        [
            enc_gain_one,
            enc_shift_one,
            enc_gain_three,
            enc_shift_three,
            enc_gain_five,
            enc_shift_five,
            dec_gain_one,
            dec_shift_one,
            dec_gain_three,
            dec_shift_three,
            dec_gain_five,
            dec_shift_five,
            mask_grad,
        ]
    )
    norm_total = norm_params.shape[0] * data_size
    norm_grad = jnp.concatenate(
        [norm_pieces, jnp.zeros((norm_total - norm_pieces.shape[0],), FLOAT_TYPE)]
    )
    norm_half = norm_share // 2
    norm_grads = low(norm_grad).reshape(data_size, 2, norm_half).transpose(1, 0, 2)
    norm_grads = jnp.pad(norm_grads, ((0, 0), (0, 0), (0, norm_room - norm_half)))
    first_grads = jnp.concatenate(
        [
            enc_qkv_grad,
            enc_proj_grad,
            patch_grad.reshape(2, width_enc, -1),
            norm_grads.reshape(2, width_enc, LANES),
        ],
        2,
    )
    first_sum = collect(first_grads.reshape(first_all.shape))

    qkv_sum, proj_sum, patch_sum, norm_sum = columns_of(first_sum, first_widths)
    up_sum, down_sum, embed_sum = columns_of(second_sum, second_widths)
    dec_in_sum, dec_out_sum, head_sum = columns_of(third_sum, third_widths)
    norm_sum = low(norm_sum.reshape(-1)[:norm_half])
    patch_sum, embed_sum = low(patch_sum), low(embed_sum)
    shared_square = sum(
        jnp.sum(jnp.square(piece.astype(FLOAT_TYPE))) for piece in (patch_sum, embed_sum)
    ) + 0.5 * jnp.sum(jnp.square(norm_sum.astype(FLOAT_TYPE)))
    own_square = sum(
        jnp.sum(jnp.square(piece))
        for piece in (qkv_sum, proj_sum, up_sum, down_sum, third_sum)
    )
    totals = total_over(
        jnp.stack([loss_part, own_square + shared_square]), ("c", "x", "y", "z")
    )
    loss_sum, grad_norm = totals[0], jnp.sqrt(totals[1])

    def both(piece, axis, place, dimension):
        other = swap(piece, axis)
        return jnp.where(
            place == 0,
            jnp.concatenate([piece, other], dimension),
            jnp.concatenate([other, piece], dimension),
        )

    patch_sum = patch_sum.reshape(patch_rows, half_enc)
    patch_sum = both(both(patch_sum, "c", c, 0), "x", x, 1)
    embed_sum = both(both(embed_sum, "c", c, 1), "x", x, 1)
    norm_sum = both(norm_sum, "x", x, 0)
    reduced = (
        jnp.concatenate([qkv_sum, up_sum], 1).reshape(encoder_in.shape),
        jnp.concatenate([proj_sum, down_sum], 1).reshape(rows_enc, -1, part_enc).transpose(1, 2, 0),
        dec_in_sum.reshape(decoder_in.shape),
        dec_out_sum.reshape(rows_dec, -1, part_dec).transpose(1, 2, 0),
        patch_sum.astype(FLOAT_TYPE),
        embed_sum.astype(FLOAT_TYPE),
        head_sum,
        norm_sum.astype(FLOAT_TYPE),
    )
    clip_scale = CLIP / jnp.maximum(grad_norm, CLIP)
    updated = []
    for number in range(8):
        step_rate = LR_NORM if number == 7 else LR_MATRIX
        decay_rate = 0.0 if number == 7 else DECAY
        updated.extend(
            adam_update(
                masters[number],
                moments[number],
                seconds[number],
                reduced[number] * clip_scale,
                step_rate,
                decay_rate,
            )
        )
    return (loss_sum, valid_count, grad_norm, *updated)


def solution(mesh):
    data, model = mesh.shape["dp"], mesh.shape["mp"]
    inner = Mesh(mesh.devices.reshape(data // 2, 2, model // 2, 2), ("z", "y", "x", "c"))
    data_axes, model_axes = ("z", "y"), ("x", "c")
    rows = P(data_axes)
    into = P(data_axes, None, model_axes)
    out_of = P(None, model_axes, data_axes)
    head = P(data_axes, model_axes)
    weights = (into, out_of, into, out_of, rows, rows, head, rows)
    triples = tuple(spec for spec in weights for _ in range(3))
    return jax.shard_map(
        on_device,
        mesh=inner,
        in_specs=(rows, rows, rows, rows) + triples,
        out_specs=(P(), P(), P()) + triples,
        check_vma=False,
    )
```

```python
import numpy as np

import jax
import jax.numpy as jnp
from jax import lax
from jax.experimental import pallas as pl
from jax.experimental.pallas import tpu as pltpu
from jax.sharding import Mesh
from jax.sharding import PartitionSpec as P

HEADS_ENC = 12
HEADS_DEC = 16
STEP = 10


EPS_NORM = 1e-05
EPS_PIX = 1e-06
CLIP = 0.0002
LR_MATRIX = 0.03
LR_NORM = 0.5
BETA_ONE = 0.9
BETA_TWO = 0.95
ADAM_EPS = 1e-10
DECAY = 0.05
FLOAT_TYPE = jnp.float32
NARROW_TYPE = jnp.bfloat16
SWAP = [(0, 1), (1, 0)]
LANES = 128
DATA = ("z", "y")


def product(spec, left, right):
    return jnp.einsum(spec, left, right, preferred_element_type=FLOAT_TYPE)


def low(values):
    return values.astype(NARROW_TYPE)


def swap(values, axis="c"):
    return lax.ppermute(values, axis, SWAP)


def join(partial):
    return partial + swap(partial)


def join_low(partial):
    mine = low(partial)
    other = swap(mine)
    return mine.astype(FLOAT_TYPE) + other.astype(FLOAT_TYPE)


def shift(values, axis, step):
    size = lax.axis_size(axis)
    return lax.ppermute(values, axis, [(i, (i + step) % size) for i in range(size)])


def total_over(values, axes):
    for axis in axes:
        size = lax.axis_size(axis)
        if size & (size - 1):
            values = lax.psum(values, axis)
            continue
        step = 1
        while step < size:
            values = values + lax.ppermute(values, axis, [(i, i ^ step) for i in range(size)])
            step *= 2
    return values


def after(value, *others):
    return lax.optimization_barrier((value,) + others)[0]


def assemble(parts, places, shape):
    dims = len(places[0])
    spots = jnp.stack([jnp.asarray(at, jnp.int32) for place in places for at in place])

    def kernel(spots_ref, *refs):
        whole = refs[len(parts)]
        for number, part in enumerate(parts):
            window = tuple(
                pl.ds(spots_ref[number * dims + dim], part.shape[dim]) for dim in range(dims)
            )
            whole[window] = refs[number][...]

    size = int(np.prod(shape)) * parts[0].dtype.itemsize
    return pl.pallas_call(
        kernel,
        out_shape=jax.ShapeDtypeStruct(shape, parts[0].dtype),
        in_specs=[pl.BlockSpec(memory_space=pltpu.SMEM)]
        + [pl.BlockSpec(memory_space=pltpu.VMEM)] * len(parts),
        out_specs=pl.BlockSpec(memory_space=pltpu.VMEM),
        compiler_params=pltpu.CompilerParams(vmem_limit_bytes=32 * 2**20),
        cost_estimate=pl.CostEstimate(flops=0, bytes_accessed=2 * size, transcendentals=0),
    )(spots, *parts)


def spread(blob, earlier_z=(), earlier=()):
    sizes = tuple(lax.axis_size(axis) for axis in ("x", "z", "y"))
    if sizes != (2, 4, 2):
        return lax.all_gather(blob, ("x", "z", "y")).reshape(sizes + blob.shape), ((), (), (), ())
    x, y, z = (lax.axis_index(axis) for axis in ("x", "y", "z"))
    half = 2
    blob = after(blob, *earlier_z)
    moved = [blob] + [shift(blob, "z", step) for step in (1, 2, 3)]
    column = assemble(
        [part[None] for part in moved], [((z - step) % 4,) for step in range(4)], (4,) + blob.shape
    )
    column = after(column, *earlier)
    from_x, from_y = swap(column, "x"), swap(column, "y")
    corner = (swap(from_x[:half], "y"), swap(from_y[half:], "x"))
    whole = assemble(
        [part[None, :, None] for part in (column, from_x, from_y, *corner)],
        [
            (x, 0, y),
            (1 - x, 0, y),
            (x, 0, 1 - y),
            (1 - x, 0, 1 - y),
            (1 - x, half, 1 - y),
        ],
        (2, 4, 2) + blob.shape,
    )
    return whole, (moved[1:], (column,), (from_x, from_y), corner)


def collect(grads):
    sizes = tuple(lax.axis_size(axis) for axis in ("x", "z", "y"))
    shape = grads.shape[3:]
    if sizes != (2, 4, 2):
        flat = grads.reshape((-1,) + shape)
        return lax.psum_scatter(flat, ("x", "z", "y"), scatter_dimension=0).astype(FLOAT_TYPE)
    x, y, z = (lax.axis_index(axis) for axis in ("x", "y", "z"))
    half = 2

    def part(at_x, at_y):
        cut = lax.dynamic_slice(grads, (at_x, 0, at_y, 0, 0), (1, sizes[1], 1) + shape)
        return cut.reshape((sizes[1],) + shape)

    def add(*terms):
        return sum(term.astype(FLOAT_TYPE) for term in terms)

    corner = part(1 - x, 1 - y)
    by_x = swap(corner[:half], "x")
    by_y = swap(corner[half:], "y")
    to_y = part(x, 1 - y)
    to_x = part(1 - x, y)
    to_y = jnp.concatenate([low(add(to_y[:half], by_x)), to_y[half:]])
    to_x = jnp.concatenate([to_x[:half], low(add(to_x[half:], by_y))])
    column = low(add(part(x, y), swap(to_y, "y"), swap(to_x, "x")))

    def at(index):
        return lax.dynamic_index_in_dim(column, index % 4, 0, keepdims=False)

    return add(at(z), *(shift(at(z + step), "z", step) for step in (1, 2, 3)))


def collect_pieces(pieces, data_size):
    grads = jnp.concatenate(pieces, 2)
    z_size = lax.axis_size("z")
    return collect(grads.reshape(2, z_size, data_size // z_size, -1, grads.shape[2]))


def exact_gelu(values):
    return jax.nn.gelu(values, approximate=False)


def places_of(count, features):
    half_width = features // 2
    freqs = np.exp(-np.log(np.float32(10000.0)) * np.arange(half_width, dtype=np.float32) / np.float32(half_width))
    angles = np.arange(count, dtype=np.float32)[:, None] * freqs[None, :]
    return jnp.asarray(np.concatenate([np.sin(angles), np.cos(angles)], axis=1))


def angles_of(places, features):
    half_width = features // 2
    freqs = jnp.exp(-jnp.log(10000.0) * jnp.arange(half_width, dtype=FLOAT_TYPE) / half_width)
    angles = places.astype(FLOAT_TYPE)[:, None] * freqs[None, :]
    return jnp.concatenate([jnp.sin(angles), jnp.cos(angles)], axis=1)


def norm_fwd(stream, gain_row, shift_row):
    centred = stream - jnp.mean(stream, -1, keepdims=True)
    inverse = lax.rsqrt(jnp.mean(centred * centred, -1, keepdims=True) + EPS_NORM)
    scaled = centred * inverse
    return (scaled * gain_row + shift_row, (scaled, inverse))


def norm_back(upstream, kept_state, gain_row):
    scaled, inverse = kept_state
    weighted = upstream * gain_row
    input_grad = inverse * (
        weighted
        - jnp.mean(weighted, -1, keepdims=True)
        - scaled * jnp.mean(weighted * scaled, -1, keepdims=True)
    )
    return (input_grad, jnp.sum(upstream * scaled, 0), jnp.sum(upstream, 0))


def attn_fwd(stream, w_qkv, w_proj, gain_row, shift_row, head_count):
    normed, norm_kept = norm_fwd(stream, gain_row, shift_row)
    normed_low = low(normed)
    length = stream.shape[0]
    width = w_proj.shape[2]
    head_size = width // head_count
    triple = low(product("ld,xdc->xlc", normed_low, w_qkv))
    split_heads = triple.reshape(2, length, 3, head_count, head_size).transpose(2, 0, 3, 1, 4)
    scores = product("xhqe,xhke->xhqk", split_heads[0], split_heads[1]) * head_size ** (-0.5)
    log_total = jax.nn.logsumexp(scores, axis=-1, keepdims=True)
    attend_low = low(jnp.exp(scores - log_total))
    mixture = low(product("xhqk,xhke->xqhe", attend_low, split_heads[2]))
    mixture = mixture.reshape(2, length, width)
    partial = product("lc,dc->ld", mixture[0], w_proj[0]) + product("lc,dc->ld", mixture[1], w_proj[1])
    return (stream + join(partial), (normed_low, norm_kept, split_heads, mixture, log_total))


def attn_back(upstream, kept_state, w_qkv, w_proj, gain_row, head_count):
    normed_low, norm_kept, split_heads, mixture, log_total = kept_state
    _, length, width = mixture.shape
    head_size = width // head_count
    factor = head_size ** (-0.5)
    upstream_low = low(upstream)
    proj_grad = low(product("ld,xlc->xdc", upstream_low, mixture))
    mix_grad = low(product("ld,xdc->xlc", upstream_low, w_proj))
    mix_grad = mix_grad.reshape(2, length, head_count, head_size).transpose(0, 2, 1, 3)
    scores = product("xhqe,xhke->xhqk", split_heads[0], split_heads[1]) * factor
    attend_full = jnp.exp(scores - log_total)
    value_grad = low(product("xhqk,xhqe->xkhe", low(attend_full), mix_grad))
    attend_grad = product("xhqe,xhke->xhqk", mix_grad, split_heads[2])
    score_grad = attend_full * (attend_grad - jnp.sum(attend_full * attend_grad, -1, keepdims=True))
    score_grad = low(score_grad)
    query_grad = low(product("xhqk,xhke->xqhe", score_grad, split_heads[1]) * factor)
    key_grad = low(product("xhqk,xhqe->xkhe", score_grad, split_heads[0]) * factor)
    triple_grad = jnp.stack([query_grad, key_grad, value_grad], axis=2).reshape(2, length, 3 * width)
    qkv_grad = low(product("ld,xlc->xdc", normed_low, triple_grad))
    normed_grad = join_low(
        product("lc,dc->ld", triple_grad[0], w_qkv[0]) + product("lc,dc->ld", triple_grad[1], w_qkv[1])
    )
    input_grad, gain_grad, shift_grad = norm_back(normed_grad, norm_kept, gain_row)
    return (upstream + input_grad, qkv_grad, proj_grad, gain_grad, shift_grad)


def mlp_fwd(stream, w_up, w_down, gain_row, shift_row):
    normed, norm_kept = norm_fwd(stream, gain_row, shift_row)
    normed_low = low(normed)
    upward = product("ld,xdc->xlc", normed_low, w_up)
    hidden = low(exact_gelu(upward))
    partial = product("lc,dc->ld", hidden[0], w_down[0]) + product("lc,dc->ld", hidden[1], w_down[1])
    return (stream + join(partial), (normed_low, norm_kept, upward, hidden))


def mlp_back(upstream, kept_state, w_up, w_down, gain_row):
    normed_low, norm_kept, upward, hidden = kept_state
    upstream_low = low(upstream)
    down_grad = low(product("ld,xlc->xdc", upstream_low, hidden))
    hidden_grad = product("ld,xdc->xlc", upstream_low, w_down)
    upward_grad = low(jax.vjp(exact_gelu, upward)[1](hidden_grad)[0])
    up_grad = low(product("ld,xlc->xdc", normed_low, upward_grad))
    normed_grad = join_low(
        product("lc,dc->ld", upward_grad[0], w_up[0]) + product("lc,dc->ld", upward_grad[1], w_up[1])
    )
    input_grad, gain_grad, shift_grad = norm_back(normed_grad, norm_kept, gain_row)
    return (upstream + input_grad, up_grad, down_grad, gain_grad, shift_grad)


def adam_update(weight, moment, second, gradient, step_rate, decay_rate):
    moment = BETA_ONE * moment + (1.0 - BETA_ONE) * gradient
    second = BETA_TWO * second + (1.0 - BETA_TWO) * gradient * gradient
    fixed_one = moment / (1.0 - BETA_ONE**STEP)
    fixed_two = second / (1.0 - BETA_TWO**STEP)
    weight = weight - step_rate * (
        fixed_one / (jnp.sqrt(fixed_two) + ADAM_EPS) + decay_rate * weight
    )
    return [weight, moment, second]


def both(piece, axis, place, dimension):
    other = swap(piece, axis)
    return jnp.where(
        place == 0,
        jnp.concatenate([piece, other], dimension),
        jnp.concatenate([other, piece], dimension),
    )


def halves_of(array, place):
    half = array.shape[1] // 2
    return jnp.where(place == 0, array[:, :half], array[:, half:])


def one_hot(visible_row, tokens):
    return visible_row[:, None] == jnp.arange(tokens)[None, :]


def pick(array, index, axis=0):
    return lax.dynamic_index_in_dim(array, index, axis, keepdims=False)


def columns_of(blob, widths):
    pieces, start = [], 0
    for width in widths:
        pieces.append(blob[..., start : start + width])
        start += width
    return pieces


def on_device(
    pixels,
    visible,
    valid,
    row_dest,
    encoder_in,
    encoder_in_moment,
    encoder_in_second,
    encoder_out,
    encoder_out_moment,
    encoder_out_second,
    decoder_in,
    decoder_in_moment,
    decoder_in_second,
    decoder_out,
    decoder_out_moment,
    decoder_out_second,
    patch_embed,
    patch_embed_moment,
    patch_embed_second,
    decoder_embed,
    decoder_embed_moment,
    decoder_embed_second,
    pixel_head,
    pixel_head_moment,
    pixel_head_second,
    norm_params,
    norm_params_moment,
    norm_params_second,
):
    masters = [
        encoder_in,
        encoder_out,
        decoder_in,
        decoder_out,
        patch_embed,
        decoder_embed,
        pixel_head,
        norm_params,
    ]
    moments = [
        encoder_in_moment,
        encoder_out_moment,
        decoder_in_moment,
        decoder_out_moment,
        patch_embed_moment,
        decoder_embed_moment,
        pixel_head_moment,
        norm_params_moment,
    ]
    seconds = [
        encoder_in_second,
        encoder_out_second,
        decoder_in_second,
        decoder_out_second,
        patch_embed_second,
        decoder_embed_second,
        pixel_head_second,
        norm_params_second,
    ]
    x, c = lax.axis_index("x"), lax.axis_index("c")
    data_size = lax.axis_size("z") * lax.axis_size("y")
    slot_total, tokens, pix_width = pixels.shape
    vis_count = visible.shape[1]
    patch_positions = valid.shape[2]
    rows_enc, _, part_enc = encoder_in.shape
    rows_dec, _, part_dec = decoder_in.shape
    width_enc, width_dec = patch_embed.shape[1], decoder_embed.shape[1]
    enc_heads = HEADS_ENC // 4
    dec_heads = HEADS_DEC // 4

    patch_rows = patch_embed.shape[0] // 2
    half_enc, quarter_dec = width_enc // 2, width_dec // 4
    patch_piece = lax.dynamic_slice(
        low(patch_embed), (x * patch_rows, c * half_enc), (patch_rows, half_enc)
    )
    embed_piece = lax.dynamic_slice(
        low(decoder_embed), (0, (2 * x + c) * quarter_dec), (rows_enc, quarter_dec)
    )
    norm_share, norm_room = norm_params.shape[0], rows_enc * LANES
    norm_piece = jnp.pad(low(norm_params), (0, norm_room - norm_share)).reshape(rows_enc, LANES)
    enc_in_low = low(encoder_in).reshape(rows_enc, -1)
    enc_out_low = low(encoder_out).transpose(2, 0, 1).reshape(rows_enc, -1)
    dec_in_low = low(decoder_in).reshape(rows_dec, -1)
    dec_out_low = low(decoder_out).transpose(2, 0, 1).reshape(rows_dec, -1)
    head_low = low(pixel_head)
    first_widths = (3 * part_enc, part_enc, patch_piece.shape[1], LANES)
    second_widths = (4 * part_enc, 4 * part_enc, quarter_dec)
    third_widths = (7 * part_dec, 5 * part_dec, head_low.shape[1])
    first_blob = jnp.concatenate(
        [enc_in_low[:, : 3 * part_enc], enc_out_low[:, :part_enc], patch_piece, norm_piece], 1
    )
    second_blob = jnp.concatenate(
        [enc_in_low[:, 3 * part_enc :], enc_out_low[:, part_enc:], embed_piece], 1
    )
    third_blob = jnp.concatenate([dec_in_low, dec_out_low, head_low], 1)
    first_all, first_marks = spread(first_blob)
    second_all, second_marks = spread(second_blob, first_marks[0], first_marks[3])
    third_all, third_marks = spread(third_blob, second_marks[0], second_marks[3])

    def flat(array):
        return array.reshape(2, -1, array.shape[-1])

    enc_qkv, enc_proj, patch_all, norm_all = columns_of(flat(first_all), first_widths)
    enc_up, enc_down, embed_all = columns_of(flat(second_all), second_widths)
    dec_in_all, dec_out_all, head_all = columns_of(flat(third_all), third_widths)
    dec_qkv, dec_up = dec_in_all[..., : 3 * part_dec], dec_in_all[..., 3 * part_dec :]
    dec_proj, dec_down = dec_out_all[..., :part_dec], dec_out_all[..., part_dec:]
    patch_all = patch_all.reshape(2, data_size, patch_rows, half_enc).transpose(1, 0, 2, 3)
    patch_all = patch_all.reshape(pix_width, half_enc)
    embed_other = swap(embed_all)
    embed_even = jnp.where(c == 0, embed_all, embed_other)
    embed_odd = jnp.where(c == 0, embed_other, embed_all)
    full_embed = jnp.concatenate([embed_even[0], embed_odd[0], embed_even[1], embed_odd[1]], 1)
    norm_full = norm_all[0].reshape(data_size, norm_room)[:, :norm_share].reshape(-1)
    norm_full = norm_full.astype(FLOAT_TYPE)
    enc_gains = norm_full[: 6 * width_enc].reshape(6, width_enc)
    dec_gains = norm_full[6 * width_enc : 6 * width_enc + 6 * width_dec].reshape(6, width_dec)
    mask_token = norm_full[6 * width_enc + 6 * width_dec : 6 * width_enc + 7 * width_dec]

    buf_rows = data_size * -(-(slot_total * vis_count) // data_size)
    alive = row_dest[:, 0] < buf_rows
    use_own = pick(alive, x)
    half_step = lax.axis_size("z") // 2

    def shown_of(visible_row):
        return jnp.any(one_hot(visible_row, tokens), axis=0).astype(FLOAT_TYPE)

    start = after(x, first_blob)
    away = slot_total - 1 - start
    own_slot, away_slot = pick(pixels, start), pick(pixels, away)

    def seen_of(slot, rows):
        chosen = low(one_hot(pick(visible, slot), tokens))
        return low(product("vt,tp->vp", chosen, rows))

    visible_row = jnp.where(use_own, pick(visible, start), shift(pick(visible, away), "z", half_step))
    seen_away = halves_of(seen_of(away, away_slot), c)
    seen_away = both(shift(seen_away, "z", half_step), "c", c, 1)
    seen_rows = jnp.where(use_own, seen_of(after(start, *first_marks[0]), own_slot), seen_away)
    chosen = low(one_hot(visible_row, tokens))
    hidden_row = 1.0 - shown_of(visible_row)

    visible_late = after(visible, *first_marks[3])
    counted = jnp.stack([1.0 - shown_of(visible_late[slot]) for slot in range(slot_total)])
    counted = counted * alive.astype(FLOAT_TYPE)[:, None]
    valid_count = jnp.sum(counted[:, :, None] * valid.astype(FLOAT_TYPE))
    valid_count = total_over(valid_count * (pix_width // patch_positions), DATA)

    def pixels_of(slot, rows):
        place = after(c, *first_marks[3])
        half = pix_width // 2
        cols = [halves_of(rows[:, first : first + half], place) for first in (0, half)]
        return jnp.concatenate(cols + [low(pick(valid, slot))], 1)

    own_pack, away_pack = pixels_of(start, own_slot), pixels_of(away, away_slot)
    pack_moved = shift(after(away_pack, *third_marks[0]), "z", half_step)

    stream = both(product("lp,pd->ld", seen_rows, patch_all), "c", c, 1) + angles_of(visible_row, width_enc)
    stream, enc_attn_kept = attn_fwd(
        stream, enc_qkv, enc_proj, enc_gains[0], enc_gains[1], enc_heads
    )
    stream, enc_mlp_kept = mlp_fwd(stream, enc_up, enc_down, enc_gains[2], enc_gains[3])
    normed, enc_norm_kept = norm_fwd(stream, enc_gains[4], enc_gains[5])
    enc_normed_low = low(normed)
    embedded = product("ld,dc->lc", enc_normed_low, full_embed)


    embedded_high = low(embedded)
    embedded_rest = low(embedded - embedded_high.astype(FLOAT_TYPE))
    placed = product("vt,vc->tc", chosen, jnp.concatenate([embedded_high, embedded_rest], 1))
    placed = placed[:, :width_dec] + placed[:, width_dec:]
    stream = placed + hidden_row[:, None] * mask_token + places_of(tokens, width_dec)
    stream, dec_attn_kept = attn_fwd(
        stream, dec_qkv, dec_proj, dec_gains[0], dec_gains[1], dec_heads
    )
    pixel_pack = jnp.where(use_own, own_pack, after(pack_moved, stream))
    pixel_cols = pixel_pack[:, : pix_width // 2].astype(FLOAT_TYPE)
    valid_cols = pixel_pack[:, pix_width // 2 :].astype(FLOAT_TYPE)
    half_mean = jnp.mean(pixel_cols, -1, keepdims=True)
    half_square = jnp.sum((pixel_cols - half_mean) ** 2, -1, keepdims=True)
    half_both = jnp.concatenate([half_mean, half_square], 1)
    other_both = swap(half_both)
    mean = 0.5 * (half_both[:, :1] + other_both[:, :1])
    gap = half_both[:, :1] - other_both[:, :1]
    variance = (half_both[:, 1:] + other_both[:, 1:]) / pix_width + 0.25 * gap * gap
    target = (pixel_cols - mean) * lax.rsqrt(variance + EPS_PIX)
    stream, dec_mlp_kept = mlp_fwd(stream, dec_up, dec_down, dec_gains[2], dec_gains[3])
    normed, dec_norm_kept = norm_fwd(stream, dec_gains[4], dec_gains[5])
    dec_normed_low = low(normed)
    predicted = product("ld,xdp->xlp", dec_normed_low, head_all)

    half_positions = patch_positions // 2
    front = jnp.where(c == 0, valid_cols[:, :half_positions], valid_cols[:, half_positions:])
    back = jnp.where(c == 0, valid_cols[:, half_positions:], valid_cols[:, :half_positions])
    part_mask = jnp.concatenate([front, back, front], 1) * hidden_row[:, None]
    loss_weights = part_mask[None]
    goal = jnp.stack([target[:, : pix_width // 4], target[:, pix_width // 4 :]])
    errors = predicted - goal
    loss_part = jnp.sum(loss_weights * errors * errors)
    pred_grad = low(loss_weights * (2.0 * errors) * (1.0 / valid_count))
    head_grad = low(product("ld,xlp->xdp", dec_normed_low, pred_grad))
    normed_grad = join_low(
        product("lp,dp->ld", pred_grad[0], head_all[0]) + product("lp,dp->ld", pred_grad[1], head_all[1])
    )
    stream_grad, dec_gain_five, dec_shift_five = norm_back(
        normed_grad, dec_norm_kept, dec_gains[4]
    )
    stream_grad, dec_up_grad, dec_down_grad, dec_gain_three, dec_shift_three = mlp_back(
        stream_grad, dec_mlp_kept, dec_up, dec_down, dec_gains[2]
    )
    dec_tail_sum = collect_pieces([dec_up_grad, dec_down_grad, head_grad], data_size)
    stream_grad, dec_qkv_grad, dec_proj_grad, dec_gain_one, dec_shift_one = attn_back(
        stream_grad, dec_attn_kept, dec_qkv, dec_proj, dec_gains[0], dec_heads
    )
    dec_attn_sum = collect_pieces([dec_qkv_grad, dec_proj_grad], data_size)
    mask_grad = jnp.sum(hidden_row[:, None] * stream_grad, axis=0)
    embedded_grad = low(product("vt,tc->vc", chosen, low(stream_grad)))
    embed_mine = jnp.stack(
        [pick(embedded_grad.reshape(vis_count, 4, quarter_dec), 2 * part + c, 1) for part in (0, 1)]
    )
    embed_grad = low(product("ld,xlc->xdc", enc_normed_low, embed_mine))
    normed_grad = product("lc,dc->ld", embedded_grad, full_embed)
    stream_grad, enc_gain_five, enc_shift_five = norm_back(
        normed_grad, enc_norm_kept, enc_gains[4]
    )
    stream_grad, enc_up_grad, enc_down_grad, enc_gain_three, enc_shift_three = mlp_back(
        stream_grad, enc_mlp_kept, enc_up, enc_down, enc_gains[2]
    )
    enc_tail_sum = collect_pieces([enc_up_grad, enc_down_grad, embed_grad], data_size)
    stream_grad, enc_qkv_grad, enc_proj_grad, enc_gain_one, enc_shift_one = attn_back(
        stream_grad, enc_attn_kept, enc_qkv, enc_proj, enc_gains[0], enc_heads
    )
    stream_low = low(stream_grad)
    patch_grad = low(product("lp,ld->pd", seen_rows, halves_of(stream_low, c)))
    patch_grad = patch_grad.reshape(data_size, 2, patch_rows, half_enc).transpose(1, 0, 2, 3)
    norm_pieces = jnp.concatenate(
        [
            enc_gain_one,
            enc_shift_one,
            enc_gain_three,
            enc_shift_three,
            enc_gain_five,
            enc_shift_five,
            dec_gain_one,
            dec_shift_one,
            dec_gain_three,
            dec_shift_three,
            dec_gain_five,
            dec_shift_five,
            mask_grad,
        ]
    )
    norm_total = norm_params.shape[0] * data_size
    norm_grad = jnp.concatenate(
        [norm_pieces, jnp.zeros((norm_total - norm_pieces.shape[0],), FLOAT_TYPE)]
    )
    norm_half = norm_share // 2
    norm_grads = low(norm_grad).reshape(data_size, 2, norm_half).transpose(1, 0, 2)
    norm_grads = jnp.pad(norm_grads, ((0, 0), (0, 0), (0, norm_room - norm_half)))
    enc_attn_sum = collect_pieces(
        [
            enc_qkv_grad,
            enc_proj_grad,
            patch_grad.reshape(2, width_enc, -1),
            norm_grads.reshape(2, width_enc, LANES),
        ],
        data_size,
    )

    qkv_sum, proj_sum, patch_sum, norm_sum = columns_of(enc_attn_sum, first_widths)
    up_sum, down_sum, embed_sum = columns_of(enc_tail_sum, second_widths)
    dec_qkv_sum, dec_proj_sum = columns_of(dec_attn_sum, (3 * part_dec, part_dec))
    dec_up_sum, dec_down_sum, head_sum = columns_of(
        dec_tail_sum, (4 * part_dec, 4 * part_dec, head_low.shape[1])
    )
    norm_sum = low(norm_sum.reshape(-1)[:norm_half])
    patch_sum, embed_sum = low(patch_sum), low(embed_sum)
    shared_square = sum(
        jnp.sum(jnp.square(piece.astype(FLOAT_TYPE))) for piece in (patch_sum, embed_sum)
    ) + 0.5 * jnp.sum(jnp.square(norm_sum.astype(FLOAT_TYPE)))
    own_square = sum(
        jnp.sum(jnp.square(piece))
        for piece in (qkv_sum, proj_sum, up_sum, down_sum, dec_attn_sum, dec_tail_sum)
    )
    totals = total_over(
        jnp.stack([loss_part, own_square + shared_square]), ("c", "x", "y", "z")
    )
    loss_sum, grad_norm = totals[0], jnp.sqrt(totals[1])

    patch_sum = both(both(patch_sum, "c", c, 1), "x", x, 0)
    embed_sum = both(both(embed_sum, "c", c, 1), "x", x, 1)
    norm_sum = both(norm_sum, "x", x, 0)
    reduced = (
        jnp.concatenate([qkv_sum, up_sum], 1).reshape(encoder_in.shape),
        jnp.concatenate([proj_sum, down_sum], 1).reshape(rows_enc, -1, part_enc).transpose(1, 2, 0),
        jnp.concatenate([dec_qkv_sum, dec_up_sum], 1).reshape(decoder_in.shape),
        jnp.concatenate([dec_proj_sum, dec_down_sum], 1)
        .reshape(rows_dec, -1, part_dec)
        .transpose(1, 2, 0),
        patch_sum.astype(FLOAT_TYPE),
        embed_sum.astype(FLOAT_TYPE),
        head_sum,
        norm_sum.astype(FLOAT_TYPE),
    )
    clip_scale = CLIP / jnp.maximum(grad_norm, CLIP)
    updated = []
    for number in range(8):
        step_rate = LR_NORM if number == 7 else LR_MATRIX
        decay_rate = 0.0 if number == 7 else DECAY
        updated.extend(
            adam_update(
                masters[number],
                moments[number],
                seconds[number],
                reduced[number] * clip_scale,
                step_rate,
                decay_rate,
            )
        )
    return (loss_sum, valid_count, grad_norm, *updated)


def solution(mesh):
    data, model = mesh.shape["dp"], mesh.shape["mp"]
    inner = Mesh(mesh.devices.reshape(data // 2, 2, model // 2, 2), ("z", "y", "x", "c"))
    data_axes, model_axes = ("z", "y"), ("x", "c")
    rows = P(data_axes)
    into = P(data_axes, None, model_axes)
    out_of = P(None, model_axes, data_axes)
    head = P(data_axes, model_axes)
    weights = (into, out_of, into, out_of, rows, rows, head, rows)
    triples = tuple(spec for spec in weights for _ in range(3))
    return jax.shard_map(
        on_device,
        mesh=inner,
        in_specs=(rows, rows, rows, rows) + triples,
        out_specs=(P(), P(), P()) + triples,
        check_vma=False,
    )
```

```python
import numpy as np

import jax
import jax.numpy as jnp
from jax import lax
from jax.experimental import pallas as pl
from jax.experimental.pallas import tpu as pltpu
from jax.sharding import Mesh
from jax.sharding import PartitionSpec as P

HEADS_ENC = 12
HEADS_DEC = 16
STEP = 10


EPS_NORM = 1e-05
EPS_PIX = 1e-06
CLIP = 0.0002
LR_MATRIX = 0.03
LR_NORM = 0.5
BETA_ONE = 0.9
BETA_TWO = 0.95
ADAM_EPS = 1e-10
DECAY = 0.05
FLOAT_TYPE = jnp.float32
NARROW_TYPE = jnp.bfloat16
SWAP = [(0, 1), (1, 0)]
ACROSS = [(0, 3), (1, 2), (2, 1), (3, 0)]
LANES = 128
VMEM_ROOM = 56 * 2**20
SQRT_HALF = 0.5**0.5
DENSITY = (2.0 * np.pi) ** -0.5
DATA = ("z", "y")


def product(spec, left, right):
    return jnp.einsum(spec, left, right, preferred_element_type=FLOAT_TYPE)


def low(values):
    return values.astype(NARROW_TYPE)


def swap(values, axis="c"):
    return lax.ppermute(values, axis, SWAP)


def join(partial):
    return partial + swap(partial)


def join_low(partial):
    mine = low(partial)
    other = swap(mine)
    return mine.astype(FLOAT_TYPE) + other.astype(FLOAT_TYPE)


def shift(values, axis, step):
    size = lax.axis_size(axis)
    return lax.ppermute(values, axis, [(i, (i + step) % size) for i in range(size)])


def total_over(values, axes):
    for axis in axes:
        size = lax.axis_size(axis)
        if size & (size - 1):
            values = lax.psum(values, axis)
            continue
        step = 1
        while step < size:
            values = values + lax.ppermute(values, axis, [(i, i ^ step) for i in range(size)])
            step *= 2
    return values


def after(value, *others):
    return lax.optimization_barrier((value,) + others)[0]


def vmem_call(body, outs, *ins, scalars=(), scratch=(), flops=0):
    shapes = [jax.ShapeDtypeStruct(shape, kind) for shape, kind in outs]
    moved = sum(int(np.prod(a.shape)) * a.dtype.itemsize for a in [*ins, *shapes])
    return pl.pallas_call(
        body,
        out_shape=shapes,
        in_specs=[pl.BlockSpec(memory_space=pltpu.SMEM)] * len(scalars)
        + [pl.BlockSpec(memory_space=pltpu.VMEM)] * len(ins),
        out_specs=[pl.BlockSpec(memory_space=pltpu.VMEM)] * len(shapes),
        scratch_shapes=list(scratch),
        compiler_params=pltpu.CompilerParams(vmem_limit_bytes=VMEM_ROOM),
        cost_estimate=pl.CostEstimate(flops=flops, bytes_accessed=moved, transcendentals=0),
    )(*scalars, *ins)


class Spread:
    def __init__(self, blob, *earlier):
        self.half = blob.shape[0] // 2
        self.blob = after(blob, *earlier)
        self.near = self.plane(self.blob[None])

    def plane(self, part):
        from_x, from_y = swap(part, "x"), swap(part, "y")
        corner = (swap(from_x[:, : self.half], "y"), swap(from_y[:, self.half :], "x"))
        return from_x, from_y, *corner

    def along_z(self, *earlier):
        blob = after(self.blob, *earlier)
        self.moved = [shift(blob, "z", step) for step in (1, 2, 3)]

    def round_plane(self, *earlier):
        self.stack = after(jnp.stack(self.moved), *earlier)
        self.far = self.plane(self.stack)

    def whole(self, widths):
        rows = self.blob.shape[0]
        x, y, z = (lax.axis_index(axis) for axis in ("x", "y", "z"))
        starts = np.cumsum([0, *widths])

        def body(spot, *refs):
            here_x, here_y, here_z = spot[0], spot[1], spot[2]
            outs = refs[10:]
            for group in (0, 5):
                own, from_x, from_y, low_corner, high_corner = refs[group : group + 5]
                for number in range(own.shape[0]):
                    level = lax.rem(here_z - number + 3 if group else here_z + 4, 4)
                    for ref, at_x, at_y, first in (
                        (own, here_x, here_y, 0),
                        (from_x, 1 - here_x, here_y, 0),
                        (from_y, here_x, 1 - here_y, 0),
                        (low_corner, 1 - here_x, 1 - here_y, 0),
                        (high_corner, 1 - here_x, 1 - here_y, self.half),
                    ):
                        count = ref.shape[1]
                        for out, start, width in zip(outs, starts, widths):
                            out[at_x, level, at_y, first : first + count, :] = ref[
                                number, :, start : start + width
                            ]

        parts = (self.blob[None], *self.near, self.stack, *self.far)
        outs = [((2, 4, 2, rows, width), self.blob.dtype) for width in widths]
        wholes = vmem_call(body, outs, *parts, scalars=(jnp.stack([x, y, z]),))
        return [whole.reshape(2, 8 * rows, -1) for whole in wholes]


def spread_all(blobs, widths, arrived):
    sizes = tuple(lax.axis_size(axis) for axis in ("x", "z", "y"))
    if sizes != (2, 4, 2):
        wholes = [lax.all_gather(blob, ("x", "z", "y")) for blob in blobs]
        wholes = [whole.reshape(2, -1, whole.shape[-1]) for whole in wholes]
        pieces = [columns_of(whole, width) for whole, width in zip(wholes, widths)]
        return pieces, [wholes[0]] * 4
    first, second, third = (Spread(blob) for blob in blobs)
    first.along_z()
    second.along_z(*first.moved, arrived)
    first.round_plane()
    third.along_z(*first.far[:2])
    second.moved = [after(moved, *first.far[:2]) for moved in second.moved]
    second.round_plane(*first.far)
    third.moved = [after(moved, *second.far[:2]) for moved in third.moved]
    third.round_plane(*second.far)
    pieces = [group.whole(width) for group, width in zip((first, second, third), widths)]
    return pieces, [first.stack, first.far[0], first.far[2], third.stack]


def share(pieces, rows, patch=None, norms=None):
    x, y = lax.axis_index("x"), lax.axis_index("y")
    levels = lax.axis_size("z")
    half = levels // 2
    if (lax.axis_size("x"), levels, lax.axis_size("y")) != (2, 4, 2):
        cuts = []
        if patch is not None:
            cut = low(product("ld,lc->dc", *patch)).reshape(2 * levels, 2, rows, -1)
            cuts.append(cut.transpose(1, 0, 2, 3).reshape(2, 2 * levels * rows, -1))
        if norms is not None:
            cuts.append(norms.reshape(2, 2 * levels * rows, -1))
        cuts += [low(product("ld,xlc->xdc", left, right)) for left, right in pieces]
        return (jnp.concatenate(cuts, 2).reshape(4 * levels, rows, -1),)
    extra = []
    columns = 0
    if patch is not None:
        extra += [*patch]
        columns += patch[1].shape[1]
    if norms is not None:
        extra += [norms]
        columns += LANES
    first_column = columns
    for left, right in pieces:
        columns += right.shape[2]
    tallest = max([left.shape[1] for left, _ in pieces] + ([patch[0].shape[1]] if patch else []))
    widest = max([right.shape[2] for _, right in pieces] + ([patch[1].shape[1]] if patch else []))
    flops = sum(4 * left.shape[0] * left.shape[1] * right.shape[2] for left, right in pieces)

    def body(spot, *refs):
        ins, outs = refs[: len(extra) + 2 * len(pieces)], refs[len(extra) + 2 * len(pieces) : -1]
        total = refs[-1]
        cuts = ((outs[0], outs[1]), (outs[2], outs[3]), (outs[4], outs[5]), (outs[6], outs[7]))

        def put(far_x, far_y, level, window, value):
            target = cuts[2 * far_x + far_y][level // half]
            target[(level % half, *window)] = value

        used, column = 0, 0
        if patch is not None:
            left, right = ins[0], ins[1]
            width = right.shape[1]
            tall = left.shape[1]
            total[:tall, :width] = dot_tn(left[...], right[...])
            for far_x in (0, 1):
                for far_y in (0, 1):
                    at_x, at_y = spot[0] ^ far_x, spot[1] ^ far_y
                    for level in range(levels):
                        start = pl.multiple_of(((2 * level + at_y) * 2 + at_x) * rows, 8)
                        value = total[pl.ds(start, rows), :width].astype(NARROW_TYPE)
                        put(far_x, far_y, level, (slice(None), slice(0, width)), value)
            used, column = 2, width
        if norms is not None:
            source = ins[used]
            count = source.shape[2]
            for far_x in (0, 1):
                for far_y in (0, 1):
                    at_x, at_y = spot[0] ^ far_x, spot[1] ^ far_y
                    for level in range(levels):
                        window = (slice(None), slice(column, column + LANES))
                        put(far_x, far_y, level, window, source[at_x, 2 * level + at_y])
            used, column = used + 1, column + LANES
        for number, (_, right) in enumerate(pieces):
            left_ref, right_ref = ins[used + 2 * number], ins[used + 2 * number + 1]
            width = right.shape[2]
            tall = left_ref.shape[1]
            for far_x in (0, 1):
                at_x = spot[0] ^ far_x
                total[:tall, :width] = dot_tn(left_ref[...], right_ref[at_x])
                for far_y in (0, 1):
                    at_y = spot[1] ^ far_y
                    for level in range(levels):
                        start = pl.multiple_of((2 * level + at_y) * rows, 8)
                        value = total[pl.ds(start, rows), :width].astype(NARROW_TYPE)
                        put(far_x, far_y, level, (slice(None), slice(column, column + width)), value)
            column += width

    outs = [((half, rows, columns), NARROW_TYPE)] * 8
    flat = [array for piece in pieces for array in piece]
    return vmem_call(
        body,
        outs,
        *extra,
        *flat,
        scalars=(jnp.stack([x, y]),),
        scratch=[pltpu.VMEM((tallest, widest), FLOAT_TYPE)],
        flops=flops,
    )


def add(*terms):
    return sum(term.astype(FLOAT_TYPE) for term in terms)


class Collect:
    def __init__(self, *cuts):
        self.direct = None
        self.mark = ()
        if len(cuts) == 1:
            self.direct = lax.psum_scatter(cuts[0], ("x", "z", "y"), scatter_dimension=0)
            return
        self.own, self.by_y, self.by_x, corner = cuts[:2], cuts[2:4], cuts[4:6], cuts[6:]
        self.corner = (swap(corner[0], "x"), swap(corner[1], "y"))
        self.early = (swap(self.by_x[0], "x"), swap(self.by_y[1], "y"))

    def second(self, *earlier):
        if self.direct is not None:
            return ()
        from_x, from_y = lax.optimization_barrier((*self.corner, *earlier))[:2]
        to_y, to_x = low(add(self.by_y[0], from_x)), low(add(self.by_x[1], from_y))
        self.late = (swap(to_y, "y"), swap(to_x, "x"))
        return to_y, to_x

    def third(self, *earlier):
        if self.direct is not None:
            return ()
        x_low, y_high, y_low, x_high = lax.optimization_barrier((*self.early, *self.late, *earlier))[:4]
        column = jnp.concatenate(
            [low(add(self.own[0], x_low, y_low)), low(add(self.own[1], x_high, y_high))]
        )
        z = lax.axis_index("z")
        parts = [lax.dynamic_index_in_dim(column, (z + n) % 4, 0, keepdims=False) for n in range(4)]
        self.mine = parts[0]
        self.moved = [shift(part, "z", step) for step, part in enumerate(parts[1:], 1)]
        return tuple(parts)

    def total(self, *earlier):
        if self.direct is not None:
            return self.direct.astype(FLOAT_TYPE)
        return add(self.mine, *lax.optimization_barrier((*self.moved, *earlier))[:3])


def dot_nn(left, right):
    return jnp.dot(left, right, preferred_element_type=FLOAT_TYPE)


def dot_nt(left, right):
    return lax.dot_general(left, right, (((1,), (1,)), ((), ())), preferred_element_type=FLOAT_TYPE)


def dot_tn(left, right):
    return lax.dot_general(left, right, (((0,), (0,)), ((), ())), preferred_element_type=FLOAT_TYPE)


def angles_of(places, features):
    half_width = features // 2
    freqs = jnp.exp(-jnp.log(10000.0) * jnp.arange(half_width, dtype=FLOAT_TYPE) / half_width)
    angles = places.astype(FLOAT_TYPE)[:, None] * freqs[None, :]
    return jnp.concatenate([jnp.sin(angles), jnp.cos(angles)], axis=1)


def places_of(count, features):
    half_width = features // 2
    powers = np.arange(half_width, dtype=np.float32) / np.float32(half_width)
    freqs = np.exp(-np.log(np.float32(10000.0)) * powers)
    angles = np.arange(count, dtype=np.float32)[:, None] * freqs[None, :]
    return jnp.asarray(np.concatenate([np.sin(angles), np.cos(angles)], axis=1))


def norm_state(stream):
    centred = stream - jnp.mean(stream, -1, keepdims=True)
    inverse = lax.rsqrt(jnp.mean(centred * centred, -1, keepdims=True) + EPS_NORM)
    return centred * inverse, inverse


def norm_low(stream, gains, row):
    return low(norm_state(stream)[0] * gains[row : row + 1, :] + gains[row + 1 : row + 2, :])


def norm_back(upstream, stream, gains, row):
    scaled, inverse = norm_state(stream)
    weighted = upstream * gains[row : row + 1, :]
    input_grad = inverse * (
        weighted
        - jnp.mean(weighted, -1, keepdims=True)
        - scaled * jnp.mean(weighted * scaled, -1, keepdims=True)
    )
    sums = (jnp.sum(upstream * scaled, 0, keepdims=True), jnp.sum(upstream, 0, keepdims=True))
    return input_grad, sums


def head_masks(width, count):
    size = width // count
    lane = lax.broadcasted_iota(jnp.int32, (1, width), 1)
    return [
        jnp.where((lane >= head * size) & (lane < (head + 1) * size), 1.0, 0.0).astype(NARROW_TYPE)
        for head in range(count)
    ]


def attn_fwd(stream, gains, w_qkv, w_proj, head_count):
    length, features = stream.shape
    width = w_proj.shape[2]
    factor = (width // head_count) ** (-0.5)

    def body(stream, gains, w_qkv, w_proj, partial, triple, mixture, log_total):
        normed = norm_low(stream[...], gains, 0)
        masks = head_masks(width, head_count)
        output = None
        for part in (0, 1):
            projected = low(dot_nn(normed, w_qkv[part]))
            triple[part] = projected
            query, key, value = (projected[:, n * width : (n + 1) * width] for n in range(3))
            mixed = None
            for head, mask in enumerate(masks):
                scores = dot_nt(query * mask, key) * factor
                largest = jnp.max(scores, -1, keepdims=True)
                powers = jnp.exp(scores - largest)
                total = jnp.sum(powers, -1, keepdims=True)
                number = part * head_count + head
                log_total[:, number : number + 1] = largest + jnp.log(total)
                term = dot_nn(low(powers * (1.0 / total)), value * mask)
                mixed = term if mixed is None else mixed + term
            mixed = low(mixed)
            mixture[part] = mixed
            term = dot_nt(mixed, w_proj[part])
            output = term if output is None else output + term
        partial[...] = output

    outs = [
        ((length, features), FLOAT_TYPE),
        ((2, length, 3 * width), NARROW_TYPE),
        ((2, length, width), NARROW_TYPE),
        ((length, 2 * head_count), FLOAT_TYPE),
    ]
    flops = 16 * length * features * width + 8 * head_count * length * length * width
    return vmem_call(body, outs, stream, gains, w_qkv, w_proj, flops=flops)


def attn_back(stream_grad, own, other, middle, stream, kept, gains, w_qkv, w_proj, head_count):
    length, features = stream.shape
    width = w_proj.shape[2]
    factor = (width // head_count) ** (-0.5)
    triple, log_total = kept

    def body(
        stream_grad, own, other, middle, stream, triple, log_total, gains, w_qkv, w_proj,
        new_grad, grad_low, normed, triple_grad, partial, norm_grads,
    ):
        upstream = own[...].astype(FLOAT_TYPE) + other[...].astype(FLOAT_TYPE)
        input_grad, sums = norm_back(upstream, middle[...], gains, 2)
        norm_grads[0:1, :], norm_grads[1:2, :] = sums
        upstream = stream_grad[...] + input_grad
        new_grad[...] = upstream
        upstream = low(upstream)
        grad_low[...] = upstream
        normed[...] = norm_low(stream[...], gains, 0)
        masks = head_masks(width, head_count)
        output = None
        for part in (0, 1):
            projected = triple[part]
            query, key, value = (projected[:, n * width : (n + 1) * width] for n in range(3))
            mix_grad = low(dot_nn(upstream, w_proj[part]))
            query_grad = key_grad = value_grad = None
            for head, mask in enumerate(masks):
                query_part, mix_part = query * mask, mix_grad * mask
                number = part * head_count + head
                scores = dot_nt(query_part, key) * factor
                attend = jnp.exp(scores - log_total[:, number : number + 1])
                attend_grad = dot_nt(mix_part, value)
                inner = jnp.sum(attend * attend_grad, -1, keepdims=True)
                score_grad = low(attend * (attend_grad - inner))
                terms = (
                    dot_nn(score_grad, key * mask),
                    dot_tn(score_grad, query_part),
                    dot_tn(low(attend), mix_part),
                )
                if head == 0:
                    query_grad, key_grad, value_grad = terms
                else:
                    query_grad, key_grad, value_grad = (
                        query_grad + terms[0],
                        key_grad + terms[1],
                        value_grad + terms[2],
                    )
            grads = (low(query_grad * factor), low(key_grad * factor), low(value_grad))
            for number, grad in enumerate(grads):
                triple_grad[part, :, number * width : (number + 1) * width] = grad
            term = dot_nt(triple_grad[part], w_qkv[part])
            output = term if output is None else output + term
        partial[...] = low(output)

    outs = [
        ((length, features), FLOAT_TYPE),
        ((length, features), NARROW_TYPE),
        ((length, features), NARROW_TYPE),
        ((2, length, 3 * width), NARROW_TYPE),
        ((length, features), NARROW_TYPE),
        ((2, features), FLOAT_TYPE),
    ]
    flops = 16 * length * features * width + 20 * head_count * length * length * width
    return vmem_call(
        body, outs, stream_grad, own, other, middle, stream, triple, log_total, gains, w_qkv, w_proj,
        flops=flops,
    )


def mlp_fwd(stream, own, other, gains, w_up, w_down):
    length, features = stream.shape
    width = w_up.shape[2]

    def body(stream, own, other, gains, w_up, w_down, middle, partial):
        values = stream[...] + (own[...] + other[...])
        middle[...] = values
        normed = norm_low(values, gains, 2)
        output = None
        for part in (0, 1):
            upward = dot_nn(normed, w_up[part])
            hidden = low(0.5 * upward * (1.0 + lax.erf(upward * SQRT_HALF)))
            term = dot_nt(hidden, w_down[part])
            output = term if output is None else output + term
        partial[...] = output

    outs = [((length, features), FLOAT_TYPE)] * 2
    flops = 8 * length * features * width
    return vmem_call(body, outs, stream, own, other, gains, w_up, w_down, flops=flops)


def mlp_back(upstream, last, middle, gains, w_up, w_down):
    length, features = last.shape
    width = w_up.shape[2]
    count = len(upstream)

    def body(*refs):
        last, middle, gains, w_up, w_down = refs[count : count + 5]
        new_grad, grad_low, normed_low, hidden_low, upward_low, partial, norm_grads = refs[count + 5 :]
        arrived = add(*(ref[...] for ref in refs[:count]))
        input_grad, sums = norm_back(arrived, last[...], gains, 4)
        norm_grads[0:1, :], norm_grads[1:2, :] = sums
        new_grad[...] = input_grad
        grad = low(input_grad)
        grad_low[...] = grad
        normed = norm_low(middle[...], gains, 2)
        normed_low[...] = normed
        output = None
        for part in (0, 1):
            upward = dot_nn(normed, w_up[part])
            below = 0.5 * (1.0 + lax.erf(upward * SQRT_HALF))
            hidden_low[part] = low(upward * below)
            slope = below + upward * (jnp.exp(-0.5 * upward * upward) * DENSITY)
            upward_grad = low(dot_nn(grad, w_down[part]) * slope)
            upward_low[part] = upward_grad
            term = dot_nt(upward_grad, w_up[part])
            output = term if output is None else output + term
        partial[...] = low(output)

    outs = [
        ((length, features), FLOAT_TYPE),
        ((length, features), NARROW_TYPE),
        ((length, features), NARROW_TYPE),
        ((2, length, width), NARROW_TYPE),
        ((2, length, width), NARROW_TYPE),
        ((length, features), NARROW_TYPE),
        ((2, features), FLOAT_TYPE),
    ]
    flops = 12 * length * features * width
    return vmem_call(body, outs, *upstream, last, middle, gains, w_up, w_down, flops=flops)


def between(middle, own, other, gains, embed, chosen, hidden_row, mask_token, places):
    length, features = middle.shape
    tokens, width = places.shape

    def body(middle, own, other, gains, embed, chosen, hidden_row, mask_token, places, last, normed_low, stream):
        values = middle[...] + (own[...] + other[...])
        last[...] = values
        normed = norm_low(values, gains, 4)
        normed_low[...] = normed
        embedded = dot_nn(normed, embed[...])
        high = low(embedded)
        rest = low(embedded - high.astype(FLOAT_TYPE))
        placed = dot_tn(chosen[...], high) + dot_tn(chosen[...], rest)
        stream[...] = placed + hidden_row[...] * mask_token[...] + places[...]

    outs = [
        ((length, features), FLOAT_TYPE),
        ((length, features), NARROW_TYPE),
        ((tokens, width), FLOAT_TYPE),
    ]
    return vmem_call(body, outs, middle, own, other, gains, embed, chosen, hidden_row, mask_token, places)


def head_loss(middle, own, other, gains, w_head, goal, mask):
    length, features = middle.shape
    width = w_head.shape[2]

    def body(middle, own, other, gains, w_head, goal, mask, last, normed_low, pred_low, partial, loss):
        values = middle[...] + (own[...] + other[...])
        last[...] = values
        normed = norm_low(values, gains, 4)
        normed_low[...] = normed
        weights = mask[...]
        output, lost = None, None
        for part in (0, 1):
            errors = dot_nn(normed, w_head[part]) - goal[part]
            weighted = weights * errors
            square = jnp.sum(weighted * errors, 0, keepdims=True)
            pred_grad = low(weighted * 2.0)
            pred_low[part] = pred_grad
            term = dot_nt(pred_grad, w_head[part])
            output = term if output is None else output + term
            lost = square if lost is None else lost + square
        partial[...] = low(output)
        loss[...] = lost

    outs = [
        ((length, features), FLOAT_TYPE),
        ((length, features), NARROW_TYPE),
        ((2, length, width), NARROW_TYPE),
        ((length, features), NARROW_TYPE),
        ((1, width), FLOAT_TYPE),
    ]
    flops = 8 * length * features * width
    return vmem_call(body, outs, middle, own, other, gains, w_head, goal, mask, flops=flops)


def decoder_end(stream_grad, own, other, stream, gains, chosen, hidden_row, embed, place):
    length, features = stream.shape
    vis_count = chosen.shape[0]
    quarter = features // 4

    def body(
        place, stream_grad, own, other, stream, gains, chosen, hidden_row, embed,
        embed_mine, normed_grad, mask_grad, norm_grads,
    ):
        upstream = own[...].astype(FLOAT_TYPE) + other[...].astype(FLOAT_TYPE)
        input_grad, sums = norm_back(upstream, stream[...], gains, 0)
        norm_grads[0:1, :], norm_grads[1:2, :] = sums
        grad = stream_grad[...] + input_grad
        mask_grad[...] = jnp.sum(grad * hidden_row[...], 0, keepdims=True)
        embedded = low(dot_nn(chosen[...], low(grad)))
        for part in (0, 1):
            start = 2 * part * quarter
            cuts = [embedded[:, start + n * quarter : start + (n + 1) * quarter] for n in (0, 1)]
            embed_mine[part] = jnp.where(place[0] == 0, *cuts)
        normed_grad[...] = dot_nt(embedded, embed[...])

    outs = [
        ((2, vis_count, quarter), NARROW_TYPE),
        ((vis_count, embed.shape[0]), FLOAT_TYPE),
        ((1, features), FLOAT_TYPE),
        ((2, features), FLOAT_TYPE),
    ]
    return vmem_call(
        body, outs, stream_grad, own, other, stream, gains, chosen, hidden_row, embed, scalars=(place,)
    )


def encoder_end(stream_grad, own, other, stream, gains, place):
    length, features = stream.shape
    half = features // 2

    def body(place, stream_grad, own, other, stream, gains, grad_mine, norm_grads):
        upstream = own[...].astype(FLOAT_TYPE) + other[...].astype(FLOAT_TYPE)
        input_grad, sums = norm_back(upstream, stream[...], gains, 0)
        norm_grads[0:1, :], norm_grads[1:2, :] = sums
        grad = low(stream_grad[...] + input_grad)
        grad_mine[...] = jnp.where(place[0] == 0, grad[:, :half], grad[:, half:])

    outs = [((length, half), NARROW_TYPE), ((2, features), FLOAT_TYPE)]
    return vmem_call(body, outs, stream_grad, own, other, stream, gains, scalars=(place,))


def adam_update(weight, moment, second, gradient, step_rate, decay_rate):
    moment = BETA_ONE * moment + (1.0 - BETA_ONE) * gradient
    second = BETA_TWO * second + (1.0 - BETA_TWO) * gradient * gradient
    fixed_one = moment / (1.0 - BETA_ONE**STEP)
    fixed_two = second / (1.0 - BETA_TWO**STEP)
    weight = weight - step_rate * (
        fixed_one / (jnp.sqrt(fixed_two) + ADAM_EPS) + decay_rate * weight
    )
    return [weight, moment, second]


def adam_all(scale, masters, moments, seconds, grads):
    orders = ((1, 0, 2), None, (1, 0, 2), (0, 2, 1))
    shapes = [array.shape for array in masters]

    def view(array, number):
        if number < 4:
            return array if orders[number] is None else array.transpose(orders[number])
        return array.reshape(-1, LANES) if array.ndim == 1 else array

    def unview(array, number):
        if number < 4 and orders[number] is not None:
            return array.transpose(np.argsort(orders[number]))
        return array.reshape(shapes[number])

    triples = [
        [view(array, number) for array in (masters[number], moments[number], seconds[number])]
        for number in range(8)
    ]
    grads = [view(grad, 7) if number == 7 else grad for number, grad in enumerate(grads)]

    def body(scale, *refs):
        arrays, gradients, outs = refs[:24], refs[24:32], refs[32:]
        factor = scale[0]
        for number in range(8):
            ins, news = arrays[3 * number : 3 * number + 3], outs[3 * number : 3 * number + 3]
            step_rate = LR_NORM if number == 7 else LR_MATRIX
            decay_rate = 0.0 if number == 7 else DECAY
            blocks = ins[0].shape[0] if number < 4 else 1
            for block in range(blocks):
                if number < 4:
                    width = ins[0].shape[1] if number == 1 else ins[0].shape[2]
                    grad = gradients[number][:, block * width : (block + 1) * width]
                    grad = grad.T if number == 1 else grad
                    values = [ref[block] for ref in ins]
                else:
                    grad = gradients[number][...].astype(FLOAT_TYPE)
                    values = [ref[...] for ref in ins]
                results = adam_update(*values, grad * factor, step_rate, decay_rate)
                for ref, result in zip(news, results):
                    if number < 4:
                        ref[block] = result
                    else:
                        ref[...] = result

    flat = [array for triple in triples for array in triple]
    outs = [(array.shape, FLOAT_TYPE) for array in flat]
    results = vmem_call(body, outs, *flat, *grads, scalars=(scale[None],))
    return [unview(result, index // 3) for index, result in enumerate(results)]


def from_all(piece, x, c):
    there = [piece, swap(piece, "c"), swap(piece, "x"), lax.ppermute(piece, ("x", "c"), ACROSS)]
    ordered = []
    for number in range(4):
        at_x, at_c = x ^ (number // 2), c ^ (number % 2)
        ordered.append(
            jnp.where(
                at_x == 0,
                jnp.where(at_c == 0, there[0], there[1]),
                jnp.where(at_c == 0, there[2], there[3]),
            )
        )
    return ordered


def both(piece, axis, place, dimension):
    other = swap(piece, axis)
    return jnp.where(
        place == 0,
        jnp.concatenate([piece, other], dimension),
        jnp.concatenate([other, piece], dimension),
    )


def halves_of(array, place):
    half = array.shape[1] // 2
    return jnp.where(place == 0, array[:, :half], array[:, half:])


def one_hot(visible_row, tokens):
    return visible_row[:, None] == jnp.arange(tokens)[None, :]


def pick(array, index, axis=0):
    return lax.dynamic_index_in_dim(array, index, axis, keepdims=False)


def columns_of(blob, widths):
    pieces, start = [], 0
    for width in widths:
        pieces.append(blob[..., start : start + width])
        start += width
    return pieces


def on_device(
    pixels,
    visible,
    valid,
    row_dest,
    encoder_in,
    encoder_in_moment,
    encoder_in_second,
    encoder_out,
    encoder_out_moment,
    encoder_out_second,
    decoder_in,
    decoder_in_moment,
    decoder_in_second,
    decoder_out,
    decoder_out_moment,
    decoder_out_second,
    patch_embed,
    patch_embed_moment,
    patch_embed_second,
    decoder_embed,
    decoder_embed_moment,
    decoder_embed_second,
    pixel_head,
    pixel_head_moment,
    pixel_head_second,
    norm_params,
    norm_params_moment,
    norm_params_second,
):
    masters = [
        encoder_in,
        encoder_out,
        decoder_in,
        decoder_out,
        patch_embed,
        decoder_embed,
        pixel_head,
        norm_params,
    ]
    moments = [
        encoder_in_moment,
        encoder_out_moment,
        decoder_in_moment,
        decoder_out_moment,
        patch_embed_moment,
        decoder_embed_moment,
        pixel_head_moment,
        norm_params_moment,
    ]
    seconds = [
        encoder_in_second,
        encoder_out_second,
        decoder_in_second,
        decoder_out_second,
        patch_embed_second,
        decoder_embed_second,
        pixel_head_second,
        norm_params_second,
    ]
    x, c = lax.axis_index("x"), lax.axis_index("c")
    data_size = lax.axis_size("z") * lax.axis_size("y")
    slot_total, tokens, pix_width = pixels.shape
    vis_count = visible.shape[1]
    patch_positions = valid.shape[2]
    rows_enc, _, part_enc = encoder_in.shape
    rows_dec, _, part_dec = decoder_in.shape
    width_enc, width_dec = patch_embed.shape[1], decoder_embed.shape[1]
    enc_heads = HEADS_ENC // 4
    dec_heads = HEADS_DEC // 4

    patch_rows = patch_embed.shape[0] // 2
    half_enc, quarter_dec = width_enc // 2, width_dec // 4
    patch_piece = lax.dynamic_slice(
        low(patch_embed), (x * patch_rows, c * half_enc), (patch_rows, half_enc)
    )
    embed_piece = lax.dynamic_slice(
        low(decoder_embed), (0, (2 * x + c) * quarter_dec), (rows_enc, quarter_dec)
    )
    norm_share, norm_room = norm_params.shape[0], rows_enc * LANES
    norm_piece = jnp.pad(low(norm_params), (0, norm_room - norm_share)).reshape(rows_enc, LANES)
    enc_in_low = low(encoder_in).reshape(rows_enc, -1)
    enc_out_low = low(encoder_out).transpose(2, 0, 1).reshape(rows_enc, -1)
    dec_in_low = low(decoder_in).reshape(rows_dec, -1)
    dec_out_low = low(decoder_out).transpose(2, 0, 1).reshape(rows_dec, -1)
    head_low = low(pixel_head)
    first_blob = jnp.concatenate(
        [patch_piece, norm_piece, enc_in_low[:, : 3 * part_enc], enc_out_low[:, :part_enc]], 1
    )
    second_blob = jnp.concatenate(
        [enc_in_low[:, 3 * part_enc :], enc_out_low[:, part_enc:], embed_piece], 1
    )
    third_blob = jnp.concatenate([dec_in_low, dec_out_low, head_low], 1)
    widths = (
        (half_enc, LANES, 3 * part_enc, part_enc),
        (4 * part_enc, 4 * part_enc, quarter_dec),
        (3 * part_dec, 4 * part_dec, part_dec, 4 * part_dec, head_low.shape[1]),
    )

    buf_rows = data_size * -(-(slot_total * vis_count) // data_size)
    alive = row_dest[:, 0] < buf_rows
    use_own = pick(alive, x)
    half_step = lax.axis_size("z") // 2

    def shown_of(visible_row):
        return jnp.any(one_hot(visible_row, tokens), axis=0).astype(FLOAT_TYPE)

    start = after(x, first_blob)
    away = slot_total - 1 - start
    own_slot, away_slot = pick(pixels, start), pick(pixels, away)

    def seen_of(slot, rows):
        return low(product("vt,tp->vp", low(one_hot(pick(visible, slot), tokens)), rows))

    visible_row = jnp.where(use_own, pick(visible, start), shift(pick(visible, away), "z", half_step))
    seen_away = shift(halves_of(seen_of(away, away_slot), c), "z", half_step)

    (first_all, second_all, third_all), marks = spread_all(
        (first_blob, second_blob, third_blob), widths, seen_away
    )

    patch_all, norm_all, enc_qkv, enc_proj = first_all
    enc_up, enc_down, embed_all = second_all
    dec_qkv, dec_up, dec_proj, dec_down, head_all = third_all
    patch_all = patch_all.reshape(2, data_size, patch_rows, half_enc).transpose(1, 0, 2, 3)
    patch_all = patch_all.reshape(pix_width, half_enc)
    embed_other = swap(embed_all)
    embed_even = jnp.where(c == 0, embed_all, embed_other)
    embed_odd = jnp.where(c == 0, embed_other, embed_all)
    full_embed = jnp.concatenate([embed_even[0], embed_odd[0], embed_even[1], embed_odd[1]], 1)
    norm_full = norm_all[0].reshape(data_size, norm_room)[:, :norm_share].reshape(-1)
    norm_full = norm_full.astype(FLOAT_TYPE)
    enc_gains = norm_full[: 6 * width_enc].reshape(6, width_enc)
    dec_gains = norm_full[6 * width_enc : 6 * width_enc + 6 * width_dec].reshape(6, width_dec)
    mask_token = norm_full[6 * width_enc + 6 * width_dec : 6 * width_enc + 7 * width_dec]

    seen_rows = jnp.where(
        use_own, seen_of(after(start, marks[0]), own_slot), both(seen_away, "c", c, 1)
    )
    chosen = low(one_hot(visible_row, tokens))
    hidden_row = (1.0 - shown_of(visible_row))[:, None]

    visible_late = after(visible, marks[2])
    counted = jnp.stack([1.0 - shown_of(visible_late[slot]) for slot in range(slot_total)])
    counted = counted * alive.astype(FLOAT_TYPE)[:, None]
    valid_count = jnp.sum(counted[:, :, None] * valid.astype(FLOAT_TYPE))
    valid_count = valid_count * (pix_width // patch_positions)

    def pixels_of(slot, rows):
        place = after(c, marks[1])
        half = pix_width // 2
        cols = [halves_of(rows[:, first : first + half], place) for first in (0, half)]
        return jnp.concatenate(cols + [low(pick(valid, slot))], 1)

    own_pack, away_pack = pixels_of(start, own_slot), pixels_of(away, away_slot)
    pack_moved = shift(after(away_pack, marks[3]), "z", half_step)

    enc_stream = both(product("lp,pd->ld", seen_rows, patch_all), "c", c, 1)
    enc_stream = enc_stream + angles_of(visible_row, width_enc)
    partial, enc_triple, enc_mixture, enc_log = attn_fwd(
        enc_stream, enc_gains, enc_qkv, enc_proj, enc_heads
    )
    enc_middle, partial = mlp_fwd(enc_stream, partial, swap(partial), enc_gains, enc_up, enc_down)
    enc_last, enc_normed, dec_stream = between(
        enc_middle,
        partial,
        swap(partial),
        enc_gains,
        full_embed,
        chosen,
        hidden_row,
        mask_token[None],
        places_of(tokens, width_dec),
    )

    partial, dec_triple, dec_mixture, dec_log = attn_fwd(
        dec_stream, dec_gains, dec_qkv, dec_proj, dec_heads
    )
    dec_middle, partial = mlp_fwd(dec_stream, partial, swap(partial), dec_gains, dec_up, dec_down)

    pixel_pack = jnp.where(use_own, own_pack, after(pack_moved, dec_stream))
    pixel_cols = pixel_pack[:, : pix_width // 2].astype(FLOAT_TYPE)
    valid_cols = pixel_pack[:, pix_width // 2 :].astype(FLOAT_TYPE)
    half_mean = jnp.mean(pixel_cols, -1, keepdims=True)
    half_square = jnp.sum((pixel_cols - half_mean) ** 2, -1, keepdims=True)
    half_both = jnp.concatenate([half_mean, half_square], 1)
    other_both = swap(half_both)
    mean = 0.5 * (half_both[:, :1] + other_both[:, :1])
    gap = half_both[:, :1] - other_both[:, :1]
    variance = (half_both[:, 1:] + other_both[:, 1:]) / pix_width + 0.25 * gap * gap
    target = (pixel_cols - mean) * lax.rsqrt(variance + EPS_PIX)
    half_positions = patch_positions // 2
    front = jnp.where(c == 0, valid_cols[:, :half_positions], valid_cols[:, half_positions:])
    back = jnp.where(c == 0, valid_cols[:, half_positions:], valid_cols[:, :half_positions])
    part_mask = jnp.concatenate([front, back, front], 1) * hidden_row
    goal = jnp.stack([target[:, : pix_width // 4], target[:, pix_width // 4 :]])
    dec_last, dec_normed, pred_low, partial, loss_part = head_loss(
        dec_middle,
        partial,
        swap(partial),
        dec_gains,
        head_all,
        goal,
        part_mask,
    )
    loss_part = jnp.sum(loss_part)

    stream_grad, grad_low, normed_low, hidden_low, upward_low, partial, dec_norms_three = mlp_back(
        (partial, swap(partial)), dec_last, dec_middle, dec_gains, dec_up, dec_down
    )
    dec_tail = Collect(
        *share(
            [(normed_low, upward_low), (grad_low, hidden_low), (dec_normed, pred_low)], rows_dec
        )
    )
    stream_grad, grad_low, normed_low, triple_grad, partial, dec_norms_two = attn_back(
        stream_grad,
        partial,
        swap(partial),
        dec_middle,
        dec_stream,
        (dec_triple, dec_log),
        dec_gains,
        dec_qkv,
        dec_proj,
        dec_heads,
    )
    normed_low = after(normed_low, *dec_tail.second(triple_grad))
    dec_attn = Collect(*share([(normed_low, triple_grad), (grad_low, dec_mixture)], rows_dec))
    embed_mine, normed_grad, mask_grad, dec_norms_one = decoder_end(
        stream_grad,
        partial,
        swap(partial),
        dec_stream,
        dec_gains,
        chosen,
        hidden_row,
        full_embed,
        c[None],
    )

    stream_grad, grad_low, normed_low, hidden_low, upward_low, partial, enc_norms_three = mlp_back(
        (after(normed_grad, *dec_attn.second(), *dec_tail.third(normed_grad)),), enc_last, enc_middle, enc_gains, enc_up, enc_down
    )
    enc_tail = Collect(
        *share([(normed_low, upward_low), (grad_low, hidden_low), (enc_normed, embed_mine)], rows_enc)
    )
    other_partial = after(swap(partial), *dec_attn.third(*enc_tail.mark))
    stream_grad, grad_low, normed_low, triple_grad, partial, enc_norms_two = attn_back(
        stream_grad,
        partial,
        other_partial,
        enc_middle,
        enc_stream,
        (enc_triple, enc_log),
        enc_gains,
        enc_qkv,
        enc_proj,
        enc_heads,
    )
    other_partial = after(swap(partial), *enc_tail.second(partial))
    patch_right, enc_norms_one = encoder_end(
        stream_grad, partial, other_partial, enc_stream, enc_gains, c[None]
    )
    norm_pieces = jnp.concatenate(
        [
            grads.reshape(-1)
            for grads in (
                enc_norms_one,
                enc_norms_two,
                enc_norms_three,
                dec_norms_one,
                dec_norms_two,
                dec_norms_three,
                mask_grad,
            )
        ]
    )
    norm_total = norm_params.shape[0] * data_size
    norm_grad = jnp.concatenate(
        [norm_pieces, jnp.zeros((norm_total - norm_pieces.shape[0],), FLOAT_TYPE)]
    )
    norm_half = norm_share // 2
    norm_grads = low(norm_grad).reshape(data_size, 2, norm_half).transpose(1, 0, 2)
    norm_grads = jnp.pad(norm_grads, ((0, 0), (0, 0), (0, norm_room - norm_half)))
    enc_attn = Collect(
        *share(
            [(normed_low, triple_grad), (grad_low, enc_mixture)],
            rows_enc,
            (seen_rows, patch_right),
            norm_grads.reshape(2, data_size, rows_enc, LANES),
        )
    )

    enc_tail_sent = enc_tail.third(*enc_attn.second())
    dec_tail_sum, dec_attn_sum = dec_tail.total(*enc_tail_sent), dec_attn.total(*enc_tail_sent)
    enc_tail_sum = enc_tail.total(*enc_attn.third())
    enc_attn_sum = enc_attn.total()
    patch_sum, norm_sum, qkv_sum, proj_sum = columns_of(enc_attn_sum, widths[0])
    up_sum, down_sum, embed_sum = columns_of(enc_tail_sum, widths[1])
    dec_qkv_sum, dec_proj_sum = columns_of(dec_attn_sum, (3 * part_dec, part_dec))
    dec_up_sum, dec_down_sum, head_sum = columns_of(
        dec_tail_sum, (4 * part_dec, 4 * part_dec, head_low.shape[1])
    )
    norm_sum = low(norm_sum.reshape(-1)[:norm_half])
    patch_sum, embed_sum = low(patch_sum), low(embed_sum)
    shared_square = sum(
        jnp.sum(jnp.square(piece.astype(FLOAT_TYPE))) for piece in (patch_sum, embed_sum)
    ) + 0.5 * jnp.sum(jnp.square(norm_sum.astype(FLOAT_TYPE)))
    own_square = sum(
        jnp.sum(jnp.square(piece))
        for piece in (qkv_sum, proj_sum, up_sum, down_sum, dec_attn_sum, dec_tail_sum)
    )
    patch_all = from_all(patch_sum, x, c)
    embed_all = from_all(embed_sum, x, c)
    norm_sum = both(norm_sum, "x", x, 0)
    patch_full = jnp.concatenate([jnp.concatenate([patch_all[n], patch_all[n + 1]], 1) for n in (0, 2)])
    embed_full = jnp.concatenate(embed_all, 1)
    totals = jnp.stack([loss_part, own_square + shared_square, valid_count * 0.25])
    totals = total_over(totals, ("c", "x", "y"))
    totals, patch_full, embed_full, norm_sum = lax.optimization_barrier(
        (totals, patch_full, embed_full, norm_sum)
    )
    totals = total_over(totals, ("z",))
    loss_sum, valid_count = totals[0], totals[2]
    grad_norm = jnp.sqrt(totals[1]) / valid_count
    scale = CLIP / jnp.maximum(grad_norm, CLIP) / valid_count
    grads = (
        jnp.concatenate([qkv_sum, up_sum], 1),
        jnp.concatenate([proj_sum, down_sum], 1),
        jnp.concatenate([dec_qkv_sum, dec_up_sum], 1),
        jnp.concatenate([dec_proj_sum, dec_down_sum], 1),
        patch_full,
        embed_full,
        head_sum,
        norm_sum,
    )
    updated = adam_all(scale, masters, moments, seconds, grads)
    return (loss_sum, valid_count, grad_norm, *updated)


def solution(mesh):
    data, model = mesh.shape["dp"], mesh.shape["mp"]
    inner = Mesh(mesh.devices.reshape(data // 2, 2, model // 2, 2), ("z", "y", "x", "c"))
    data_axes, model_axes = ("z", "y"), ("x", "c")
    rows = P(data_axes)
    into = P(data_axes, None, model_axes)
    out_of = P(None, model_axes, data_axes)
    head = P(data_axes, model_axes)
    weights = (into, out_of, into, out_of, rows, rows, head, rows)
    triples = tuple(spec for spec in weights for _ in range(3))
    return jax.shard_map(
        on_device,
        mesh=inner,
        in_specs=(rows, rows, rows, rows) + triples,
        out_specs=(P(), P(), P()) + triples,
        check_vma=False,
    )
```

```python
import numpy as np

import jax
import jax.numpy as jnp
from jax import lax
from jax.experimental import pallas as pl
from jax.experimental.pallas import tpu as pltpu
from jax.sharding import Mesh
from jax.sharding import PartitionSpec as P

HEADS_ENC = 12
HEADS_DEC = 16
STEP = 10


EPS_NORM = 1e-05
EPS_PIX = 1e-06
CLIP = 0.0002
LR_MATRIX = 0.03
LR_NORM = 0.5
BETA_ONE = 0.9
BETA_TWO = 0.95
ADAM_EPS = 1e-10
DECAY = 0.05
FLOAT_TYPE = jnp.float32
NARROW_TYPE = jnp.bfloat16
SWAP = [(0, 1), (1, 0)]
ACROSS = [(0, 3), (1, 2), (2, 1), (3, 0)]
LANES = 128
VMEM_ROOM = 56 * 2**20
SQRT_HALF = 0.5**0.5
DENSITY = (2.0 * np.pi) ** -0.5
DATA = ("z", "y")


def product(spec, left, right):
    return jnp.einsum(spec, left, right, preferred_element_type=FLOAT_TYPE)


def low(values):
    return values.astype(NARROW_TYPE)


def swap(values, axis="c"):
    return lax.ppermute(values, axis, SWAP)


def join(partial):
    return partial + swap(partial)


def join_low(partial):
    mine = low(partial)
    other = swap(mine)
    return mine.astype(FLOAT_TYPE) + other.astype(FLOAT_TYPE)


def shift(values, axis, step):
    size = lax.axis_size(axis)
    return lax.ppermute(values, axis, [(i, (i + step) % size) for i in range(size)])


def total_over(values, axes):
    for axis in axes:
        size = lax.axis_size(axis)
        if size & (size - 1):
            values = lax.psum(values, axis)
            continue
        step = 1
        while step < size:
            values = values + lax.ppermute(values, axis, [(i, i ^ step) for i in range(size)])
            step *= 2
    return values


def after(value, *others):
    return lax.optimization_barrier((value,) + others)[0]


def vmem_call(body, outs, *ins, scalars=(), scratch=(), flops=0):
    shapes = [jax.ShapeDtypeStruct(shape, kind) for shape, kind in outs]
    moved = sum(int(np.prod(a.shape)) * a.dtype.itemsize for a in [*ins, *shapes])
    return pl.pallas_call(
        body,
        out_shape=shapes,
        in_specs=[pl.BlockSpec(memory_space=pltpu.SMEM)] * len(scalars)
        + [pl.BlockSpec(memory_space=pltpu.VMEM)] * len(ins),
        out_specs=[pl.BlockSpec(memory_space=pltpu.VMEM)] * len(shapes),
        scratch_shapes=list(scratch),
        compiler_params=pltpu.CompilerParams(vmem_limit_bytes=VMEM_ROOM),
        cost_estimate=pl.CostEstimate(flops=flops, bytes_accessed=moved, transcendentals=0),
    )(*scalars, *ins)


class Spread:
    def __init__(self, blob, *earlier):
        self.half = blob.shape[0] // 2
        self.blob = after(blob, *earlier)
        self.near = self.plane(self.blob[None])

    def plane(self, part):
        from_x, from_y = swap(part, "x"), swap(part, "y")
        corner = (swap(from_x[:, : self.half], "y"), swap(from_y[:, self.half :], "x"))
        return from_x, from_y, *corner

    def along_z(self, *earlier):
        blob = after(self.blob, *earlier)
        self.moved = [shift(blob, "z", step) for step in (1, 2, 3)]

    def round_plane(self, *earlier):
        self.stack = after(jnp.stack(self.moved), *earlier)
        self.far = self.plane(self.stack)

    def whole(self, widths):
        rows = self.blob.shape[0]
        x, y, z = (lax.axis_index(axis) for axis in ("x", "y", "z"))
        starts = np.cumsum([0, *widths])

        def body(spot, *refs):
            here_x, here_y, here_z = spot[0], spot[1], spot[2]
            outs = refs[10:]
            for group in (0, 5):
                own, from_x, from_y, low_corner, high_corner = refs[group : group + 5]
                for number in range(own.shape[0]):
                    level = lax.rem(here_z - number + 3 if group else here_z + 4, 4)
                    for ref, at_x, at_y, first in (
                        (own, here_x, here_y, 0),
                        (from_x, 1 - here_x, here_y, 0),
                        (from_y, here_x, 1 - here_y, 0),
                        (low_corner, 1 - here_x, 1 - here_y, 0),
                        (high_corner, 1 - here_x, 1 - here_y, self.half),
                    ):
                        count = ref.shape[1]
                        for out, start, width in zip(outs, starts, widths):
                            out[at_x, level, at_y, first : first + count, :] = ref[
                                number, :, start : start + width
                            ]

        parts = (self.blob[None], *self.near, self.stack, *self.far)
        outs = [((2, 4, 2, rows, width), self.blob.dtype) for width in widths]
        wholes = vmem_call(body, outs, *parts, scalars=(jnp.stack([x, y, z]),))
        return [whole.reshape(2, 8 * rows, -1) for whole in wholes]


def spread_all(blobs, widths, picked):
    sizes = tuple(lax.axis_size(axis) for axis in ("x", "z", "y"))
    if sizes != (2, 4, 2):
        wholes = [lax.all_gather(blob, ("x", "z", "y")) for blob in blobs]
        wholes = [whole.reshape(2, -1, whole.shape[-1]) for whole in wholes]
        pieces = [columns_of(whole, width) for whole, width in zip(wholes, widths)]
        return pieces, [wholes[0]] * 4
    first = Spread(blobs[0])
    first.along_z()
    second, third = (Spread(blob, picked) for blob in blobs[1:])
    second.along_z(*first.moved)
    first.round_plane()
    third.along_z(*first.far[:2])
    second.moved = [after(moved, *first.far[:2]) for moved in second.moved]
    second.round_plane(*first.far)
    third.moved = [after(moved, *second.far[:2]) for moved in third.moved]
    third.round_plane(*second.far)
    pieces = [group.whole(width) for group, width in zip((first, second, third), widths)]
    return pieces, [first.stack, first.far[0], first.far[2], second.far[0]]


def share(pieces, rows, patch=None, norms=None):
    x, y = lax.axis_index("x"), lax.axis_index("y")
    levels = lax.axis_size("z")
    half = levels // 2
    if (lax.axis_size("x"), levels, lax.axis_size("y")) != (2, 4, 2):
        cuts = []
        if patch is not None:
            cut = low(product("ld,lc->dc", *patch)).reshape(2 * levels, 2, rows, -1)
            cuts.append(cut.transpose(1, 0, 2, 3).reshape(2, 2 * levels * rows, -1))
        if norms is not None:
            cuts.append(norms.reshape(2, 2 * levels * rows, -1))
        cuts += [low(product("ld,xlc->xdc", left, right)) for left, right in pieces]
        return (jnp.concatenate(cuts, 2).reshape(4 * levels, rows, -1),)
    extra = []
    columns = 0
    if patch is not None:
        extra += [*patch]
        columns += patch[1].shape[1]
    if norms is not None:
        extra += [norms]
        columns += LANES
    first_column = columns
    for left, right in pieces:
        columns += right.shape[2]
    tallest = max([left.shape[1] for left, _ in pieces] + ([patch[0].shape[1]] if patch else []))
    widest = max([right.shape[2] for _, right in pieces] + ([patch[1].shape[1]] if patch else []))
    flops = sum(4 * left.shape[0] * left.shape[1] * right.shape[2] for left, right in pieces)

    def body(spot, *refs):
        ins, outs = refs[: len(extra) + 2 * len(pieces)], refs[len(extra) + 2 * len(pieces) : -1]
        total = refs[-1]
        cuts = ((outs[0], outs[1]), (outs[2], outs[3]), (outs[4], outs[5]), (outs[6], outs[7]))

        def put(far_x, far_y, level, window, value):
            target = cuts[2 * far_x + far_y][level // half]
            target[(level % half, *window)] = value

        used, column = 0, 0
        if patch is not None:
            left, right = ins[0], ins[1]
            width = right.shape[1]
            tall = left.shape[1]
            total[:tall, :width] = dot_tn(left[...], right[...])
            for far_x in (0, 1):
                for far_y in (0, 1):
                    at_x, at_y = spot[0] ^ far_x, spot[1] ^ far_y
                    for level in range(levels):
                        start = pl.multiple_of(((2 * level + at_y) * 2 + at_x) * rows, 8)
                        value = total[pl.ds(start, rows), :width].astype(NARROW_TYPE)
                        put(far_x, far_y, level, (slice(None), slice(0, width)), value)
            used, column = 2, width
        if norms is not None:
            source = ins[used]
            count = source.shape[2]
            for far_x in (0, 1):
                for far_y in (0, 1):
                    at_x, at_y = spot[0] ^ far_x, spot[1] ^ far_y
                    for level in range(levels):
                        window = (slice(None), slice(column, column + LANES))
                        put(far_x, far_y, level, window, source[at_x, 2 * level + at_y])
            used, column = used + 1, column + LANES
        for number, (_, right) in enumerate(pieces):
            left_ref, right_ref = ins[used + 2 * number], ins[used + 2 * number + 1]
            width = right.shape[2]
            tall = left_ref.shape[1]
            for far_x in (0, 1):
                at_x = spot[0] ^ far_x
                total[:tall, :width] = dot_tn(left_ref[...], right_ref[at_x])
                for far_y in (0, 1):
                    at_y = spot[1] ^ far_y
                    for level in range(levels):
                        start = pl.multiple_of((2 * level + at_y) * rows, 8)
                        value = total[pl.ds(start, rows), :width].astype(NARROW_TYPE)
                        put(far_x, far_y, level, (slice(None), slice(column, column + width)), value)
            column += width

    outs = [((half, rows, columns), NARROW_TYPE)] * 8
    flat = [array for piece in pieces for array in piece]
    return vmem_call(
        body,
        outs,
        *extra,
        *flat,
        scalars=(jnp.stack([x, y]),),
        scratch=[pltpu.VMEM((tallest, widest), FLOAT_TYPE)],
        flops=flops,
    )


def add(*terms):
    return sum(term.astype(FLOAT_TYPE) for term in terms)


class Collect:
    def __init__(self, cuts, *earlier):
        self.direct = None
        self.corner = self.early = self.late = self.moved = ()
        if len(cuts) == 1:
            self.direct = lax.psum_scatter(cuts[0], ("x", "z", "y"), scatter_dimension=0)
            return
        cuts = lax.optimization_barrier((*cuts, *earlier))
        self.own, self.by_y, self.by_x, corner = cuts[:2], cuts[2:4], cuts[4:6], cuts[6:8]
        self.corner = (swap(corner[0], "x"), swap(corner[1], "y"))
        self.early = (swap(self.by_x[0], "x"), swap(self.by_y[1], "y"))

    def second(self, *earlier):
        if self.direct is not None:
            return ()
        from_x, from_y = lax.optimization_barrier((*self.corner, *earlier))[:2]
        to_y, to_x = low(add(self.by_y[0], from_x)), low(add(self.by_x[1], from_y))
        self.late = (swap(to_y, "y"), swap(to_x, "x"))
        return to_y, to_x

    def third(self, *earlier):
        if self.direct is not None:
            return ()
        x_low, y_high, y_low, x_high = lax.optimization_barrier((*self.early, *self.late, *earlier))[:4]
        column = jnp.concatenate(
            [low(add(self.own[0], x_low, y_low)), low(add(self.own[1], x_high, y_high))]
        )
        z = lax.axis_index("z")
        parts = [lax.dynamic_index_in_dim(column, (z + n) % 4, 0, keepdims=False) for n in range(4)]
        self.mine = parts[0]
        self.moved = [shift(part, "z", step) for step, part in enumerate(parts[1:], 1)]
        return tuple(parts)

    def terms(self, *earlier):
        if self.direct is not None:
            return (self.direct,)
        return self.mine, *lax.optimization_barrier((*self.moved, *earlier))[:3]


def dot_nn(left, right):
    return jnp.dot(left, right, preferred_element_type=FLOAT_TYPE)


def dot_nt(left, right):
    return lax.dot_general(left, right, (((1,), (1,)), ((), ())), preferred_element_type=FLOAT_TYPE)


def dot_tn(left, right):
    return lax.dot_general(left, right, (((0,), (0,)), ((), ())), preferred_element_type=FLOAT_TYPE)


def angles_of(places, features):
    half_width = features // 2
    freqs = jnp.exp(-jnp.log(10000.0) * jnp.arange(half_width, dtype=FLOAT_TYPE) / half_width)
    angles = places.astype(FLOAT_TYPE)[:, None] * freqs[None, :]
    return jnp.concatenate([jnp.sin(angles), jnp.cos(angles)], axis=1)


def places_of(count, features):
    half_width = features // 2
    powers = np.arange(half_width, dtype=np.float32) / np.float32(half_width)
    freqs = np.exp(-np.log(np.float32(10000.0)) * powers)
    angles = np.arange(count, dtype=np.float32)[:, None] * freqs[None, :]
    return jnp.asarray(np.concatenate([np.sin(angles), np.cos(angles)], axis=1))


def norm_state(stream):
    centred = stream - jnp.mean(stream, -1, keepdims=True)
    inverse = lax.rsqrt(jnp.mean(centred * centred, -1, keepdims=True) + EPS_NORM)
    return centred * inverse, inverse


def norm_low(stream, gains, row):
    return low(norm_state(stream)[0] * gains[row : row + 1, :] + gains[row + 1 : row + 2, :])


def norm_back(upstream, stream, gains, row):
    scaled, inverse = norm_state(stream)
    weighted = upstream * gains[row : row + 1, :]
    input_grad = inverse * (
        weighted
        - jnp.mean(weighted, -1, keepdims=True)
        - scaled * jnp.mean(weighted * scaled, -1, keepdims=True)
    )
    sums = (jnp.sum(upstream * scaled, 0, keepdims=True), jnp.sum(upstream, 0, keepdims=True))
    return input_grad, sums


def head_masks(width, count):
    size = width // count
    lane = lax.broadcasted_iota(jnp.int32, (1, width), 1)
    return [
        jnp.where((lane >= head * size) & (lane < (head + 1) * size), 1.0, 0.0).astype(NARROW_TYPE)
        for head in range(count)
    ]


def attn_fwd(stream, gains, w_qkv, w_proj, head_count):
    length, features = stream.shape
    width = w_proj.shape[2]
    factor = (width // head_count) ** (-0.5)

    def body(stream, gains, w_qkv, w_proj, partial, triple, mixture, log_total):
        normed = norm_low(stream[...], gains, 0)
        masks = head_masks(width, head_count)
        output = None
        for part in (0, 1):
            projected = low(dot_nn(normed, w_qkv[part]))
            triple[part] = projected
            query, key, value = (projected[:, n * width : (n + 1) * width] for n in range(3))
            mixed = None
            for head, mask in enumerate(masks):
                scores = dot_nt(query * mask, key) * factor
                largest = jnp.max(scores, -1, keepdims=True)
                powers = jnp.exp(scores - largest)
                total = jnp.sum(powers, -1, keepdims=True)
                number = part * head_count + head
                log_total[:, number : number + 1] = largest + jnp.log(total)
                term = dot_nn(low(powers * (1.0 / total)), value * mask)
                mixed = term if mixed is None else mixed + term
            mixed = low(mixed)
            mixture[part] = mixed
            term = dot_nt(mixed, w_proj[part])
            output = term if output is None else output + term
        partial[...] = output

    outs = [
        ((length, features), FLOAT_TYPE),
        ((2, length, 3 * width), NARROW_TYPE),
        ((2, length, width), NARROW_TYPE),
        ((length, 2 * head_count), FLOAT_TYPE),
    ]
    flops = 16 * length * features * width + 8 * head_count * length * length * width
    return vmem_call(body, outs, stream, gains, w_qkv, w_proj, flops=flops)


def attn_back(stream_grad, own, other, middle, stream, kept, gains, w_qkv, w_proj, head_count):
    length, features = stream.shape
    width = w_proj.shape[2]
    factor = (width // head_count) ** (-0.5)
    triple, log_total = kept

    def body(
        stream_grad, own, other, middle, stream, triple, log_total, gains, w_qkv, w_proj,
        new_grad, grad_low, normed, triple_grad, partial, norm_grads,
    ):
        upstream = own[...].astype(FLOAT_TYPE) + other[...].astype(FLOAT_TYPE)
        input_grad, sums = norm_back(upstream, middle[...], gains, 2)
        norm_grads[0:1, :], norm_grads[1:2, :] = sums
        upstream = stream_grad[...] + input_grad
        new_grad[...] = upstream
        upstream = low(upstream)
        grad_low[...] = upstream
        normed[...] = norm_low(stream[...], gains, 0)
        masks = head_masks(width, head_count)
        output = None
        for part in (0, 1):
            projected = triple[part]
            query, key, value = (projected[:, n * width : (n + 1) * width] for n in range(3))
            mix_grad = low(dot_nn(upstream, w_proj[part]))
            query_grad = key_grad = value_grad = None
            for head, mask in enumerate(masks):
                query_part, mix_part = query * mask, mix_grad * mask
                number = part * head_count + head
                scores = dot_nt(query_part, key) * factor
                attend = jnp.exp(scores - log_total[:, number : number + 1])
                attend_grad = dot_nt(mix_part, value)
                inner = jnp.sum(attend * attend_grad, -1, keepdims=True)
                score_grad = low(attend * (attend_grad - inner))
                terms = (
                    dot_nn(score_grad, key * mask),
                    dot_tn(score_grad, query_part),
                    dot_tn(low(attend), mix_part),
                )
                if head == 0:
                    query_grad, key_grad, value_grad = terms
                else:
                    query_grad, key_grad, value_grad = (
                        query_grad + terms[0],
                        key_grad + terms[1],
                        value_grad + terms[2],
                    )
            grads = (low(query_grad * factor), low(key_grad * factor), low(value_grad))
            for number, grad in enumerate(grads):
                triple_grad[part, :, number * width : (number + 1) * width] = grad
            term = dot_nt(triple_grad[part], w_qkv[part])
            output = term if output is None else output + term
        partial[...] = low(output)

    outs = [
        ((length, features), FLOAT_TYPE),
        ((length, features), NARROW_TYPE),
        ((length, features), NARROW_TYPE),
        ((2, length, 3 * width), NARROW_TYPE),
        ((length, features), NARROW_TYPE),
        ((2, features), FLOAT_TYPE),
    ]
    flops = 16 * length * features * width + 20 * head_count * length * length * width
    return vmem_call(
        body, outs, stream_grad, own, other, middle, stream, triple, log_total, gains, w_qkv, w_proj,
        flops=flops,
    )


def mlp_fwd(stream, own, other, gains, w_up, w_down):
    length, features = stream.shape
    width = w_up.shape[2]

    def body(stream, own, other, gains, w_up, w_down, middle, partial):
        values = stream[...] + (own[...] + other[...])
        middle[...] = values
        normed = norm_low(values, gains, 2)
        output = None
        for part in (0, 1):
            upward = dot_nn(normed, w_up[part])
            hidden = low(0.5 * upward * (1.0 + lax.erf(upward * SQRT_HALF)))
            term = dot_nt(hidden, w_down[part])
            output = term if output is None else output + term
        partial[...] = output

    outs = [((length, features), FLOAT_TYPE)] * 2
    flops = 8 * length * features * width
    return vmem_call(body, outs, stream, own, other, gains, w_up, w_down, flops=flops)


def mlp_back(upstream, last, middle, gains, w_up, w_down):
    length, features = last.shape
    width = w_up.shape[2]
    count = len(upstream)

    def body(*refs):
        last, middle, gains, w_up, w_down = refs[count : count + 5]
        new_grad, grad_low, normed_low, hidden_low, upward_low, partial, norm_grads = refs[count + 5 :]
        arrived = add(*(ref[...] for ref in refs[:count]))
        input_grad, sums = norm_back(arrived, last[...], gains, 4)
        norm_grads[0:1, :], norm_grads[1:2, :] = sums
        new_grad[...] = input_grad
        grad = low(input_grad)
        grad_low[...] = grad
        normed = norm_low(middle[...], gains, 2)
        normed_low[...] = normed
        output = None
        for part in (0, 1):
            upward = dot_nn(normed, w_up[part])
            below = 0.5 * (1.0 + lax.erf(upward * SQRT_HALF))
            hidden_low[part] = low(upward * below)
            slope = below + upward * (jnp.exp(-0.5 * upward * upward) * DENSITY)
            upward_grad = low(dot_nn(grad, w_down[part]) * slope)
            upward_low[part] = upward_grad
            term = dot_nt(upward_grad, w_up[part])
            output = term if output is None else output + term
        partial[...] = low(output)

    outs = [
        ((length, features), FLOAT_TYPE),
        ((length, features), NARROW_TYPE),
        ((length, features), NARROW_TYPE),
        ((2, length, width), NARROW_TYPE),
        ((2, length, width), NARROW_TYPE),
        ((length, features), NARROW_TYPE),
        ((2, features), FLOAT_TYPE),
    ]
    flops = 12 * length * features * width
    return vmem_call(body, outs, *upstream, last, middle, gains, w_up, w_down, flops=flops)


def between(middle, own, other, gains, embed, chosen, hidden_row, mask_token, places):
    length, features = middle.shape
    tokens, width = places.shape

    def body(middle, own, other, gains, embed, chosen, hidden_row, mask_token, places, last, normed_low, stream):
        values = middle[...] + (own[...] + other[...])
        last[...] = values
        normed = norm_low(values, gains, 4)
        normed_low[...] = normed
        embedded = dot_nn(normed, embed[...])
        high = low(embedded)
        rest = low(embedded - high.astype(FLOAT_TYPE))
        placed = dot_tn(chosen[...], high) + dot_tn(chosen[...], rest)
        stream[...] = placed + hidden_row[...] * mask_token[...] + places[...]

    outs = [
        ((length, features), FLOAT_TYPE),
        ((length, features), NARROW_TYPE),
        ((tokens, width), FLOAT_TYPE),
    ]
    return vmem_call(body, outs, middle, own, other, gains, embed, chosen, hidden_row, mask_token, places)


def head_loss(middle, own, other, gains, w_head, goal, mask):
    length, features = middle.shape
    width = w_head.shape[2]

    def body(middle, own, other, gains, w_head, goal, mask, last, normed_low, pred_low, partial, loss):
        values = middle[...] + (own[...] + other[...])
        last[...] = values
        normed = norm_low(values, gains, 4)
        normed_low[...] = normed
        weights = mask[...]
        output, lost = None, None
        for part in (0, 1):
            errors = dot_nn(normed, w_head[part]) - goal[part]
            weighted = weights * errors
            square = jnp.sum(weighted * errors, 0, keepdims=True)
            pred_grad = low(weighted * 2.0)
            pred_low[part] = pred_grad
            term = dot_nt(pred_grad, w_head[part])
            output = term if output is None else output + term
            lost = square if lost is None else lost + square
        partial[...] = low(output)
        loss[...] = lost

    outs = [
        ((length, features), FLOAT_TYPE),
        ((length, features), NARROW_TYPE),
        ((2, length, width), NARROW_TYPE),
        ((length, features), NARROW_TYPE),
        ((1, width), FLOAT_TYPE),
    ]
    flops = 8 * length * features * width
    return vmem_call(body, outs, middle, own, other, gains, w_head, goal, mask, flops=flops)


def decoder_end(stream_grad, own, other, stream, gains, chosen, hidden_row, embed, place):
    length, features = stream.shape
    vis_count = chosen.shape[0]
    quarter = features // 4

    def body(
        place, stream_grad, own, other, stream, gains, chosen, hidden_row, embed,
        embed_mine, normed_grad, mask_grad, norm_grads,
    ):
        upstream = own[...].astype(FLOAT_TYPE) + other[...].astype(FLOAT_TYPE)
        input_grad, sums = norm_back(upstream, stream[...], gains, 0)
        norm_grads[0:1, :], norm_grads[1:2, :] = sums
        grad = stream_grad[...] + input_grad
        mask_grad[...] = jnp.sum(grad * hidden_row[...], 0, keepdims=True)
        embedded = low(dot_nn(chosen[...], low(grad)))
        for part in (0, 1):
            start = 2 * part * quarter
            cuts = [embedded[:, start + n * quarter : start + (n + 1) * quarter] for n in (0, 1)]
            embed_mine[part] = jnp.where(place[0] == 0, *cuts)
        normed_grad[...] = dot_nt(embedded, embed[...])

    outs = [
        ((2, vis_count, quarter), NARROW_TYPE),
        ((vis_count, embed.shape[0]), FLOAT_TYPE),
        ((1, features), FLOAT_TYPE),
        ((2, features), FLOAT_TYPE),
    ]
    return vmem_call(
        body, outs, stream_grad, own, other, stream, gains, chosen, hidden_row, embed, scalars=(place,)
    )


def encoder_end(stream_grad, own, other, stream, gains, place):
    length, features = stream.shape
    half = features // 2

    def body(place, stream_grad, own, other, stream, gains, grad_mine, norm_grads):
        upstream = own[...].astype(FLOAT_TYPE) + other[...].astype(FLOAT_TYPE)
        input_grad, sums = norm_back(upstream, stream[...], gains, 0)
        norm_grads[0:1, :], norm_grads[1:2, :] = sums
        grad = low(stream_grad[...] + input_grad)
        grad_mine[...] = jnp.where(place[0] == 0, grad[:, :half], grad[:, half:])

    outs = [((length, half), NARROW_TYPE), ((2, features), FLOAT_TYPE)]
    return vmem_call(body, outs, stream_grad, own, other, stream, gains, scalars=(place,))


def adam_update(weight, moment, second, gradient, step_rate, decay_rate):
    moment = BETA_ONE * moment + (1.0 - BETA_ONE) * gradient
    second = BETA_TWO * second + (1.0 - BETA_TWO) * gradient * gradient
    fixed_one = moment / (1.0 - BETA_ONE**STEP)
    fixed_two = second / (1.0 - BETA_TWO**STEP)
    weight = weight - step_rate * (
        fixed_one / (jnp.sqrt(fixed_two) + ADAM_EPS) + decay_rate * weight
    )
    return [weight, moment, second]


def lane_is(number):
    return lax.broadcasted_iota(jnp.int32, (1, LANES), 1) == number


def sum_early(groups, embed_width):
    count = sum(len(group) for group in groups)

    def body(*refs):
        outs = refs[count:]
        used, square = 0, 0.0
        for number, group in enumerate(groups):
            total = add(*(ref[...] for ref in refs[used : used + len(group)]))
            used += len(group)
            if number == len(groups) - 1:
                embed = low(total[:, total.shape[1] - embed_width :])
                outs[number + 1][...] = embed
                total = total[:, : total.shape[1] - embed_width]
                embed = embed.astype(FLOAT_TYPE)
                square = square + jnp.sum(embed * embed, keepdims=True)
            outs[number][...] = total
            square = square + jnp.sum(total * total, keepdims=True)
        outs[-1][...] = square

    outs = []
    for number, group in enumerate(groups):
        rows, columns = group[0].shape
        outs.append(((rows, columns - embed_width * (number == len(groups) - 1)), FLOAT_TYPE))
    outs += [((groups[-1][0].shape[0], embed_width), NARROW_TYPE), ((1, 1), FLOAT_TYPE)]
    flat = [term for group in groups for term in group]
    *sums, embed, square = vmem_call(body, outs, *flat)
    return sums, embed, square


def sum_late(terms, embed, square, loss_part, valid_count, patch_width):
    count = len(terms)
    rows, columns = terms[0].shape
    split = patch_width + LANES

    def body(*refs):
        embed, square, loss, valid, rest, exchanged, totals = refs[count:]
        total = add(*(ref[...] for ref in refs[:count]))
        kept = total[:, split:]
        rest[...] = kept
        sent = low(total[:, :split])
        exchanged[:, :split] = sent
        exchanged[:, split:] = embed[...]
        sent = sent.astype(FLOAT_TYPE)
        squares = sent * sent
        gathered = (
            square[...]
            + jnp.sum(kept * kept, keepdims=True)
            + jnp.sum(squares[:, :patch_width], keepdims=True)
            + 0.5 * jnp.sum(squares[:, patch_width:], keepdims=True)
        )
        loss = jnp.sum(loss[...], keepdims=True)
        totals[...] = jnp.where(
            lane_is(0), loss, jnp.where(lane_is(1), 0.25 * valid[...], jnp.where(lane_is(2), gathered, 0.0))
        )

    outs = [
        ((rows, columns - split), FLOAT_TYPE),
        ((rows, split + embed.shape[1]), NARROW_TYPE),
        ((1, LANES), FLOAT_TYPE),
    ]
    return vmem_call(body, outs, *terms, embed, square, loss_part, valid_count.reshape(1, 1))


def adam_all(place, totals, masters, moments, seconds, sums, exchanged, norm_sum):
    orders = ((1, 0, 2), None, (1, 0, 2), (0, 2, 1))
    shapes = [array.shape for array in masters]

    def view(array, number):
        if number < 4:
            return array if orders[number] is None else array.transpose(orders[number])
        return array.reshape(-1, LANES) if array.ndim == 1 else array

    def unview(array, number):
        if number < 4 and orders[number] is not None:
            return array.transpose(np.argsort(orders[number]))
        return array.reshape(shapes[number])

    triples = [
        [view(array, number) for array in (masters[number], moments[number], seconds[number])]
        for number in range(8)
    ]
    flat = [array for triple in triples for array in triple]
    part_enc, part_dec = shapes[0][2], shapes[2][2]
    patch_rows, patch_width = shapes[4][0] // 2, shapes[4][1] // 2
    embed_width = shapes[5][1] // 4

    def body(place, totals, *refs):
        arrays, refs = refs[:24], refs[24:]
        (dec_attn, dec_tail, enc_tail, enc_attn, *parts, norm_sum), refs = refs[:9], refs[9:]
        scalars, outs = refs[0], refs[1:]
        loss, count, square = (
            jnp.sum(jnp.where(lane_is(n), totals[...], 0.0), keepdims=True) for n in range(3)
        )
        grad_norm = jnp.sqrt(square) / count
        factor = CLIP / jnp.maximum(grad_norm, CLIP) / count
        scalars[...] = jnp.where(lane_is(0), loss, jnp.where(lane_is(1), count, grad_norm))

        def update(number, where, grad):
            step_rate = LR_NORM if number == 7 else LR_MATRIX
            decay_rate = 0.0 if number == 7 else DECAY
            values = (ref[where] for ref in arrays[3 * number : 3 * number + 3])
            results = adam_update(*values, grad * factor, step_rate, decay_rate)
            for ref, result in zip(outs[3 * number : 3 * number + 3], results):
                ref[where] = result

        def piece(at_x, at_c, columns):
            far_x, far_c = place[0] != at_x, place[1] != at_c
            cuts = [part[:, columns] for part in parts]
            rows = [jnp.where(far_c, cuts[n + 1], cuts[n]) for n in (0, 2)]
            return jnp.where(far_x, rows[1], rows[0]).astype(FLOAT_TYPE)

        for number, attn, tail, width in (
            (0, enc_attn, enc_tail, part_enc),
            (2, dec_attn, dec_tail, part_dec),
        ):
            for block in range(7):
                source, first = (attn, block) if block < 3 else (tail, block - 3)
                update(number, block, source[:, first * width : (first + 1) * width])
            for block in range(5):
                source, first = (attn, 3) if block == 0 else (tail, 3 + block)
                grad = source[:, first * width : (first + 1) * width]
                update(number + 1, block, grad.T if number == 0 else grad)
        for at_x in (0, 1):
            for at_c in (0, 1):
                grad = piece(at_x, at_c, slice(0, patch_width))
                rows = slice(at_x * patch_rows, (at_x + 1) * patch_rows)
                columns = slice(at_c * patch_width, (at_c + 1) * patch_width)
                update(4, (rows, columns), grad)
                first = patch_width + LANES
                grad = piece(at_x, at_c, slice(first, first + embed_width))
                number = 2 * at_x + at_c
                update(5, (slice(None), slice(number * embed_width, (number + 1) * embed_width)), grad)
        update(6, Ellipsis, dec_tail[:, 8 * part_dec :])
        update(7, Ellipsis, norm_sum[...].astype(FLOAT_TYPE))

    outs = [((1, LANES), FLOAT_TYPE)] + [(array.shape, FLOAT_TYPE) for array in flat]
    scalars, *results = vmem_call(
        body, outs, totals, *flat, *sums, *exchanged, view(norm_sum, 7), scalars=(place,)
    )
    return scalars, [unview(result, index // 3) for index, result in enumerate(results)]


def both(piece, axis, place, dimension):
    other = swap(piece, axis)
    return jnp.where(
        place == 0,
        jnp.concatenate([piece, other], dimension),
        jnp.concatenate([other, piece], dimension),
    )


def halves_of(array, place):
    half = array.shape[1] // 2
    return jnp.where(place == 0, array[:, :half], array[:, half:])


def one_hot(visible_row, tokens):
    return visible_row[:, None] == jnp.arange(tokens)[None, :]


def pick(array, index, axis=0):
    return lax.dynamic_index_in_dim(array, index, axis, keepdims=False)


def columns_of(blob, widths):
    pieces, start = [], 0
    for width in widths:
        pieces.append(blob[..., start : start + width])
        start += width
    return pieces


def on_device(
    pixels,
    visible,
    valid,
    row_dest,
    encoder_in,
    encoder_in_moment,
    encoder_in_second,
    encoder_out,
    encoder_out_moment,
    encoder_out_second,
    decoder_in,
    decoder_in_moment,
    decoder_in_second,
    decoder_out,
    decoder_out_moment,
    decoder_out_second,
    patch_embed,
    patch_embed_moment,
    patch_embed_second,
    decoder_embed,
    decoder_embed_moment,
    decoder_embed_second,
    pixel_head,
    pixel_head_moment,
    pixel_head_second,
    norm_params,
    norm_params_moment,
    norm_params_second,
):
    masters = [
        encoder_in,
        encoder_out,
        decoder_in,
        decoder_out,
        patch_embed,
        decoder_embed,
        pixel_head,
        norm_params,
    ]
    moments = [
        encoder_in_moment,
        encoder_out_moment,
        decoder_in_moment,
        decoder_out_moment,
        patch_embed_moment,
        decoder_embed_moment,
        pixel_head_moment,
        norm_params_moment,
    ]
    seconds = [
        encoder_in_second,
        encoder_out_second,
        decoder_in_second,
        decoder_out_second,
        patch_embed_second,
        decoder_embed_second,
        pixel_head_second,
        norm_params_second,
    ]
    x, c = lax.axis_index("x"), lax.axis_index("c")
    data_size = lax.axis_size("z") * lax.axis_size("y")
    slot_total, tokens, pix_width = pixels.shape
    vis_count = visible.shape[1]
    patch_positions = valid.shape[2]
    rows_enc, _, part_enc = encoder_in.shape
    rows_dec, _, part_dec = decoder_in.shape
    width_enc, width_dec = patch_embed.shape[1], decoder_embed.shape[1]
    enc_heads = HEADS_ENC // 4
    dec_heads = HEADS_DEC // 4

    patch_rows = patch_embed.shape[0] // 2
    half_enc, quarter_dec = width_enc // 2, width_dec // 4
    patch_piece = lax.dynamic_slice(
        low(patch_embed), (x * patch_rows, c * half_enc), (patch_rows, half_enc)
    )
    embed_piece = lax.dynamic_slice(
        low(decoder_embed), (0, (2 * x + c) * quarter_dec), (rows_enc, quarter_dec)
    )
    norm_share, norm_room = norm_params.shape[0], rows_enc * LANES
    norm_piece = jnp.pad(low(norm_params), (0, norm_room - norm_share)).reshape(rows_enc, LANES)
    enc_in_low = low(encoder_in).reshape(rows_enc, -1)
    enc_out_low = low(encoder_out).transpose(2, 0, 1).reshape(rows_enc, -1)
    dec_in_low = low(decoder_in).reshape(rows_dec, -1)
    dec_out_low = low(decoder_out).transpose(2, 0, 1).reshape(rows_dec, -1)
    head_low = low(pixel_head)
    first_blob = jnp.concatenate(
        [patch_piece, norm_piece, enc_in_low[:, : 3 * part_enc], enc_out_low[:, :part_enc]], 1
    )
    second_blob = jnp.concatenate(
        [enc_in_low[:, 3 * part_enc :], enc_out_low[:, part_enc:], embed_piece], 1
    )
    third_blob = jnp.concatenate([dec_in_low, dec_out_low, head_low], 1)
    widths = (
        (half_enc, LANES, 3 * part_enc, part_enc),
        (4 * part_enc, 4 * part_enc, quarter_dec),
        (3 * part_dec, 4 * part_dec, part_dec, 4 * part_dec, head_low.shape[1]),
    )

    buf_rows = data_size * -(-(slot_total * vis_count) // data_size)
    alive = row_dest[:, 0] < buf_rows
    use_own = pick(alive, x)
    half_step = lax.axis_size("z") // 2

    def shown_of(visible_row):
        return jnp.any(one_hot(visible_row, tokens), axis=0).astype(FLOAT_TYPE)

    start = after(x, first_blob)
    away = slot_total - 1 - start
    own_slot, away_slot = pick(pixels, start), pick(pixels, away)

    def seen_of(slot, rows):
        return low(product("vt,tp->vp", low(one_hot(pick(visible, slot), tokens)), rows))

    visible_row = jnp.where(use_own, pick(visible, start), shift(pick(visible, away), "z", half_step))
    seen_away = shift(halves_of(seen_of(away, away_slot), c), "z", half_step)

    (first_all, second_all, third_all), marks = spread_all(
        (first_blob, second_blob, third_blob), widths, own_slot
    )

    patch_all, norm_all, enc_qkv, enc_proj = first_all
    enc_up, enc_down, embed_all = second_all
    dec_qkv, dec_up, dec_proj, dec_down, head_all = third_all
    patch_all = patch_all.reshape(2, data_size, patch_rows, half_enc).transpose(1, 0, 2, 3)
    patch_all = patch_all.reshape(pix_width, half_enc)
    embed_other = swap(embed_all)
    embed_even = jnp.where(c == 0, embed_all, embed_other)
    embed_odd = jnp.where(c == 0, embed_other, embed_all)
    full_embed = jnp.concatenate([embed_even[0], embed_odd[0], embed_even[1], embed_odd[1]], 1)
    norm_full = norm_all[0].reshape(data_size, norm_room)[:, :norm_share].reshape(-1)
    norm_full = norm_full.astype(FLOAT_TYPE)
    enc_gains = norm_full[: 6 * width_enc].reshape(6, width_enc)
    dec_gains = norm_full[6 * width_enc : 6 * width_enc + 6 * width_dec].reshape(6, width_dec)
    mask_token = norm_full[6 * width_enc + 6 * width_dec : 6 * width_enc + 7 * width_dec]

    seen_rows = jnp.where(
        use_own, seen_of(after(start, marks[0]), own_slot), both(seen_away, "c", c, 1)
    )
    chosen = low(one_hot(visible_row, tokens))
    hidden_row = (1.0 - shown_of(visible_row))[:, None]

    visible_late = after(visible, marks[2])
    counted = jnp.stack([1.0 - shown_of(visible_late[slot]) for slot in range(slot_total)])
    counted = counted * alive.astype(FLOAT_TYPE)[:, None]
    valid_count = jnp.sum(counted[:, :, None] * valid.astype(FLOAT_TYPE))
    valid_count = valid_count * (pix_width // patch_positions)

    def pixels_of(slot, rows):
        place = after(c, marks[1])
        half = pix_width // 2
        cols = [halves_of(rows[:, first : first + half], place) for first in (0, half)]
        return jnp.concatenate(cols + [low(pick(valid, slot))], 1)

    own_pack, away_pack = pixels_of(start, own_slot), pixels_of(away, away_slot)
    pack_moved = shift(after(away_pack, marks[3]), "z", half_step)

    enc_stream = both(product("lp,pd->ld", seen_rows, patch_all), "c", c, 1)
    enc_stream = enc_stream + angles_of(visible_row, width_enc)
    partial, enc_triple, enc_mixture, enc_log = attn_fwd(
        enc_stream, enc_gains, enc_qkv, enc_proj, enc_heads
    )
    enc_middle, partial = mlp_fwd(enc_stream, partial, swap(partial), enc_gains, enc_up, enc_down)
    enc_last, enc_normed, dec_stream = between(
        enc_middle,
        partial,
        swap(partial),
        enc_gains,
        full_embed,
        chosen,
        hidden_row,
        mask_token[None],
        places_of(tokens, width_dec),
    )

    partial, dec_triple, dec_mixture, dec_log = attn_fwd(
        dec_stream, dec_gains, dec_qkv, dec_proj, dec_heads
    )
    dec_middle, partial = mlp_fwd(dec_stream, partial, swap(partial), dec_gains, dec_up, dec_down)

    pixel_pack = jnp.where(use_own, own_pack, after(pack_moved, dec_stream))
    pixel_cols = pixel_pack[:, : pix_width // 2].astype(FLOAT_TYPE)
    valid_cols = pixel_pack[:, pix_width // 2 :].astype(FLOAT_TYPE)
    half_mean = jnp.mean(pixel_cols, -1, keepdims=True)
    half_square = jnp.sum((pixel_cols - half_mean) ** 2, -1, keepdims=True)
    half_both = jnp.concatenate([half_mean, half_square], 1)
    other_both = swap(half_both)
    mean = 0.5 * (half_both[:, :1] + other_both[:, :1])
    gap = half_both[:, :1] - other_both[:, :1]
    variance = (half_both[:, 1:] + other_both[:, 1:]) / pix_width + 0.25 * gap * gap
    target = (pixel_cols - mean) * lax.rsqrt(variance + EPS_PIX)
    half_positions = patch_positions // 2
    front = jnp.where(c == 0, valid_cols[:, :half_positions], valid_cols[:, half_positions:])
    back = jnp.where(c == 0, valid_cols[:, half_positions:], valid_cols[:, :half_positions])
    part_mask = jnp.concatenate([front, back, front], 1) * hidden_row
    goal = jnp.stack([target[:, : pix_width // 4], target[:, pix_width // 4 :]])
    dec_last, dec_normed, pred_low, partial, loss_part = head_loss(
        dec_middle,
        partial,
        swap(partial),
        dec_gains,
        head_all,
        goal,
        part_mask,
    )

    stream_grad, grad_low, normed_low, hidden_low, upward_low, partial, dec_norms_three = mlp_back(
        (partial, swap(partial)), dec_last, dec_middle, dec_gains, dec_up, dec_down
    )
    dec_tail = Collect(
        share([(normed_low, upward_low), (grad_low, hidden_low), (dec_normed, pred_low)], rows_dec)
    )
    stream_grad, grad_low, normed_low, triple_grad, partial, dec_norms_two = attn_back(
        stream_grad,
        partial,
        swap(partial),
        dec_middle,
        dec_stream,
        (dec_triple, dec_log),
        dec_gains,
        dec_qkv,
        dec_proj,
        dec_heads,
    )
    normed_low = after(normed_low, *dec_tail.second(triple_grad))
    dec_attn = Collect(
        share([(normed_low, triple_grad), (grad_low, dec_mixture)], rows_dec), *dec_tail.late
    )
    embed_mine, normed_grad, mask_grad, dec_norms_one = decoder_end(
        stream_grad,
        partial,
        swap(partial),
        dec_stream,
        dec_gains,
        chosen,
        hidden_row,
        full_embed,
        c[None],
    )

    stream_grad, grad_low, normed_low, hidden_low, upward_low, partial, enc_norms_three = mlp_back(
        (after(normed_grad, *dec_attn.second(), *dec_tail.third()),), enc_last, enc_middle, enc_gains, enc_up, enc_down
    )
    enc_tail = Collect(
        share([(normed_low, upward_low), (grad_low, hidden_low), (enc_normed, embed_mine)], rows_enc),
        *dec_attn.late,
    )
    other_partial = after(swap(partial), *dec_attn.third(), *dec_tail.moved)
    stream_grad, grad_low, normed_low, triple_grad, partial, enc_norms_two = attn_back(
        stream_grad,
        partial,
        other_partial,
        enc_middle,
        enc_stream,
        (enc_triple, enc_log),
        enc_gains,
        enc_qkv,
        enc_proj,
        enc_heads,
    )
    other_partial = after(swap(partial), *enc_tail.second(), *dec_attn.moved)
    patch_right, enc_norms_one = encoder_end(
        stream_grad, partial, other_partial, enc_stream, enc_gains, c[None]
    )
    norm_pieces = jnp.concatenate(
        [
            grads.reshape(-1)
            for grads in (
                enc_norms_one,
                enc_norms_two,
                enc_norms_three,
                dec_norms_one,
                dec_norms_two,
                dec_norms_three,
                mask_grad,
            )
        ]
    )
    norm_total = norm_params.shape[0] * data_size
    norm_grad = jnp.concatenate(
        [norm_pieces, jnp.zeros((norm_total - norm_pieces.shape[0],), FLOAT_TYPE)]
    )
    norm_half = norm_share // 2
    norm_grads = low(norm_grad).reshape(data_size, 2, norm_half).transpose(1, 0, 2)
    norm_grads = jnp.pad(norm_grads, ((0, 0), (0, 0), (0, norm_room - norm_half)))
    enc_attn = Collect(
        share(
            [(normed_low, triple_grad), (grad_low, enc_mixture)],
            rows_enc,
            (seen_rows, patch_right),
            norm_grads.reshape(2, data_size, rows_enc, LANES),
        ),
        *enc_tail.late,
    )

    enc_tail_sent = enc_tail.third()
    enc_attn_sent = enc_attn.second(*enc_tail_sent)
    early_sums, embed_sum, square = sum_early(
        [group.terms(*enc_attn_sent) for group in (dec_attn, dec_tail, enc_tail)], quarter_dec
    )
    enc_attn.third(*enc_tail.moved)
    late_sum, exchanged, totals = sum_late(
        enc_attn.terms(), embed_sum, square, loss_part, valid_count, half_enc
    )
    exchanged = [
        exchanged,
        swap(exchanged, "c"),
        swap(exchanged, "x"),
        lax.ppermute(exchanged, ("x", "c"), ACROSS),
    ]
    norm_cuts = [
        part[:, half_enc : half_enc + LANES].reshape(-1)[:norm_half]
        for part in (exchanged[0], exchanged[2])
    ]
    norm_sum = jnp.where(x == 0, jnp.concatenate(norm_cuts), jnp.concatenate(norm_cuts[::-1]))
    totals = total_over(totals, ("c", "x", "y"))
    totals, *exchanged = lax.optimization_barrier((totals, *exchanged))
    totals = total_over(totals, ("z",))
    scalars, updated = adam_all(
        jnp.stack([x, c]), totals, masters, moments, seconds, [*early_sums, late_sum], exchanged, norm_sum
    )
    return (scalars[0, 0], scalars[0, 1], scalars[0, 2], *updated)


def solution(mesh):
    data, model = mesh.shape["dp"], mesh.shape["mp"]
    inner = Mesh(mesh.devices.reshape(data // 2, 2, model // 2, 2), ("z", "y", "x", "c"))
    data_axes, model_axes = ("z", "y"), ("x", "c")
    rows = P(data_axes)
    into = P(data_axes, None, model_axes)
    out_of = P(None, model_axes, data_axes)
    head = P(data_axes, model_axes)
    weights = (into, out_of, into, out_of, rows, rows, head, rows)
    triples = tuple(spec for spec in weights for _ in range(3))
    return jax.shard_map(
        on_device,
        mesh=inner,
        in_specs=(rows, rows, rows, rows) + triples,
        out_specs=(P(), P(), P()) + triples,
        check_vma=False,
    )
```

```python
import numpy as np

import jax
import jax.numpy as jnp
from jax import lax
from jax.experimental import pallas as pl
from jax.experimental.pallas import tpu as pltpu
from jax.sharding import Mesh
from jax.sharding import PartitionSpec as P

HEADS_ENC = 12
HEADS_DEC = 16
STEP = 10


EPS_NORM = 1e-05
EPS_PIX = 1e-06
CLIP = 0.0002
LR_MATRIX = 0.03
LR_NORM = 0.5
BETA_ONE = 0.9
BETA_TWO = 0.95
ADAM_EPS = 1e-10
DECAY = 0.05
FLOAT_TYPE = jnp.float32
NARROW_TYPE = jnp.bfloat16
SWAP = [(0, 1), (1, 0)]
ACROSS = [(0, 3), (1, 2), (2, 1), (3, 0)]
LANES = 128
NORM_ROWS = 64
VMEM_ROOM = 16 * 2**20
WIDE_ROOM = 56 * 2**20
SQRT_HALF = 0.5**0.5
DENSITY = (2.0 * np.pi) ** -0.5
DATA = ("z", "y")


def product(spec, left, right):
    return jnp.einsum(spec, left, right, preferred_element_type=FLOAT_TYPE)


def low(values):
    return values.astype(NARROW_TYPE)


def swap(values, axis="c"):
    return lax.ppermute(values, axis, SWAP)


def join(partial):
    return partial + swap(partial)


def join_low(partial):
    mine = low(partial)
    other = swap(mine)
    return mine.astype(FLOAT_TYPE) + other.astype(FLOAT_TYPE)


def shift(values, axis, step):
    size = lax.axis_size(axis)
    return lax.ppermute(values, axis, [(i, (i + step) % size) for i in range(size)])


def total_over(values, axes):
    for axis in axes:
        size = lax.axis_size(axis)
        if size & (size - 1):
            values = lax.psum(values, axis)
            continue
        step = 1
        while step < size:
            values = values + lax.ppermute(values, axis, [(i, i ^ step) for i in range(size)])
            step *= 2
    return values


def after(value, *others):
    return lax.optimization_barrier((value,) + others)[0]


def vmem_call(body, outs, *ins, scalars=(), scratch=(), flops=0, room=VMEM_ROOM):
    shapes = [jax.ShapeDtypeStruct(shape, kind) for shape, kind in outs]
    moved = sum(int(np.prod(a.shape)) * a.dtype.itemsize for a in [*ins, *shapes])
    return pl.pallas_call(
        body,
        out_shape=shapes,
        in_specs=[pl.BlockSpec(memory_space=pltpu.SMEM)] * len(scalars)
        + [pl.BlockSpec(memory_space=pltpu.VMEM)] * len(ins),
        out_specs=[pl.BlockSpec(memory_space=pltpu.VMEM)] * len(shapes),
        scratch_shapes=list(scratch),
        compiler_params=pltpu.CompilerParams(vmem_limit_bytes=room),
        cost_estimate=pl.CostEstimate(flops=flops, bytes_accessed=moved, transcendentals=0),
    )(*scalars, *ins)


class Spread:
    def __init__(self, blob, favour):
        self.favour = favour
        self.blob = blob
        self.near = self.sides(blob[None])

    def sides(self, part):
        return swap(part, "x"), swap(part, "y")

    def corners(self, from_x, from_y, favour):
        low_part, high_part = from_y[:favour], from_x[favour:]
        return [
            swap(part, axis) for part, axis in ((low_part, "x"), (high_part, "y")) if part.shape[0]
        ]

    def near_corners(self, *earlier):
        sides = lax.optimization_barrier((*self.near, *earlier))[:2]
        self.near = (*self.near, *self.corners(*sides, self.favour - 1))

    def along_z(self, *earlier):
        blob = after(self.blob, *earlier)
        self.moved = [shift(blob, "z", step) for step in (1, 2, 3)]

    def far_sides(self, *earlier):
        self.stack = after(jnp.stack(lax.optimization_barrier((*self.moved, *earlier))[:3]), *earlier)
        self.far = self.sides(self.stack)

    def far_corners(self, *earlier):
        sides = lax.optimization_barrier((*self.far, *earlier))[:2]
        self.far = (*self.far, *self.corners(*sides, self.favour))

    def whole(self, widths):
        rows = self.blob.shape[0]
        x, y, z = (lax.axis_index(axis) for axis in ("x", "y", "z"))
        starts = np.cumsum([0, *widths])

        parts = [(self.blob[None], 0, 0, (0,)), (self.stack, 0, 0, (1, 2, 3))]
        for sides, steps, favour in (
            (self.near, (0,), self.favour - 1),
            (self.far, (1, 2, 3), self.favour),
        ):
            parts += [(sides[0], 1, 0, steps), (sides[1], 0, 1, steps)]
            corners = [part for part in (steps[:favour], steps[favour:]) if part]
            parts += [(part, 1, 1, cut) for part, cut in zip(sides[2:], corners)]
        count = len(parts)

        def body(spot, *refs):
            here_x, here_y, here_z = spot[0], spot[1], spot[2]
            outs = refs[count:]
            for ref, (_, far_x, far_y, steps) in zip(refs, parts):
                at_x = 1 - here_x if far_x else here_x
                at_y = 1 - here_y if far_y else here_y
                for number, step in enumerate(steps):
                    level = lax.rem(here_z + (4 - step), 4)
                    for out, first, width in zip(outs, starts, widths):
                        out[at_x, level, at_y] = ref[number, :, first : first + width]

        outs = [((2, 4, 2, rows, width), self.blob.dtype) for width in widths]
        wholes = vmem_call(
            body, outs, *(part[0] for part in parts), scalars=(jnp.stack([x, y, z]),)
        )
        return [whole.reshape(2, 8 * rows, -1) for whole in wholes]


def pack_first(place, enc_in, enc_out, patch, norms):
    rows, width = enc_in.shape[1:]
    half_rows, half_columns = patch.shape[0] // 2, patch.shape[1] // 2
    columns = half_columns + LANES + 4 * width

    def body(place, enc_in, enc_out, patch, norms, blob):
        cuts = [
            jnp.where(place[1] == 0, patch[cut, :half_columns], patch[cut, half_columns:])
            for cut in (slice(0, half_rows), slice(half_rows, 2 * half_rows))
        ]
        blob[:, :half_columns] = low(jnp.where(place[0] == 0, *cuts))
        start = half_columns
        blob[:, start : start + LANES] = jnp.zeros((rows, LANES), NARROW_TYPE)
        blob[: norms.shape[0], start : start + LANES] = low(norms[...])
        start += LANES
        for block in range(3):
            blob[:, start : start + width] = low(enc_in[block])
            start += width
        blob[:, start:] = low(enc_out[0].T)

    return vmem_call(
        body, [((rows, columns), NARROW_TYPE)], enc_in, enc_out, patch, norms, scalars=(place,)
    )[0]


def pack_rest(place, enc_in, enc_out, dec_in, dec_out, embed, head):
    rows, width = enc_in.shape[1:]
    rows_dec, width_dec = dec_in.shape[1:]
    quarter = embed.shape[1] // 4

    def body(place, enc_in, enc_out, dec_in, dec_out, embed, head, second, third):
        for block in range(4):
            second[:, block * width : (block + 1) * width] = low(enc_in[3 + block])
            second[:, (4 + block) * width : (5 + block) * width] = low(enc_out[1 + block].T)
        cuts = [embed[:, n * quarter : (n + 1) * quarter] for n in range(4)]
        pairs = [jnp.where(place[1] == 0, cuts[n], cuts[n + 1]) for n in (0, 2)]
        second[:, 8 * width :] = low(jnp.where(place[0] == 0, *pairs))
        for block in range(7):
            third[:, block * width_dec : (block + 1) * width_dec] = low(dec_in[block])
        for block in range(5):
            third[:, (7 + block) * width_dec : (8 + block) * width_dec] = low(dec_out[block])
        third[:, 12 * width_dec :] = low(head[...])

    outs = [
        ((rows, 8 * width + quarter), NARROW_TYPE),
        ((rows_dec, 12 * width_dec + head.shape[1]), NARROW_TYPE),
    ]
    return vmem_call(body, outs, enc_in, enc_out, dec_in, dec_out, embed, head, scalars=(place,))


def spread_all(blobs, widths, arrived, last):
    sizes = tuple(lax.axis_size(axis) for axis in ("x", "z", "y"))
    if sizes != (2, 4, 2):
        wholes = [lax.all_gather(blob, ("x", "z", "y")) for blob in blobs]
        wholes = [whole.reshape(2, -1, whole.shape[-1]) for whole in wholes]
        pieces = [columns_of(whole, width) for whole, width in zip(wholes, widths)]
        marks = [wholes[0]] * 4
        return pieces, marks, last(marks)
    first = Spread(blobs[0], 2)
    first.along_z()
    second, third = (Spread(blob, favour) for blob, favour in ((blobs[1], 1), (blobs[2], 2)))
    for group in (first, second, third):
        group.near_corners()
    second.along_z(*first.moved)
    third.along_z(*first.moved)
    first.far_sides(*first.near, *second.near[:2], *third.near[:2], arrived)
    first.far_corners(*second.near[2:], *third.near[2:])
    second.far_sides(*first.far, *third.moved)
    second.far_corners()
    third.far_sides(*second.far)
    marks = (first.stack, first.far[0], first.far[2], third.moved[2])
    moved = last(marks)
    third.far_corners(moved)
    pieces = [group.whole(width) for group, width in zip((first, second, third), widths)]
    return pieces, marks, moved


def share(pieces, rows, patch=None, norms=None):
    x, y = lax.axis_index("x"), lax.axis_index("y")
    levels = lax.axis_size("z")
    half = levels // 2
    if (lax.axis_size("x"), levels, lax.axis_size("y")) != (2, 4, 2):
        cuts = []
        if patch is not None:
            cut = low(product("ld,lc->dc", *patch)).reshape(2 * levels, 2, rows, -1)
            cuts.append(cut.transpose(1, 0, 2, 3).reshape(2, 2 * levels * rows, -1))
        if norms is not None:
            norms = low(norms[:, :4]).reshape(2 * levels, 2, -1).transpose(1, 0, 2)
            norms = jnp.pad(norms, ((0, 0), (0, 0), (0, rows * LANES - norms.shape[2])))
            cuts.append(norms.reshape(2, 2 * levels * rows, LANES))
        cuts += [low(product("ld,xlc->xdc", left, right)) for left, right in pieces]
        return (jnp.concatenate(cuts, 2).reshape(4 * levels, rows, -1),)
    extra = []
    columns = 0
    if patch is not None:
        extra += [*patch]
        columns += patch[1].shape[1]
    if norms is not None:
        extra += [norms]
        columns += LANES
    first_column = columns
    for left, right in pieces:
        columns += right.shape[2]
    tallest = max([left.shape[1] for left, _ in pieces] + ([patch[0].shape[1]] if patch else []))
    widest = max([right.shape[2] for _, right in pieces] + ([patch[1].shape[1]] if patch else []))
    flops = sum(4 * left.shape[0] * left.shape[1] * right.shape[2] for left, right in pieces)

    def body(spot, *refs):
        ins, outs = refs[: len(extra) + 2 * len(pieces)], refs[len(extra) + 2 * len(pieces) : -1]
        total = refs[-1]
        cuts = ((outs[0], outs[1]), (outs[2], outs[3]), (outs[4], outs[5]), (outs[6], outs[7]))

        def put(far_x, far_y, level, window, value):
            target = cuts[2 * far_x + far_y][level // half]
            target[(level % half, *window)] = value

        used, column = 0, 0
        if patch is not None:
            left, right = ins[0], ins[1]
            width = right.shape[1]
            tall = left.shape[1]
            total[:tall, :width] = dot_tn(left[...], right[...])
            for far_x in (0, 1):
                for far_y in (0, 1):
                    at_x, at_y = spot[0] ^ far_x, spot[1] ^ far_y
                    for level in range(levels):
                        start = pl.multiple_of(((2 * level + at_y) * 2 + at_x) * rows, 8)
                        value = total[pl.ds(start, rows), :width].astype(NARROW_TYPE)
                        put(far_x, far_y, level, (slice(None), slice(0, width)), value)
            used, column = 2, width
        if norms is not None:
            source = ins[used]
            for far_x in (0, 1):
                for far_y in (0, 1):
                    at_x, at_y = spot[0] ^ far_x, spot[1] ^ far_y
                    for level in range(levels):
                        values = source[2 * (2 * level + at_y) + at_x]
                        values = jnp.concatenate(
                            [values, jnp.zeros((rows - values.shape[0], LANES), FLOAT_TYPE)]
                        )
                        window = (slice(None), slice(column, column + LANES))
                        put(far_x, far_y, level, window, low(values))
            used, column = used + 1, column + LANES
        for number, (_, right) in enumerate(pieces):
            left_ref, right_ref = ins[used + 2 * number], ins[used + 2 * number + 1]
            width = right.shape[2]
            tall = left_ref.shape[1]
            for far_x in (0, 1):
                at_x = spot[0] ^ far_x
                total[:tall, :width] = dot_tn(left_ref[...], right_ref[at_x])
                for far_y in (0, 1):
                    at_y = spot[1] ^ far_y
                    for level in range(levels):
                        start = pl.multiple_of((2 * level + at_y) * rows, 8)
                        value = total[pl.ds(start, rows), :width].astype(NARROW_TYPE)
                        put(far_x, far_y, level, (slice(None), slice(column, column + width)), value)
            column += width

    outs = [((half, rows, columns), NARROW_TYPE)] * 8
    flat = [array for piece in pieces for array in piece]
    return vmem_call(
        body,
        outs,
        *extra,
        *flat,
        scalars=(jnp.stack([x, y]),),
        scratch=[pltpu.VMEM((tallest, widest), FLOAT_TYPE)],
        flops=flops,
    )


def add(*terms):
    return sum(term.astype(FLOAT_TYPE) for term in terms)


class Collect:
    def __init__(self, cuts, *earlier):
        self.direct = None
        self.corner = self.early = self.late = self.moved = ()
        if len(cuts) == 1:
            self.direct = lax.psum_scatter(cuts[0], ("x", "z", "y"), scatter_dimension=0)
            return
        cuts = lax.optimization_barrier((*cuts, *earlier))
        self.own, self.by_y, self.by_x, corner = cuts[:2], cuts[2:4], cuts[4:6], cuts[6:8]
        self.corner = (swap(corner[0], "x"), swap(corner[1], "y"))
        self.early = (swap(self.by_x[0], "x"), swap(self.by_y[1], "y"))

    def second(self, *earlier):
        if self.direct is not None:
            return ()
        from_x, from_y = lax.optimization_barrier((*self.corner, *earlier))[:2]
        to_y, to_x = low(add(self.by_y[0], from_x)), low(add(self.by_x[1], from_y))
        self.late = (swap(to_y, "y"), swap(to_x, "x"))
        return to_y, to_x

    def third(self, *earlier):
        if self.direct is not None:
            return ()
        x_low, y_high, y_low, x_high = lax.optimization_barrier((*self.early, *self.late, *earlier))[:4]
        column = jnp.concatenate(
            [low(add(self.own[0], x_low, y_low)), low(add(self.own[1], x_high, y_high))]
        )
        z = lax.axis_index("z")
        parts = [lax.dynamic_index_in_dim(column, (z + n) % 4, 0, keepdims=False) for n in range(4)]
        self.mine = parts[0]
        self.moved = [shift(part, "z", step) for step, part in enumerate(parts[1:], 1)]
        return tuple(parts)

    def terms(self, *earlier):
        if self.direct is not None:
            return (self.direct,)
        return self.mine, *lax.optimization_barrier((*self.moved, *earlier))[:3]


def dot_nn(left, right):
    return jnp.dot(left, right, preferred_element_type=FLOAT_TYPE)


def dot_nt(left, right):
    return lax.dot_general(left, right, (((1,), (1,)), ((), ())), preferred_element_type=FLOAT_TYPE)


def dot_tn(left, right):
    return lax.dot_general(left, right, (((0,), (0,)), ((), ())), preferred_element_type=FLOAT_TYPE)


def angles_of(places, features):
    half_width = features // 2
    freqs = jnp.exp(-jnp.log(10000.0) * jnp.arange(half_width, dtype=FLOAT_TYPE) / half_width)
    angles = places.astype(FLOAT_TYPE)[:, None] * freqs[None, :]
    return jnp.concatenate([jnp.sin(angles), jnp.cos(angles)], axis=1)


def places_of(count, features):
    half_width = features // 2
    powers = np.arange(half_width, dtype=np.float32) / np.float32(half_width)
    freqs = np.exp(-np.log(np.float32(10000.0)) * powers)
    angles = np.arange(count, dtype=np.float32)[:, None] * freqs[None, :]
    return jnp.asarray(np.concatenate([np.sin(angles), np.cos(angles)], axis=1))


def norm_state(stream):
    centred = stream - jnp.mean(stream, -1, keepdims=True)
    inverse = lax.rsqrt(jnp.mean(centred * centred, -1, keepdims=True) + EPS_NORM)
    return centred * inverse, inverse


def norm_low(stream, gains, row):
    return low(norm_state(stream)[0] * gains[row : row + 1, :] + gains[row + 1 : row + 2, :])


def norm_back(upstream, stream, gains, row):
    scaled, inverse = norm_state(stream)
    weighted = upstream * gains[row : row + 1, :]
    input_grad = inverse * (
        weighted
        - jnp.mean(weighted, -1, keepdims=True)
        - scaled * jnp.mean(weighted * scaled, -1, keepdims=True)
    )
    sums = (jnp.sum(upstream * scaled, 0, keepdims=True), jnp.sum(upstream, 0, keepdims=True))
    return input_grad, sums


def head_masks(width, count):
    size = width // count
    lane = lax.broadcasted_iota(jnp.int32, (1, width), 1)
    return [
        jnp.where((lane >= head * size) & (lane < (head + 1) * size), 1.0, 0.0).astype(NARROW_TYPE)
        for head in range(count)
    ]


def attn_fwd(stream, gains, w_qkv, w_proj, head_count):
    length, features = stream.shape
    width = w_proj.shape[2]
    factor = (width // head_count) ** (-0.5)

    def body(stream, gains, w_qkv, w_proj, partial, triple, mixture, log_total):
        normed = norm_low(stream[...], gains, 0)
        masks = head_masks(width, head_count)
        output = None
        for part in (0, 1):
            projected = low(dot_nn(normed, w_qkv[part]))
            triple[part] = projected
            query, key, value = (projected[:, n * width : (n + 1) * width] for n in range(3))
            mixed = None
            for head, mask in enumerate(masks):
                scores = dot_nt(query * mask, key) * factor
                largest = jnp.max(scores, -1, keepdims=True)
                powers = jnp.exp(scores - largest)
                total = jnp.sum(powers, -1, keepdims=True)
                number = part * head_count + head
                log_total[:, number : number + 1] = largest + jnp.log(total)
                term = dot_nn(low(powers * (1.0 / total)), value * mask)
                mixed = term if mixed is None else mixed + term
            mixed = low(mixed)
            mixture[part] = mixed
            term = dot_nt(mixed, w_proj[part])
            output = term if output is None else output + term
        partial[...] = output

    outs = [
        ((length, features), FLOAT_TYPE),
        ((2, length, 3 * width), NARROW_TYPE),
        ((2, length, width), NARROW_TYPE),
        ((length, 2 * head_count), FLOAT_TYPE),
    ]
    flops = 16 * length * features * width + 8 * head_count * length * length * width
    return vmem_call(body, outs, stream, gains, w_qkv, w_proj, flops=flops)


def attn_back(stream_grad, own, other, middle, stream, kept, gains, w_qkv, w_proj, head_count):
    length, features = stream.shape
    width = w_proj.shape[2]
    factor = (width // head_count) ** (-0.5)
    triple, log_total = kept

    def body(
        stream_grad, own, other, middle, stream, triple, log_total, gains, w_qkv, w_proj,
        new_grad, grad_low, normed, triple_grad, partial, norm_grads,
    ):
        upstream = own[...].astype(FLOAT_TYPE) + other[...].astype(FLOAT_TYPE)
        input_grad, sums = norm_back(upstream, middle[...], gains, 2)
        norm_grads[0:1, :], norm_grads[1:2, :] = sums
        upstream = stream_grad[...] + input_grad
        new_grad[...] = upstream
        upstream = low(upstream)
        grad_low[...] = upstream
        normed[...] = norm_low(stream[...], gains, 0)
        masks = head_masks(width, head_count)
        output = None
        for part in (0, 1):
            projected = triple[part]
            query, key, value = (projected[:, n * width : (n + 1) * width] for n in range(3))
            mix_grad = low(dot_nn(upstream, w_proj[part]))
            query_grad = key_grad = value_grad = None
            for head, mask in enumerate(masks):
                query_part, mix_part = query * mask, mix_grad * mask
                number = part * head_count + head
                scores = dot_nt(query_part, key) * factor
                attend = jnp.exp(scores - log_total[:, number : number + 1])
                attend_grad = dot_nt(mix_part, value)
                inner = jnp.sum(attend * attend_grad, -1, keepdims=True)
                score_grad = low(attend * (attend_grad - inner))
                terms = (
                    dot_nn(score_grad, key * mask),
                    dot_tn(score_grad, query_part),
                    dot_tn(low(attend), mix_part),
                )
                if head == 0:
                    query_grad, key_grad, value_grad = terms
                else:
                    query_grad, key_grad, value_grad = (
                        query_grad + terms[0],
                        key_grad + terms[1],
                        value_grad + terms[2],
                    )
            grads = (low(query_grad * factor), low(key_grad * factor), low(value_grad))
            for number, grad in enumerate(grads):
                triple_grad[part, :, number * width : (number + 1) * width] = grad
            term = dot_nt(triple_grad[part], w_qkv[part])
            output = term if output is None else output + term
        partial[...] = low(output)

    outs = [
        ((length, features), FLOAT_TYPE),
        ((length, features), NARROW_TYPE),
        ((length, features), NARROW_TYPE),
        ((2, length, 3 * width), NARROW_TYPE),
        ((length, features), NARROW_TYPE),
        ((2, features), FLOAT_TYPE),
    ]
    flops = 16 * length * features * width + 20 * head_count * length * length * width
    return vmem_call(
        body, outs, stream_grad, own, other, middle, stream, triple, log_total, gains, w_qkv, w_proj,
        flops=flops,
    )


def mlp_fwd(stream, own, other, gains, w_up, w_down):
    length, features = stream.shape
    width = w_up.shape[2]

    def body(stream, own, other, gains, w_up, w_down, middle, partial):
        values = stream[...] + (own[...] + other[...])
        middle[...] = values
        normed = norm_low(values, gains, 2)
        output = None
        for part in (0, 1):
            upward = dot_nn(normed, w_up[part])
            hidden = low(0.5 * upward * (1.0 + lax.erf(upward * SQRT_HALF)))
            term = dot_nt(hidden, w_down[part])
            output = term if output is None else output + term
        partial[...] = output

    outs = [((length, features), FLOAT_TYPE)] * 2
    flops = 8 * length * features * width
    return vmem_call(body, outs, stream, own, other, gains, w_up, w_down, flops=flops)


def mlp_back(upstream, last, middle, gains, w_up, w_down):
    length, features = last.shape
    width = w_up.shape[2]
    count = len(upstream)

    def body(*refs):
        last, middle, gains, w_up, w_down = refs[count : count + 5]
        new_grad, grad_low, normed_low, hidden_low, upward_low, partial, norm_grads = refs[count + 5 :]
        arrived = add(*(ref[...] for ref in refs[:count]))
        input_grad, sums = norm_back(arrived, last[...], gains, 4)
        norm_grads[0:1, :], norm_grads[1:2, :] = sums
        new_grad[...] = input_grad
        grad = low(input_grad)
        grad_low[...] = grad
        normed = norm_low(middle[...], gains, 2)
        normed_low[...] = normed
        output = None
        for part in (0, 1):
            upward = dot_nn(normed, w_up[part])
            below = 0.5 * (1.0 + lax.erf(upward * SQRT_HALF))
            hidden_low[part] = low(upward * below)
            slope = below + upward * (jnp.exp(-0.5 * upward * upward) * DENSITY)
            upward_grad = low(dot_nn(grad, w_down[part]) * slope)
            upward_low[part] = upward_grad
            term = dot_nt(upward_grad, w_up[part])
            output = term if output is None else output + term
        partial[...] = low(output)

    outs = [
        ((length, features), FLOAT_TYPE),
        ((length, features), NARROW_TYPE),
        ((length, features), NARROW_TYPE),
        ((2, length, width), NARROW_TYPE),
        ((2, length, width), NARROW_TYPE),
        ((length, features), NARROW_TYPE),
        ((2, features), FLOAT_TYPE),
    ]
    flops = 12 * length * features * width
    return vmem_call(body, outs, *upstream, last, middle, gains, w_up, w_down, flops=flops)


def between(middle, own, other, gains, embed, chosen, hidden_row, mask_token, places):
    length, features = middle.shape
    tokens, width = places.shape

    def body(middle, own, other, gains, embed, chosen, hidden_row, mask_token, places, last, normed_low, stream):
        values = middle[...] + (own[...] + other[...])
        last[...] = values
        normed = norm_low(values, gains, 4)
        normed_low[...] = normed
        embedded = dot_nn(normed, embed[...])
        high = low(embedded)
        rest = low(embedded - high.astype(FLOAT_TYPE))
        placed = dot_tn(chosen[...], high) + dot_tn(chosen[...], rest)
        stream[...] = placed + hidden_row[...] * mask_token[...] + places[...]

    outs = [
        ((length, features), FLOAT_TYPE),
        ((length, features), NARROW_TYPE),
        ((tokens, width), FLOAT_TYPE),
    ]
    return vmem_call(body, outs, middle, own, other, gains, embed, chosen, hidden_row, mask_token, places)


def head_loss(middle, own, other, gains, w_head, goal, mask):
    length, features = middle.shape
    width = w_head.shape[2]

    def body(middle, own, other, gains, w_head, goal, mask, last, normed_low, pred_low, partial, loss):
        values = middle[...] + (own[...] + other[...])
        last[...] = values
        normed = norm_low(values, gains, 4)
        normed_low[...] = normed
        weights = mask[...]
        output, lost = None, None
        for part in (0, 1):
            errors = dot_nn(normed, w_head[part]) - goal[part]
            weighted = weights * errors
            square = jnp.sum(weighted * errors, 0, keepdims=True)
            pred_grad = low(weighted * 2.0)
            pred_low[part] = pred_grad
            term = dot_nt(pred_grad, w_head[part])
            output = term if output is None else output + term
            lost = square if lost is None else lost + square
        partial[...] = low(output)
        loss[...] = lost

    outs = [
        ((length, features), FLOAT_TYPE),
        ((length, features), NARROW_TYPE),
        ((2, length, width), NARROW_TYPE),
        ((length, features), NARROW_TYPE),
        ((1, width), FLOAT_TYPE),
    ]
    flops = 8 * length * features * width
    return vmem_call(body, outs, middle, own, other, gains, w_head, goal, mask, flops=flops)


def decoder_end(stream_grad, own, other, stream, gains, chosen, hidden_row, embed, place):
    length, features = stream.shape
    vis_count = chosen.shape[0]
    quarter = features // 4

    def body(
        place, stream_grad, own, other, stream, gains, chosen, hidden_row, embed,
        embed_mine, normed_grad, mask_grad, norm_grads,
    ):
        upstream = own[...].astype(FLOAT_TYPE) + other[...].astype(FLOAT_TYPE)
        input_grad, sums = norm_back(upstream, stream[...], gains, 0)
        norm_grads[0:1, :], norm_grads[1:2, :] = sums
        grad = stream_grad[...] + input_grad
        mask_grad[...] = jnp.sum(grad * hidden_row[...], 0, keepdims=True)
        embedded = low(dot_nn(chosen[...], low(grad)))
        for part in (0, 1):
            start = 2 * part * quarter
            cuts = [embedded[:, start + n * quarter : start + (n + 1) * quarter] for n in (0, 1)]
            embed_mine[part] = jnp.where(place[0] == 0, *cuts)
        normed_grad[...] = dot_nt(embedded, embed[...])

    outs = [
        ((2, vis_count, quarter), NARROW_TYPE),
        ((vis_count, embed.shape[0]), FLOAT_TYPE),
        ((1, features), FLOAT_TYPE),
        ((2, features), FLOAT_TYPE),
    ]
    return vmem_call(
        body, outs, stream_grad, own, other, stream, gains, chosen, hidden_row, embed, scalars=(place,)
    )


def encoder_end(stream_grad, own, other, stream, gains, place, norms, mask_grad):
    length, features = stream.shape
    half = features // 2
    width_dec = mask_grad.shape[1]
    rows = (6 * features + 7 * width_dec) // LANES

    def body(place, stream_grad, own, other, stream, gains, *refs):
        norms, (mask, grad_mine, gathered) = refs[:5], refs[5:]
        upstream = own[...].astype(FLOAT_TYPE) + other[...].astype(FLOAT_TYPE)
        input_grad, sums = norm_back(upstream, stream[...], gains, 0)
        grad = low(stream_grad[...] + input_grad)
        grad_mine[...] = jnp.where(place[0] == 0, grad[:, :half], grad[:, half:])
        gathered[...] = jnp.zeros_like(gathered)
        row = 0
        for source in (*sums, *(ref[n : n + 1, :] for ref in norms for n in (0, 1)), mask[...]):
            for start in range(0, source.shape[1], LANES):
                gathered[row // 4, row % 4 : row % 4 + 1, :] = source[:, start : start + LANES]
                row += 1

    groups = max(rows, NORM_ROWS) // 4
    outs = [((length, half), NARROW_TYPE), ((groups, 8, LANES), FLOAT_TYPE)]
    return vmem_call(
        body, outs, stream_grad, own, other, stream, gains, *norms, mask_grad, scalars=(place,)
    )


def adam_update(weight, moment, second, gradient, step_rate, decay_rate):
    moment = BETA_ONE * moment + (1.0 - BETA_ONE) * gradient
    second = BETA_TWO * second + (1.0 - BETA_TWO) * gradient * gradient
    fixed_one = moment / (1.0 - BETA_ONE**STEP)
    fixed_two = second / (1.0 - BETA_TWO**STEP)
    weight = weight - step_rate * (
        fixed_one / (jnp.sqrt(fixed_two) + ADAM_EPS) + decay_rate * weight
    )
    return [weight, moment, second]


def lane_is(number):
    return lax.broadcasted_iota(jnp.int32, (1, LANES), 1) == number


def sum_early(groups, embed_width):
    count = sum(len(group) for group in groups)

    def body(*refs):
        outs = refs[count:]
        used, square = 0, 0.0
        for number, group in enumerate(groups):
            total = add(*(ref[...] for ref in refs[used : used + len(group)]))
            used += len(group)
            if number == len(groups) - 1:
                embed = low(total[:, total.shape[1] - embed_width :])
                outs[number + 1][...] = embed
                total = total[:, : total.shape[1] - embed_width]
                embed = embed.astype(FLOAT_TYPE)
                square = square + jnp.sum(embed * embed, keepdims=True)
            outs[number][...] = total
            square = square + jnp.sum(total * total, keepdims=True)
        outs[-1][...] = square

    outs = []
    for number, group in enumerate(groups):
        rows, columns = group[0].shape
        outs.append(((rows, columns - embed_width * (number == len(groups) - 1)), FLOAT_TYPE))
    outs += [((groups[-1][0].shape[0], embed_width), NARROW_TYPE), ((1, 1), FLOAT_TYPE)]
    flat = [term for group in groups for term in group]
    *sums, embed, square = vmem_call(body, outs, *flat)
    return sums, embed, square


def sum_late(terms, first_terms, embed, square, loss_part, valid_count, patch_width):
    count, both_count = len(terms), len(terms) + len(first_terms)
    rows, columns = terms[0].shape
    split = first_terms[0].shape[1]

    def body(*refs):
        embed, square, loss, valid, rest, exchanged, totals = refs[both_count:]
        kept = add(*(ref[...] for ref in refs[:count]))
        rest[...] = kept
        sent = low(add(*(ref[...] for ref in refs[count:both_count])))
        exchanged[:, :split] = sent
        exchanged[:, split:] = embed[...]
        sent = sent.astype(FLOAT_TYPE)
        squares = sent * sent
        gathered = (
            square[...]
            + jnp.sum(kept * kept, keepdims=True)
            + jnp.sum(squares[:, :patch_width], keepdims=True)
            + 0.5 * jnp.sum(squares[:, patch_width:], keepdims=True)
        )
        loss = jnp.sum(loss[...], keepdims=True)
        totals[...] = jnp.where(
            lane_is(0), loss, jnp.where(lane_is(1), 0.25 * valid[...], jnp.where(lane_is(2), gathered, 0.0))
        )

    outs = [
        ((rows, columns), FLOAT_TYPE),
        ((rows, split + embed.shape[1]), NARROW_TYPE),
        ((1, LANES), FLOAT_TYPE),
    ]
    return vmem_call(
        body, outs, *terms, *first_terms, embed, square, loss_part, valid_count.reshape(1, 1)
    )


def adam_all(place, totals, masters, moments, seconds, sums, exchanged, norm_sum):
    orders = ((1, 0, 2), None, (1, 0, 2), (0, 2, 1))
    shapes = [array.shape for array in masters]

    def view(array, number):
        if number < 4:
            return array if orders[number] is None else array.transpose(orders[number])
        return array.reshape(-1, LANES) if array.ndim == 1 else array

    def unview(array, number):
        if number < 4 and orders[number] is not None:
            return array.transpose(np.argsort(orders[number]))
        return array.reshape(shapes[number])

    triples = [
        [view(array, number) for array in (masters[number], moments[number], seconds[number])]
        for number in range(8)
    ]
    flat = [array for triple in triples for array in triple]
    part_enc, part_dec = shapes[0][2], shapes[2][2]
    patch_rows, patch_width = shapes[4][0] // 2, shapes[4][1] // 2
    embed_width = shapes[5][1] // 4

    def body(place, totals, *refs):
        arrays, refs = refs[:24], refs[24:]
        (dec_attn, dec_tail, enc_tail, enc_attn, *parts, norm_sum), refs = refs[:9], refs[9:]
        scalars, outs = refs[0], refs[1:]
        loss, count, square = (
            jnp.sum(jnp.where(lane_is(n), totals[...], 0.0), keepdims=True) for n in range(3)
        )
        grad_norm = jnp.sqrt(square) / count
        factor = CLIP / jnp.maximum(grad_norm, CLIP) / count
        scalars[...] = jnp.where(lane_is(0), loss, jnp.where(lane_is(1), count, grad_norm))

        def update(number, where, grad):
            step_rate = LR_NORM if number == 7 else LR_MATRIX
            decay_rate = 0.0 if number == 7 else DECAY
            values = (ref[where] for ref in arrays[3 * number : 3 * number + 3])
            results = adam_update(*values, grad * factor, step_rate, decay_rate)
            for ref, result in zip(outs[3 * number : 3 * number + 3], results):
                ref[where] = result

        def piece(at_x, at_c, columns):
            far_x, far_c = place[0] != at_x, place[1] != at_c
            cuts = [part[:, columns] for part in parts]
            rows = [jnp.where(far_c, cuts[n + 1], cuts[n]) for n in (0, 2)]
            return jnp.where(far_x, rows[1], rows[0]).astype(FLOAT_TYPE)

        for number, attn, tail, width in (
            (0, enc_attn, enc_tail, part_enc),
            (2, dec_attn, dec_tail, part_dec),
        ):
            for block in range(7):
                source, first = (attn, block) if block < 3 else (tail, block - 3)
                update(number, block, source[:, first * width : (first + 1) * width])
            for block in range(5):
                source, first = (attn, 3) if block == 0 else (tail, 3 + block)
                grad = source[:, first * width : (first + 1) * width]
                update(number + 1, block, grad.T if number == 0 else grad)
        for at_x in (0, 1):
            for at_c in (0, 1):
                grad = piece(at_x, at_c, slice(0, patch_width))
                rows = slice(at_x * patch_rows, (at_x + 1) * patch_rows)
                columns = slice(at_c * patch_width, (at_c + 1) * patch_width)
                update(4, (rows, columns), grad)
                first = patch_width + LANES
                grad = piece(at_x, at_c, slice(first, first + embed_width))
                number = 2 * at_x + at_c
                update(5, (slice(None), slice(number * embed_width, (number + 1) * embed_width)), grad)
        update(6, Ellipsis, dec_tail[:, 8 * part_dec :])
        update(7, Ellipsis, norm_sum[...].astype(FLOAT_TYPE))

    outs = [((1, LANES), FLOAT_TYPE)] + [(array.shape, FLOAT_TYPE) for array in flat]
    scalars, *results = vmem_call(
        body, outs, totals, *flat, *sums, *exchanged, view(norm_sum, 7), scalars=(place,), room=WIDE_ROOM
    )
    return scalars, [unview(result, index // 3) for index, result in enumerate(results)]


def both(piece, axis, place, dimension):
    other = swap(piece, axis)
    return jnp.where(
        place == 0,
        jnp.concatenate([piece, other], dimension),
        jnp.concatenate([other, piece], dimension),
    )


def halves_of(array, place):
    half = array.shape[1] // 2
    return jnp.where(place == 0, array[:, :half], array[:, half:])


def one_hot(visible_row, tokens):
    return visible_row[:, None] == jnp.arange(tokens)[None, :]


def pick(array, index, axis=0):
    return lax.dynamic_index_in_dim(array, index, axis, keepdims=False)


def columns_of(blob, widths):
    pieces, start = [], 0
    for width in widths:
        pieces.append(blob[..., start : start + width])
        start += width
    return pieces


def on_device(
    pixels,
    visible,
    valid,
    row_dest,
    encoder_in,
    encoder_in_moment,
    encoder_in_second,
    encoder_out,
    encoder_out_moment,
    encoder_out_second,
    decoder_in,
    decoder_in_moment,
    decoder_in_second,
    decoder_out,
    decoder_out_moment,
    decoder_out_second,
    patch_embed,
    patch_embed_moment,
    patch_embed_second,
    decoder_embed,
    decoder_embed_moment,
    decoder_embed_second,
    pixel_head,
    pixel_head_moment,
    pixel_head_second,
    norm_params,
    norm_params_moment,
    norm_params_second,
):
    masters = [
        encoder_in,
        encoder_out,
        decoder_in,
        decoder_out,
        patch_embed,
        decoder_embed,
        pixel_head,
        norm_params,
    ]
    moments = [
        encoder_in_moment,
        encoder_out_moment,
        decoder_in_moment,
        decoder_out_moment,
        patch_embed_moment,
        decoder_embed_moment,
        pixel_head_moment,
        norm_params_moment,
    ]
    seconds = [
        encoder_in_second,
        encoder_out_second,
        decoder_in_second,
        decoder_out_second,
        patch_embed_second,
        decoder_embed_second,
        pixel_head_second,
        norm_params_second,
    ]
    x, c = lax.axis_index("x"), lax.axis_index("c")
    data_size = lax.axis_size("z") * lax.axis_size("y")
    slot_total, tokens, pix_width = pixels.shape
    vis_count = visible.shape[1]
    patch_positions = valid.shape[2]
    rows_enc, _, part_enc = encoder_in.shape
    rows_dec, _, part_dec = decoder_in.shape
    width_enc, width_dec = patch_embed.shape[1], decoder_embed.shape[1]
    enc_heads = HEADS_ENC // 4
    dec_heads = HEADS_DEC // 4

    patch_rows = patch_embed.shape[0] // 2
    half_enc, quarter_dec = width_enc // 2, width_dec // 4
    norm_share, norm_room = norm_params.shape[0], rows_enc * LANES
    place = jnp.stack([x, c])
    enc_in_blocks = encoder_in.transpose(1, 0, 2)
    first_blob = pack_first(place, enc_in_blocks, encoder_out, patch_embed, norm_params.reshape(-1, LANES))
    second_blob, third_blob = pack_rest(
        after(place, first_blob),
        enc_in_blocks,
        encoder_out,
        decoder_in.transpose(1, 0, 2),
        decoder_out.transpose(0, 2, 1),
        decoder_embed,
        pixel_head,
    )
    widths = (
        (half_enc, LANES, 3 * part_enc, part_enc),
        (4 * part_enc, 4 * part_enc, quarter_dec),
        (3 * part_dec, 4 * part_dec, part_dec, 4 * part_dec, pixel_head.shape[1]),
    )

    buf_rows = data_size * -(-(slot_total * vis_count) // data_size)
    alive = row_dest[:, 0] < buf_rows
    use_own = pick(alive, x)
    half_step = lax.axis_size("z") // 2

    def shown_of(visible_row):
        return jnp.any(one_hot(visible_row, tokens), axis=0).astype(FLOAT_TYPE)

    away = slot_total - 1 - x
    visible_moved = shift(pick(visible, away), "z", half_step)
    visible_row = jnp.where(use_own, pick(visible, x), visible_moved)

    def packs_of(marks):
        start = after(x, marks[0])
        own_slot, away_slot = pick(pixels, start), pick(pixels, slot_total - 1 - start)

        def seen_of(slot, rows):
            return low(product("vt,tp->vp", low(one_hot(pick(visible, slot), tokens)), rows))

        seen_away = shift(halves_of(seen_of(away, away_slot), c), "z", half_step)
        seen_away = both(seen_away, "c", c, 1)
        seen.append(jnp.where(use_own, seen_of(x, own_slot), seen_away))

        def pixels_of(slot, rows):
            place = after(c, marks[1])
            half = pix_width // 2
            cols = [halves_of(rows[:, first : first + half], place) for first in (0, half)]
            return jnp.concatenate(cols + [low(pick(valid, slot))], 1)

        seen.append(pixels_of(start, own_slot))
        away_pack = pixels_of(slot_total - 1 - start, away_slot)
        return shift(after(away_pack, marks[3]), "z", half_step)

    seen = []
    (first_all, second_all, third_all), marks, pack_moved = spread_all(
        (first_blob, second_blob, third_blob), widths, visible_moved, packs_of
    )
    seen_rows, own_pack = seen

    patch_all, norm_all, enc_qkv, enc_proj = first_all
    enc_up, enc_down, embed_all = second_all
    dec_qkv, dec_up, dec_proj, dec_down, head_all = third_all
    patch_all = patch_all.reshape(2, data_size, patch_rows, half_enc).transpose(1, 0, 2, 3)
    patch_all = patch_all.reshape(pix_width, half_enc)
    embed_other = swap(embed_all)
    embed_even = jnp.where(c == 0, embed_all, embed_other)
    embed_odd = jnp.where(c == 0, embed_other, embed_all)
    full_embed = jnp.concatenate([embed_even[0], embed_odd[0], embed_even[1], embed_odd[1]], 1)
    norm_full = norm_all[0].reshape(data_size, norm_room)[:, :norm_share].reshape(-1)
    norm_full = norm_full.astype(FLOAT_TYPE)
    enc_gains = norm_full[: 6 * width_enc].reshape(6, width_enc)
    dec_gains = norm_full[6 * width_enc : 6 * width_enc + 6 * width_dec].reshape(6, width_dec)
    mask_token = norm_full[6 * width_enc + 6 * width_dec : 6 * width_enc + 7 * width_dec]

    chosen = low(one_hot(visible_row, tokens))
    hidden_row = (1.0 - shown_of(visible_row))[:, None]

    visible_late = after(visible, marks[2])
    counted = jnp.stack([1.0 - shown_of(visible_late[slot]) for slot in range(slot_total)])
    counted = counted * alive.astype(FLOAT_TYPE)[:, None]
    valid_count = jnp.sum(counted[:, :, None] * valid.astype(FLOAT_TYPE))
    valid_count = valid_count * (pix_width // patch_positions)

    enc_stream = both(product("lp,pd->ld", seen_rows, patch_all), "c", c, 1)
    enc_stream = enc_stream + angles_of(visible_row, width_enc)
    partial, enc_triple, enc_mixture, enc_log = attn_fwd(
        enc_stream, enc_gains, enc_qkv, enc_proj, enc_heads
    )
    enc_middle, partial = mlp_fwd(enc_stream, partial, swap(partial), enc_gains, enc_up, enc_down)
    enc_last, enc_normed, dec_stream = between(
        enc_middle,
        partial,
        swap(partial),
        enc_gains,
        full_embed,
        chosen,
        hidden_row,
        mask_token[None],
        places_of(tokens, width_dec),
    )

    partial, dec_triple, dec_mixture, dec_log = attn_fwd(
        dec_stream, dec_gains, dec_qkv, dec_proj, dec_heads
    )
    dec_middle, partial = mlp_fwd(dec_stream, partial, swap(partial), dec_gains, dec_up, dec_down)

    pixel_pack = jnp.where(use_own, own_pack, after(pack_moved, dec_triple))
    pixel_cols = pixel_pack[:, : pix_width // 2].astype(FLOAT_TYPE)
    valid_cols = pixel_pack[:, pix_width // 2 :].astype(FLOAT_TYPE)
    half_mean = jnp.mean(pixel_cols, -1, keepdims=True)
    half_square = jnp.sum((pixel_cols - half_mean) ** 2, -1, keepdims=True)
    half_both = jnp.concatenate([half_mean, half_square], 1)
    other_both = swap(half_both)
    mean = 0.5 * (half_both[:, :1] + other_both[:, :1])
    gap = half_both[:, :1] - other_both[:, :1]
    variance = (half_both[:, 1:] + other_both[:, 1:]) / pix_width + 0.25 * gap * gap
    target = (pixel_cols - mean) * lax.rsqrt(variance + EPS_PIX)
    half_positions = patch_positions // 2
    front = jnp.where(c == 0, valid_cols[:, :half_positions], valid_cols[:, half_positions:])
    back = jnp.where(c == 0, valid_cols[:, half_positions:], valid_cols[:, :half_positions])
    part_mask = jnp.concatenate([front, back, front], 1) * hidden_row
    goal = jnp.stack([target[:, : pix_width // 4], target[:, pix_width // 4 :]])
    dec_last, dec_normed, pred_low, partial, loss_part = head_loss(
        dec_middle,
        partial,
        swap(partial),
        dec_gains,
        head_all,
        goal,
        part_mask,
    )

    stream_grad, grad_low, normed_low, hidden_low, upward_low, partial, dec_norms_three = mlp_back(
        (partial, swap(partial)), dec_last, dec_middle, dec_gains, dec_up, dec_down
    )
    dec_tail = Collect(
        share([(normed_low, upward_low), (grad_low, hidden_low), (dec_normed, pred_low)], rows_dec)
    )
    stream_grad, grad_low, normed_low, triple_grad, partial, dec_norms_two = attn_back(
        stream_grad,
        partial,
        swap(partial),
        dec_middle,
        dec_stream,
        (dec_triple, dec_log),
        dec_gains,
        dec_qkv,
        dec_proj,
        dec_heads,
    )
    normed_low = after(normed_low, *dec_tail.second(triple_grad))
    dec_attn = Collect(
        share([(normed_low, triple_grad), (grad_low, dec_mixture)], rows_dec), *dec_tail.late
    )
    embed_mine, normed_grad, mask_grad, dec_norms_one = decoder_end(
        stream_grad,
        partial,
        swap(partial),
        dec_stream,
        dec_gains,
        chosen,
        hidden_row,
        full_embed,
        c[None],
    )

    stream_grad, grad_low, normed_low, hidden_low, upward_low, partial, enc_norms_three = mlp_back(
        (after(normed_grad, *dec_attn.second(), *dec_tail.third()),), enc_last, enc_middle, enc_gains, enc_up, enc_down
    )
    enc_tail = Collect(
        share([(normed_low, upward_low), (grad_low, hidden_low), (enc_normed, embed_mine)], rows_enc),
        *dec_attn.late,
    )
    other_partial = after(swap(partial), *dec_attn.third(), *dec_tail.moved)
    stream_grad, grad_low, normed_low, triple_grad, partial, enc_norms_two = attn_back(
        stream_grad,
        partial,
        other_partial,
        enc_middle,
        enc_stream,
        (enc_triple, enc_log),
        enc_gains,
        enc_qkv,
        enc_proj,
        enc_heads,
    )
    enc_tail_late = enc_tail.second(triple_grad)
    normed_low = after(normed_low, *enc_tail_late)
    enc_attn = Collect(
        share([(normed_low, triple_grad), (grad_low, enc_mixture)], rows_enc), *enc_tail.late
    )
    other_partial = after(swap(partial), *enc_tail_late, *dec_attn.moved)
    patch_right, norm_grads = encoder_end(
        stream_grad,
        partial,
        other_partial,
        enc_stream,
        enc_gains,
        c[None],
        (enc_norms_two, enc_norms_three, dec_norms_one, dec_norms_two, dec_norms_three),
        mask_grad,
    )
    norm_half = norm_share // 2
    enc_attn_late = enc_attn.second()
    enc_first = Collect(
        share(
            [],
            rows_enc,
            (seen_rows, patch_right),
            norm_grads,
        ),
        *enc_attn_late,
    )

    enc_tail_sent = enc_tail.third()
    enc_attn_sent = enc_attn.third(*enc_tail_sent)
    enc_first_late = enc_first.second(*enc_tail.moved)
    early_sums, embed_sum, square = sum_early(
        [
            group.terms(*enc_attn_sent, *enc_first_late)
            for group in (dec_attn, dec_tail, enc_tail)
        ],
        quarter_dec,
    )
    enc_first_sent = enc_first.third()
    late_sum, exchanged, totals = sum_late(
        enc_attn.terms(*enc_first_sent), enc_first.terms(), embed_sum, square, loss_part, valid_count, half_enc
    )
    exchanged = [
        exchanged,
        swap(exchanged, "c"),
        swap(exchanged, "x"),
        lax.ppermute(exchanged, ("x", "c"), ACROSS),
    ]
    norm_cuts = [
        part[:, half_enc : half_enc + LANES].reshape(-1)[:norm_half]
        for part in (exchanged[0], exchanged[2])
    ]
    norm_sum = jnp.where(x == 0, jnp.concatenate(norm_cuts), jnp.concatenate(norm_cuts[::-1]))
    totals = total_over(totals, ("c", "x", "y"))
    totals, *exchanged = lax.optimization_barrier((totals, *exchanged))
    totals = total_over(totals, ("z",))
    scalars, updated = adam_all(
        jnp.stack([x, c]), totals, masters, moments, seconds, [*early_sums, late_sum], exchanged, norm_sum
    )
    return (scalars[0, 0], scalars[0, 1], scalars[0, 2], *updated)


def solution(mesh):
    data, model = mesh.shape["dp"], mesh.shape["mp"]
    inner = Mesh(mesh.devices.reshape(data // 2, 2, model // 2, 2), ("z", "y", "x", "c"))
    data_axes, model_axes = ("z", "y"), ("x", "c")
    rows = P(data_axes)
    into = P(data_axes, None, model_axes)
    out_of = P(None, model_axes, data_axes)
    head = P(data_axes, model_axes)
    weights = (into, out_of, into, out_of, rows, rows, head, rows)
    triples = tuple(spec for spec in weights for _ in range(3))
    return jax.shard_map(
        on_device,
        mesh=inner,
        in_specs=(rows, rows, rows, rows) + triples,
        out_specs=(P(), P(), P()) + triples,
        check_vma=False,
    )
```

```python
import numpy as np

import jax
import jax.numpy as jnp
from jax import lax
from jax.experimental import pallas as pl
from jax.experimental.pallas import tpu as pltpu
from jax.sharding import Mesh
from jax.sharding import PartitionSpec as P

HEADS_ENC = 12
HEADS_DEC = 16
STEP = 10


EPS_NORM = 1e-05
EPS_PIX = 1e-06
CLIP = 0.0002
LR_MATRIX = 0.03
LR_NORM = 0.5
BETA_ONE = 0.9
BETA_TWO = 0.95
ADAM_EPS = 1e-10
DECAY = 0.05
FLOAT_TYPE = jnp.float32
NARROW_TYPE = jnp.bfloat16
SWAP = [(0, 1), (1, 0)]
ACROSS = [(0, 3), (1, 2), (2, 1), (3, 0)]
LANES = 128
NORM_ROWS = 64
VMEM_ROOM = 16 * 2**20
WIDE_ROOM = 56 * 2**20
SQRT_HALF = 0.5**0.5
DENSITY = (2.0 * np.pi) ** -0.5
DATA = ("z", "y")


def product(spec, left, right):
    return jnp.einsum(spec, left, right, preferred_element_type=FLOAT_TYPE)


def low(values):
    return values.astype(NARROW_TYPE)


def swap(values, axis="c"):
    return lax.ppermute(values, axis, SWAP)


def join(partial):
    return partial + swap(partial)


def join_low(partial):
    mine = low(partial)
    other = swap(mine)
    return mine.astype(FLOAT_TYPE) + other.astype(FLOAT_TYPE)


def shift(values, axis, step):
    size = lax.axis_size(axis)
    return lax.ppermute(values, axis, [(i, (i + step) % size) for i in range(size)])


def total_over(values, axes):
    for axis in axes:
        size = lax.axis_size(axis)
        if size & (size - 1):
            values = lax.psum(values, axis)
            continue
        step = 1
        while step < size:
            values = values + lax.ppermute(values, axis, [(i, i ^ step) for i in range(size)])
            step *= 2
    return values


def after(value, *others):
    return lax.optimization_barrier((value,) + others)[0]


def vmem_call(body, outs, *ins, scalars=(), scratch=(), flops=0, room=VMEM_ROOM):
    shapes = [jax.ShapeDtypeStruct(shape, kind) for shape, kind in outs]
    moved = sum(int(np.prod(a.shape)) * a.dtype.itemsize for a in [*ins, *shapes])
    return pl.pallas_call(
        body,
        out_shape=shapes,
        in_specs=[pl.BlockSpec(memory_space=pltpu.SMEM)] * len(scalars)
        + [pl.BlockSpec(memory_space=pltpu.VMEM)] * len(ins),
        out_specs=[pl.BlockSpec(memory_space=pltpu.VMEM)] * len(shapes),
        scratch_shapes=list(scratch),
        compiler_params=pltpu.CompilerParams(vmem_limit_bytes=room),
        cost_estimate=pl.CostEstimate(flops=flops, bytes_accessed=moved, transcendentals=0),
    )(*scalars, *ins)


class Spread:
    def __init__(self, blob, favour):
        self.favour = favour
        self.blob = blob
        self.near = self.sides(blob[None])

    def sides(self, part):
        return swap(part, "x"), swap(part, "y")

    def corners(self, from_x, from_y, favour):
        low_part, high_part = from_y[:favour], from_x[favour:]
        return [
            swap(part, axis) for part, axis in ((low_part, "x"), (high_part, "y")) if part.shape[0]
        ]

    def near_corners(self, *earlier):
        sides = lax.optimization_barrier((*self.near, *earlier))[:2]
        self.near = (*self.near, *self.corners(*sides, self.favour - 1))

    def along_z(self, *earlier):
        blob = after(self.blob, *earlier)
        self.moved = [shift(blob, "z", step) for step in (1, 2, 3)]

    def far_sides(self, *earlier):
        self.stack = after(jnp.stack(lax.optimization_barrier((*self.moved, *earlier))[:3]), *earlier)
        self.far = self.sides(self.stack)

    def far_corners(self, *earlier):
        sides = lax.optimization_barrier((*self.far, *earlier))[:2]
        self.far = (*self.far, *self.corners(*sides, self.favour))

    def whole(self, widths):
        rows = self.blob.shape[0]
        x, y, z = (lax.axis_index(axis) for axis in ("x", "y", "z"))
        starts = np.cumsum([0, *widths])

        parts = [(self.blob[None], 0, 0, (0,)), (self.stack, 0, 0, (1, 2, 3))]
        for sides, steps, favour in (
            (self.near, (0,), self.favour - 1),
            (self.far, (1, 2, 3), self.favour),
        ):
            parts += [(sides[0], 1, 0, steps), (sides[1], 0, 1, steps)]
            corners = [part for part in (steps[:favour], steps[favour:]) if part]
            parts += [(part, 1, 1, cut) for part, cut in zip(sides[2:], corners)]
        count = len(parts)

        def body(spot, *refs):
            here_x, here_y, here_z = spot[0], spot[1], spot[2]
            outs = refs[count:]
            for ref, (_, far_x, far_y, steps) in zip(refs, parts):
                at_x = 1 - here_x if far_x else here_x
                at_y = 1 - here_y if far_y else here_y
                for number, step in enumerate(steps):
                    level = lax.rem(here_z + (4 - step), 4)
                    for out, first, width in zip(outs, starts, widths):
                        out[at_x, level, at_y] = ref[number, :, first : first + width]

        outs = [((2, 4, 2, rows, width), self.blob.dtype) for width in widths]
        wholes = vmem_call(
            body, outs, *(part[0] for part in parts), scalars=(jnp.stack([x, y, z]),)
        )
        return [whole.reshape(2, 8 * rows, -1) for whole in wholes]


def pack_first(place, enc_in, enc_out, patch, norms):
    rows, width = enc_in.shape[1:]
    half_rows, half_columns = patch.shape[0] // 2, patch.shape[1] // 2
    columns = half_columns + LANES + 4 * width

    def body(place, enc_in, enc_out, patch, norms, blob):
        cuts = [
            jnp.where(place[1] == 0, patch[cut, :half_columns], patch[cut, half_columns:])
            for cut in (slice(0, half_rows), slice(half_rows, 2 * half_rows))
        ]
        blob[:, :half_columns] = low(jnp.where(place[0] == 0, *cuts))
        start = half_columns
        blob[:, start : start + LANES] = jnp.zeros((rows, LANES), NARROW_TYPE)
        blob[: norms.shape[0], start : start + LANES] = low(norms[...])
        start += LANES
        for block in range(3):
            blob[:, start : start + width] = low(enc_in[block])
            start += width
        blob[:, start:] = low(enc_out[0].T)

    return vmem_call(
        body, [((rows, columns), NARROW_TYPE)], enc_in, enc_out, patch, norms, scalars=(place,)
    )[0]


def pack_rest(place, enc_in, enc_out, dec_in, dec_out, embed, head):
    rows, width = enc_in.shape[1:]
    rows_dec, width_dec = dec_in.shape[1:]
    quarter = embed.shape[1] // 4

    def body(place, enc_in, enc_out, dec_in, dec_out, embed, head, second, third):
        for block in range(4):
            second[:, block * width : (block + 1) * width] = low(enc_in[3 + block])
            second[:, (4 + block) * width : (5 + block) * width] = low(enc_out[1 + block].T)
        cuts = [embed[:, n * quarter : (n + 1) * quarter] for n in range(4)]
        pairs = [jnp.where(place[1] == 0, cuts[n], cuts[n + 1]) for n in (0, 2)]
        second[:, 8 * width :] = low(jnp.where(place[0] == 0, *pairs))
        for block in range(7):
            third[:, block * width_dec : (block + 1) * width_dec] = low(dec_in[block])
        for block in range(5):
            third[:, (7 + block) * width_dec : (8 + block) * width_dec] = low(dec_out[block])
        third[:, 12 * width_dec :] = low(head[...])

    outs = [
        ((rows, 8 * width + quarter), NARROW_TYPE),
        ((rows_dec, 12 * width_dec + head.shape[1]), NARROW_TYPE),
    ]
    return vmem_call(body, outs, enc_in, enc_out, dec_in, dec_out, embed, head, scalars=(place,))


def spread_all(blobs, widths, arrived, early, last):
    sizes = tuple(lax.axis_size(axis) for axis in ("x", "z", "y"))
    if sizes != (2, 4, 2):
        wholes = [lax.all_gather(blob, ("x", "z", "y")) for blob in blobs]
        wholes = [whole.reshape(2, -1, whole.shape[-1]) for whole in wholes]
        pieces = [columns_of(whole, width) for whole, width in zip(wholes, widths)]
        marks = [wholes[0]] * 4
        early(wholes[0])
        return pieces, marks, last(marks)
    first = Spread(blobs[0], 2)
    first.along_z()
    second, third = (Spread(blob, favour) for blob, favour in ((blobs[1], 1), (blobs[2], 2)))
    for group in (first, second, third):
        group.near_corners()
    second.along_z(*first.moved)
    third.along_z(*first.moved)
    first.far_sides(*first.near, *second.near, *third.near, arrived)
    picked = early(first.stack)
    first.far_corners(picked)
    second.far_sides(*first.far, *third.moved)
    second.far_corners()
    third.far_sides(*second.far)
    marks = (first.stack, first.far[0], first.far[2], third.moved[2])
    moved = last(marks)
    third.far_corners()
    pieces = [group.whole(width) for group, width in zip((first, second, third), widths)]
    return pieces, marks, moved


def share(pieces, rows, patch=None, norms=None):
    x, y = lax.axis_index("x"), lax.axis_index("y")
    levels = lax.axis_size("z")
    half = levels // 2
    if (lax.axis_size("x"), levels, lax.axis_size("y")) != (2, 4, 2):
        cuts = []
        if patch is not None:
            cut = low(product("ld,lc->dc", *patch)).reshape(2 * levels, 2, rows, -1)
            cuts.append(cut.transpose(1, 0, 2, 3).reshape(2, 2 * levels * rows, -1))
        if norms is not None:
            norms = low(norms[:, :4]).reshape(2 * levels, 2, -1).transpose(1, 0, 2)
            norms = jnp.pad(norms, ((0, 0), (0, 0), (0, rows * LANES - norms.shape[2])))
            cuts.append(norms.reshape(2, 2 * levels * rows, LANES))
        cuts += [low(product("ld,xlc->xdc", left, right)) for left, right in pieces]
        return (jnp.concatenate(cuts, 2).reshape(4 * levels, rows, -1),)
    extra = []
    columns = 0
    if patch is not None:
        extra += [*patch]
        columns += patch[1].shape[1]
    if norms is not None:
        extra += [norms]
        columns += LANES
    first_column = columns
    for left, right in pieces:
        columns += right.shape[2]
    tallest = max([left.shape[1] for left, _ in pieces] + ([patch[0].shape[1]] if patch else []))
    widest = max([right.shape[2] for _, right in pieces] + ([patch[1].shape[1]] if patch else []))
    flops = sum(4 * left.shape[0] * left.shape[1] * right.shape[2] for left, right in pieces)

    def body(spot, *refs):
        ins, outs = refs[: len(extra) + 2 * len(pieces)], refs[len(extra) + 2 * len(pieces) : -1]
        total = refs[-1]
        cuts = ((outs[0], outs[1]), (outs[2], outs[3]), (outs[4], outs[5]), (outs[6], outs[7]))

        def put(far_x, far_y, level, window, value):
            target = cuts[2 * far_x + far_y][level // half]
            target[(level % half, *window)] = value

        used, column = 0, 0
        if patch is not None:
            left, right = ins[0], ins[1]
            width = right.shape[1]
            tall = left.shape[1]
            total[:tall, :width] = dot_tn(left[...], right[...])
            for far_x in (0, 1):
                for far_y in (0, 1):
                    at_x, at_y = spot[0] ^ far_x, spot[1] ^ far_y
                    for level in range(levels):
                        start = pl.multiple_of(((2 * level + at_y) * 2 + at_x) * rows, 8)
                        value = total[pl.ds(start, rows), :width].astype(NARROW_TYPE)
                        put(far_x, far_y, level, (slice(None), slice(0, width)), value)
            used, column = 2, width
        if norms is not None:
            source = ins[used]
            for far_x in (0, 1):
                for far_y in (0, 1):
                    at_x, at_y = spot[0] ^ far_x, spot[1] ^ far_y
                    for level in range(levels):
                        values = source[2 * (2 * level + at_y) + at_x]
                        values = jnp.concatenate(
                            [values, jnp.zeros((rows - values.shape[0], LANES), FLOAT_TYPE)]
                        )
                        window = (slice(None), slice(column, column + LANES))
                        put(far_x, far_y, level, window, low(values))
            used, column = used + 1, column + LANES
        for number, (_, right) in enumerate(pieces):
            left_ref, right_ref = ins[used + 2 * number], ins[used + 2 * number + 1]
            width = right.shape[2]
            tall = left_ref.shape[1]
            for far_x in (0, 1):
                at_x = spot[0] ^ far_x
                total[:tall, :width] = dot_tn(left_ref[...], right_ref[at_x])
                for far_y in (0, 1):
                    at_y = spot[1] ^ far_y
                    for level in range(levels):
                        start = pl.multiple_of((2 * level + at_y) * rows, 8)
                        value = total[pl.ds(start, rows), :width].astype(NARROW_TYPE)
                        put(far_x, far_y, level, (slice(None), slice(column, column + width)), value)
            column += width

    outs = [((half, rows, columns), NARROW_TYPE)] * 8
    flat = [array for piece in pieces for array in piece]
    return vmem_call(
        body,
        outs,
        *extra,
        *flat,
        scalars=(jnp.stack([x, y]),),
        scratch=[pltpu.VMEM((tallest, widest), FLOAT_TYPE)],
        flops=flops,
    )


def add(*terms):
    return sum(term.astype(FLOAT_TYPE) for term in terms)


class Collect:
    def __init__(self, cuts, *earlier):
        self.direct = None
        self.corner = self.early = self.late = self.moved = ()
        if len(cuts) == 1:
            self.direct = lax.psum_scatter(cuts[0], ("x", "z", "y"), scatter_dimension=0)
            return
        cuts = lax.optimization_barrier((*cuts, *earlier))
        self.own, self.by_y, self.by_x, corner = cuts[:2], cuts[2:4], cuts[4:6], cuts[6:8]
        self.corner = (swap(corner[0], "x"), swap(corner[1], "y"))
        self.early = (swap(self.by_x[0], "x"), swap(self.by_y[1], "y"))

    def second(self, *earlier):
        if self.direct is not None:
            return ()
        from_x, from_y = lax.optimization_barrier((*self.corner, *earlier))[:2]
        to_y, to_x = low(add(self.by_y[0], from_x)), low(add(self.by_x[1], from_y))
        self.late = (swap(to_y, "y"), swap(to_x, "x"))
        return to_y, to_x

    def third(self, *earlier):
        if self.direct is not None:
            return ()
        x_low, y_high, y_low, x_high = lax.optimization_barrier((*self.early, *self.late, *earlier))[:4]
        column = jnp.concatenate(
            [low(add(self.own[0], x_low, y_low)), low(add(self.own[1], x_high, y_high))]
        )
        z = lax.axis_index("z")
        parts = [lax.dynamic_index_in_dim(column, (z + n) % 4, 0, keepdims=False) for n in range(4)]
        self.mine = parts[0]
        self.moved = [shift(part, "z", step) for step, part in enumerate(parts[1:], 1)]
        return tuple(parts)

    def terms(self, *earlier):
        if self.direct is not None:
            return (self.direct,)
        return self.mine, *lax.optimization_barrier((*self.moved, *earlier))[:3]


def dot_nn(left, right):
    return jnp.dot(left, right, preferred_element_type=FLOAT_TYPE)


def dot_nt(left, right):
    return lax.dot_general(left, right, (((1,), (1,)), ((), ())), preferred_element_type=FLOAT_TYPE)


def dot_tn(left, right):
    return lax.dot_general(left, right, (((0,), (0,)), ((), ())), preferred_element_type=FLOAT_TYPE)


def angles_of(places, features):
    half_width = features // 2
    freqs = jnp.exp(-jnp.log(10000.0) * jnp.arange(half_width, dtype=FLOAT_TYPE) / half_width)
    angles = places.astype(FLOAT_TYPE)[:, None] * freqs[None, :]
    return jnp.concatenate([jnp.sin(angles), jnp.cos(angles)], axis=1)


def places_of(count, features):
    half_width = features // 2
    powers = np.arange(half_width, dtype=np.float32) / np.float32(half_width)
    freqs = np.exp(-np.log(np.float32(10000.0)) * powers)
    angles = np.arange(count, dtype=np.float32)[:, None] * freqs[None, :]
    return jnp.asarray(np.concatenate([np.sin(angles), np.cos(angles)], axis=1))


def norm_state(stream):
    centred = stream - jnp.mean(stream, -1, keepdims=True)
    inverse = lax.rsqrt(jnp.mean(centred * centred, -1, keepdims=True) + EPS_NORM)
    return centred * inverse, inverse


def norm_low(stream, gains, row):
    return low(norm_state(stream)[0] * gains[row : row + 1, :] + gains[row + 1 : row + 2, :])


def norm_back(upstream, stream, gains, row):
    scaled, inverse = norm_state(stream)
    weighted = upstream * gains[row : row + 1, :]
    input_grad = inverse * (
        weighted
        - jnp.mean(weighted, -1, keepdims=True)
        - scaled * jnp.mean(weighted * scaled, -1, keepdims=True)
    )
    sums = (jnp.sum(upstream * scaled, 0, keepdims=True), jnp.sum(upstream, 0, keepdims=True))
    return input_grad, sums


def head_masks(width, count):
    size = width // count
    lane = lax.broadcasted_iota(jnp.int32, (1, width), 1)
    return [
        jnp.where((lane >= head * size) & (lane < (head + 1) * size), 1.0, 0.0).astype(NARROW_TYPE)
        for head in range(count)
    ]


def attn_fwd(stream, gains, w_qkv, w_proj, head_count):
    length, features = stream.shape
    width = w_proj.shape[2]
    factor = (width // head_count) ** (-0.5)

    def body(stream, gains, w_qkv, w_proj, partial, triple, mixture, log_total):
        normed = norm_low(stream[...], gains, 0)
        masks = head_masks(width, head_count)
        output = None
        for part in (0, 1):
            projected = low(dot_nn(normed, w_qkv[part]))
            triple[part] = projected
            query, key, value = (projected[:, n * width : (n + 1) * width] for n in range(3))
            mixed = None
            for head, mask in enumerate(masks):
                scores = dot_nt(query * mask, key) * factor
                largest = jnp.max(scores, -1, keepdims=True)
                powers = jnp.exp(scores - largest)
                total = jnp.sum(powers, -1, keepdims=True)
                number = part * head_count + head
                log_total[:, number : number + 1] = largest + jnp.log(total)
                term = dot_nn(low(powers * (1.0 / total)), value * mask)
                mixed = term if mixed is None else mixed + term
            mixed = low(mixed)
            mixture[part] = mixed
            term = dot_nt(mixed, w_proj[part])
            output = term if output is None else output + term
        partial[...] = output

    outs = [
        ((length, features), FLOAT_TYPE),
        ((2, length, 3 * width), NARROW_TYPE),
        ((2, length, width), NARROW_TYPE),
        ((length, 2 * head_count), FLOAT_TYPE),
    ]
    flops = 16 * length * features * width + 8 * head_count * length * length * width
    return vmem_call(body, outs, stream, gains, w_qkv, w_proj, flops=flops)


def attn_back(stream_grad, own, other, middle, stream, kept, gains, w_qkv, w_proj, head_count):
    length, features = stream.shape
    width = w_proj.shape[2]
    factor = (width // head_count) ** (-0.5)
    triple, log_total = kept

    def body(
        stream_grad, own, other, middle, stream, triple, log_total, gains, w_qkv, w_proj,
        new_grad, grad_low, normed, triple_grad, partial, norm_grads,
    ):
        upstream = own[...].astype(FLOAT_TYPE) + other[...].astype(FLOAT_TYPE)
        input_grad, sums = norm_back(upstream, middle[...], gains, 2)
        norm_grads[0:1, :], norm_grads[1:2, :] = sums
        upstream = stream_grad[...] + input_grad
        new_grad[...] = upstream
        upstream = low(upstream)
        grad_low[...] = upstream
        normed[...] = norm_low(stream[...], gains, 0)
        masks = head_masks(width, head_count)
        output = None
        for part in (0, 1):
            projected = triple[part]
            query, key, value = (projected[:, n * width : (n + 1) * width] for n in range(3))
            mix_grad = low(dot_nn(upstream, w_proj[part]))
            query_grad = key_grad = value_grad = None
            for head, mask in enumerate(masks):
                query_part, mix_part = query * mask, mix_grad * mask
                number = part * head_count + head
                scores = dot_nt(query_part, key) * factor
                attend = jnp.exp(scores - log_total[:, number : number + 1])
                attend_grad = dot_nt(mix_part, value)
                inner = jnp.sum(attend * attend_grad, -1, keepdims=True)
                score_grad = low(attend * (attend_grad - inner))
                terms = (
                    dot_nn(score_grad, key * mask),
                    dot_tn(score_grad, query_part),
                    dot_tn(low(attend), mix_part),
                )
                if head == 0:
                    query_grad, key_grad, value_grad = terms
                else:
                    query_grad, key_grad, value_grad = (
                        query_grad + terms[0],
                        key_grad + terms[1],
                        value_grad + terms[2],
                    )
            grads = (low(query_grad * factor), low(key_grad * factor), low(value_grad))
            for number, grad in enumerate(grads):
                triple_grad[part, :, number * width : (number + 1) * width] = grad
            term = dot_nt(triple_grad[part], w_qkv[part])
            output = term if output is None else output + term
        partial[...] = low(output)

    outs = [
        ((length, features), FLOAT_TYPE),
        ((length, features), NARROW_TYPE),
        ((length, features), NARROW_TYPE),
        ((2, length, 3 * width), NARROW_TYPE),
        ((length, features), NARROW_TYPE),
        ((2, features), FLOAT_TYPE),
    ]
    flops = 16 * length * features * width + 20 * head_count * length * length * width
    return vmem_call(
        body, outs, stream_grad, own, other, middle, stream, triple, log_total, gains, w_qkv, w_proj,
        flops=flops,
    )


def mlp_fwd(stream, own, other, gains, w_up, w_down):
    length, features = stream.shape
    width = w_up.shape[2]

    def body(stream, own, other, gains, w_up, w_down, middle, partial):
        values = stream[...] + (own[...] + other[...])
        middle[...] = values
        normed = norm_low(values, gains, 2)
        output = None
        for part in (0, 1):
            upward = dot_nn(normed, w_up[part])
            hidden = low(0.5 * upward * (1.0 + lax.erf(upward * SQRT_HALF)))
            term = dot_nt(hidden, w_down[part])
            output = term if output is None else output + term
        partial[...] = output

    outs = [((length, features), FLOAT_TYPE)] * 2
    flops = 8 * length * features * width
    return vmem_call(body, outs, stream, own, other, gains, w_up, w_down, flops=flops)


def mlp_back(upstream, last, middle, gains, w_up, w_down):
    length, features = last.shape
    width = w_up.shape[2]
    count = len(upstream)

    def body(*refs):
        last, middle, gains, w_up, w_down = refs[count : count + 5]
        new_grad, grad_low, normed_low, hidden_low, upward_low, partial, norm_grads = refs[count + 5 :]
        arrived = add(*(ref[...] for ref in refs[:count]))
        input_grad, sums = norm_back(arrived, last[...], gains, 4)
        norm_grads[0:1, :], norm_grads[1:2, :] = sums
        new_grad[...] = input_grad
        grad = low(input_grad)
        grad_low[...] = grad
        normed = norm_low(middle[...], gains, 2)
        normed_low[...] = normed
        output = None
        for part in (0, 1):
            upward = dot_nn(normed, w_up[part])
            below = 0.5 * (1.0 + lax.erf(upward * SQRT_HALF))
            hidden_low[part] = low(upward * below)
            slope = below + upward * (jnp.exp(-0.5 * upward * upward) * DENSITY)
            upward_grad = low(dot_nn(grad, w_down[part]) * slope)
            upward_low[part] = upward_grad
            term = dot_nt(upward_grad, w_up[part])
            output = term if output is None else output + term
        partial[...] = low(output)

    outs = [
        ((length, features), FLOAT_TYPE),
        ((length, features), NARROW_TYPE),
        ((length, features), NARROW_TYPE),
        ((2, length, width), NARROW_TYPE),
        ((2, length, width), NARROW_TYPE),
        ((length, features), NARROW_TYPE),
        ((2, features), FLOAT_TYPE),
    ]
    flops = 12 * length * features * width
    return vmem_call(body, outs, *upstream, last, middle, gains, w_up, w_down, flops=flops)


def between(middle, own, other, gains, embed, chosen, hidden_row, mask_token, places):
    length, features = middle.shape
    tokens, width = places.shape

    def body(middle, own, other, gains, embed, chosen, hidden_row, mask_token, places, last, normed_low, stream):
        values = middle[...] + (own[...] + other[...])
        last[...] = values
        normed = norm_low(values, gains, 4)
        normed_low[...] = normed
        embedded = dot_nn(normed, embed[...])
        high = low(embedded)
        rest = low(embedded - high.astype(FLOAT_TYPE))
        placed = dot_tn(chosen[...], high) + dot_tn(chosen[...], rest)
        stream[...] = placed + hidden_row[...] * mask_token[...] + places[...]

    outs = [
        ((length, features), FLOAT_TYPE),
        ((length, features), NARROW_TYPE),
        ((tokens, width), FLOAT_TYPE),
    ]
    return vmem_call(body, outs, middle, own, other, gains, embed, chosen, hidden_row, mask_token, places)


def head_loss(middle, own, other, gains, w_head, goal, mask):
    length, features = middle.shape
    width = w_head.shape[2]

    def body(middle, own, other, gains, w_head, goal, mask, last, normed_low, pred_low, partial, loss):
        values = middle[...] + (own[...] + other[...])
        last[...] = values
        normed = norm_low(values, gains, 4)
        normed_low[...] = normed
        weights = mask[...]
        output, lost = None, None
        for part in (0, 1):
            errors = dot_nn(normed, w_head[part]) - goal[part]
            weighted = weights * errors
            square = jnp.sum(weighted * errors, 0, keepdims=True)
            pred_grad = low(weighted * 2.0)
            pred_low[part] = pred_grad
            term = dot_nt(pred_grad, w_head[part])
            output = term if output is None else output + term
            lost = square if lost is None else lost + square
        partial[...] = low(output)
        loss[...] = lost

    outs = [
        ((length, features), FLOAT_TYPE),
        ((length, features), NARROW_TYPE),
        ((2, length, width), NARROW_TYPE),
        ((length, features), NARROW_TYPE),
        ((1, width), FLOAT_TYPE),
    ]
    flops = 8 * length * features * width
    return vmem_call(body, outs, middle, own, other, gains, w_head, goal, mask, flops=flops)


def decoder_end(stream_grad, own, other, stream, gains, chosen, hidden_row, embed, place):
    length, features = stream.shape
    vis_count = chosen.shape[0]
    quarter = features // 4

    def body(
        place, stream_grad, own, other, stream, gains, chosen, hidden_row, embed,
        embed_mine, normed_grad, mask_grad, norm_grads,
    ):
        upstream = own[...].astype(FLOAT_TYPE) + other[...].astype(FLOAT_TYPE)
        input_grad, sums = norm_back(upstream, stream[...], gains, 0)
        norm_grads[0:1, :], norm_grads[1:2, :] = sums
        grad = stream_grad[...] + input_grad
        mask_grad[...] = jnp.sum(grad * hidden_row[...], 0, keepdims=True)
        embedded = low(dot_nn(chosen[...], low(grad)))
        for part in (0, 1):
            start = 2 * part * quarter
            cuts = [embedded[:, start + n * quarter : start + (n + 1) * quarter] for n in (0, 1)]
            embed_mine[part] = jnp.where(place[0] == 0, *cuts)
        normed_grad[...] = dot_nt(embedded, embed[...])

    outs = [
        ((2, vis_count, quarter), NARROW_TYPE),
        ((vis_count, embed.shape[0]), FLOAT_TYPE),
        ((1, features), FLOAT_TYPE),
        ((2, features), FLOAT_TYPE),
    ]
    return vmem_call(
        body, outs, stream_grad, own, other, stream, gains, chosen, hidden_row, embed, scalars=(place,)
    )


def encoder_end(stream_grad, own, other, stream, gains, place, norms, mask_grad):
    length, features = stream.shape
    half = features // 2
    width_dec = mask_grad.shape[1]
    rows = (6 * features + 7 * width_dec) // LANES

    def body(place, stream_grad, own, other, stream, gains, *refs):
        norms, (mask, grad_mine, gathered) = refs[:5], refs[5:]
        upstream = own[...].astype(FLOAT_TYPE) + other[...].astype(FLOAT_TYPE)
        input_grad, sums = norm_back(upstream, stream[...], gains, 0)
        grad = low(stream_grad[...] + input_grad)
        grad_mine[...] = jnp.where(place[0] == 0, grad[:, :half], grad[:, half:])
        gathered[...] = jnp.zeros_like(gathered)
        row = 0
        for source in (*sums, *(ref[n : n + 1, :] for ref in norms for n in (0, 1)), mask[...]):
            for start in range(0, source.shape[1], LANES):
                gathered[row // 4, row % 4 : row % 4 + 1, :] = source[:, start : start + LANES]
                row += 1

    groups = max(rows, NORM_ROWS) // 4
    outs = [((length, half), NARROW_TYPE), ((groups, 8, LANES), FLOAT_TYPE)]
    return vmem_call(
        body, outs, stream_grad, own, other, stream, gains, *norms, mask_grad, scalars=(place,)
    )


def adam_update(weight, moment, second, gradient, step_rate, decay_rate):
    moment = BETA_ONE * moment + (1.0 - BETA_ONE) * gradient
    second = BETA_TWO * second + (1.0 - BETA_TWO) * gradient * gradient
    fixed_one = moment / (1.0 - BETA_ONE**STEP)
    fixed_two = second / (1.0 - BETA_TWO**STEP)
    weight = weight - step_rate * (
        fixed_one / (jnp.sqrt(fixed_two) + ADAM_EPS) + decay_rate * weight
    )
    return [weight, moment, second]


def lane_is(number):
    return lax.broadcasted_iota(jnp.int32, (1, LANES), 1) == number


def sum_early(groups, embed_width):
    count = sum(len(group) for group in groups)

    def body(*refs):
        outs = refs[count:]
        used, square = 0, 0.0
        for number, group in enumerate(groups):
            total = add(*(ref[...] for ref in refs[used : used + len(group)]))
            used += len(group)
            if number == len(groups) - 1:
                embed = low(total[:, total.shape[1] - embed_width :])
                outs[number + 1][...] = embed
                total = total[:, : total.shape[1] - embed_width]
                embed = embed.astype(FLOAT_TYPE)
                square = square + jnp.sum(embed * embed, keepdims=True)
            outs[number][...] = total
            square = square + jnp.sum(total * total, keepdims=True)
        outs[-1][...] = square

    outs = []
    for number, group in enumerate(groups):
        rows, columns = group[0].shape
        outs.append(((rows, columns - embed_width * (number == len(groups) - 1)), FLOAT_TYPE))
    outs += [((groups[-1][0].shape[0], embed_width), NARROW_TYPE), ((1, 1), FLOAT_TYPE)]
    flat = [term for group in groups for term in group]
    *sums, embed, square = vmem_call(body, outs, *flat)
    return sums, embed, square


def sum_late(terms, first_terms, embed, square, loss_part, valid_count, patch_width):
    count, both_count = len(terms), len(terms) + len(first_terms)
    rows, columns = terms[0].shape
    split = first_terms[0].shape[1]

    def body(*refs):
        embed, square, loss, valid, rest, exchanged, totals = refs[both_count:]
        kept = add(*(ref[...] for ref in refs[:count]))
        rest[...] = kept
        sent = low(add(*(ref[...] for ref in refs[count:both_count])))
        exchanged[:, :split] = sent
        exchanged[:, split:] = embed[...]
        sent = sent.astype(FLOAT_TYPE)
        squares = sent * sent
        gathered = (
            square[...]
            + jnp.sum(kept * kept, keepdims=True)
            + jnp.sum(squares[:, :patch_width], keepdims=True)
            + 0.5 * jnp.sum(squares[:, patch_width:], keepdims=True)
        )
        loss = jnp.sum(loss[...], keepdims=True)
        totals[...] = jnp.where(
            lane_is(0), loss, jnp.where(lane_is(1), 0.25 * valid[...], jnp.where(lane_is(2), gathered, 0.0))
        )

    outs = [
        ((rows, columns), FLOAT_TYPE),
        ((rows, split + embed.shape[1]), NARROW_TYPE),
        ((1, LANES), FLOAT_TYPE),
    ]
    return vmem_call(
        body, outs, *terms, *first_terms, embed, square, loss_part, valid_count.reshape(1, 1)
    )


def adam_all(place, totals, masters, moments, seconds, sums, exchanged, norm_sum):
    orders = ((1, 0, 2), None, (1, 0, 2), (0, 2, 1))
    shapes = [array.shape for array in masters]

    def view(array, number):
        if number < 4:
            return array if orders[number] is None else array.transpose(orders[number])
        return array.reshape(-1, LANES) if array.ndim == 1 else array

    def unview(array, number):
        if number < 4 and orders[number] is not None:
            return array.transpose(np.argsort(orders[number]))
        return array.reshape(shapes[number])

    triples = [
        [view(array, number) for array in (masters[number], moments[number], seconds[number])]
        for number in range(8)
    ]
    flat = [array for triple in triples for array in triple]
    part_enc, part_dec = shapes[0][2], shapes[2][2]
    patch_rows, patch_width = shapes[4][0] // 2, shapes[4][1] // 2
    embed_width = shapes[5][1] // 4

    def body(place, totals, *refs):
        arrays, refs = refs[:24], refs[24:]
        (dec_attn, dec_tail, enc_tail, enc_attn, *parts, norm_sum), refs = refs[:9], refs[9:]
        scalars, outs = refs[0], refs[1:]
        loss, count, square = (
            jnp.sum(jnp.where(lane_is(n), totals[...], 0.0), keepdims=True) for n in range(3)
        )
        grad_norm = jnp.sqrt(square) / count
        factor = CLIP / jnp.maximum(grad_norm, CLIP) / count
        scalars[...] = jnp.where(lane_is(0), loss, jnp.where(lane_is(1), count, grad_norm))

        def update(number, where, grad):
            step_rate = LR_NORM if number == 7 else LR_MATRIX
            decay_rate = 0.0 if number == 7 else DECAY
            values = (ref[where] for ref in arrays[3 * number : 3 * number + 3])
            results = adam_update(*values, grad * factor, step_rate, decay_rate)
            for ref, result in zip(outs[3 * number : 3 * number + 3], results):
                ref[where] = result

        def piece(at_x, at_c, columns):
            far_x, far_c = place[0] != at_x, place[1] != at_c
            cuts = [part[:, columns] for part in parts]
            rows = [jnp.where(far_c, cuts[n + 1], cuts[n]) for n in (0, 2)]
            return jnp.where(far_x, rows[1], rows[0]).astype(FLOAT_TYPE)

        for number, attn, tail, width in (
            (0, enc_attn, enc_tail, part_enc),
            (2, dec_attn, dec_tail, part_dec),
        ):
            for block in range(7):
                source, first = (attn, block) if block < 3 else (tail, block - 3)
                update(number, block, source[:, first * width : (first + 1) * width])
            for block in range(5):
                source, first = (attn, 3) if block == 0 else (tail, 3 + block)
                grad = source[:, first * width : (first + 1) * width]
                update(number + 1, block, grad.T if number == 0 else grad)
        for at_x in (0, 1):
            for at_c in (0, 1):
                grad = piece(at_x, at_c, slice(0, patch_width))
                rows = slice(at_x * patch_rows, (at_x + 1) * patch_rows)
                columns = slice(at_c * patch_width, (at_c + 1) * patch_width)
                update(4, (rows, columns), grad)
                first = patch_width + LANES
                grad = piece(at_x, at_c, slice(first, first + embed_width))
                number = 2 * at_x + at_c
                update(5, (slice(None), slice(number * embed_width, (number + 1) * embed_width)), grad)
        update(6, Ellipsis, dec_tail[:, 8 * part_dec :])
        update(7, Ellipsis, norm_sum[...].astype(FLOAT_TYPE))

    outs = [((1, LANES), FLOAT_TYPE)] + [(array.shape, FLOAT_TYPE) for array in flat]
    scalars, *results = vmem_call(
        body, outs, totals, *flat, *sums, *exchanged, view(norm_sum, 7), scalars=(place,), room=WIDE_ROOM
    )
    return scalars, [unview(result, index // 3) for index, result in enumerate(results)]


def both(piece, axis, place, dimension):
    other = swap(piece, axis)
    return jnp.where(
        place == 0,
        jnp.concatenate([piece, other], dimension),
        jnp.concatenate([other, piece], dimension),
    )


def halves_of(array, place):
    half = array.shape[1] // 2
    return jnp.where(place == 0, array[:, :half], array[:, half:])


def one_hot(visible_row, tokens):
    return visible_row[:, None] == jnp.arange(tokens)[None, :]


def pick(array, index, axis=0):
    return lax.dynamic_index_in_dim(array, index, axis, keepdims=False)


def columns_of(blob, widths):
    pieces, start = [], 0
    for width in widths:
        pieces.append(blob[..., start : start + width])
        start += width
    return pieces


def on_device(
    pixels,
    visible,
    valid,
    row_dest,
    encoder_in,
    encoder_in_moment,
    encoder_in_second,
    encoder_out,
    encoder_out_moment,
    encoder_out_second,
    decoder_in,
    decoder_in_moment,
    decoder_in_second,
    decoder_out,
    decoder_out_moment,
    decoder_out_second,
    patch_embed,
    patch_embed_moment,
    patch_embed_second,
    decoder_embed,
    decoder_embed_moment,
    decoder_embed_second,
    pixel_head,
    pixel_head_moment,
    pixel_head_second,
    norm_params,
    norm_params_moment,
    norm_params_second,
):
    masters = [
        encoder_in,
        encoder_out,
        decoder_in,
        decoder_out,
        patch_embed,
        decoder_embed,
        pixel_head,
        norm_params,
    ]
    moments = [
        encoder_in_moment,
        encoder_out_moment,
        decoder_in_moment,
        decoder_out_moment,
        patch_embed_moment,
        decoder_embed_moment,
        pixel_head_moment,
        norm_params_moment,
    ]
    seconds = [
        encoder_in_second,
        encoder_out_second,
        decoder_in_second,
        decoder_out_second,
        patch_embed_second,
        decoder_embed_second,
        pixel_head_second,
        norm_params_second,
    ]
    x, c = lax.axis_index("x"), lax.axis_index("c")
    data_size = lax.axis_size("z") * lax.axis_size("y")
    slot_total, tokens, pix_width = pixels.shape
    vis_count = visible.shape[1]
    patch_positions = valid.shape[2]
    rows_enc, _, part_enc = encoder_in.shape
    rows_dec, _, part_dec = decoder_in.shape
    width_enc, width_dec = patch_embed.shape[1], decoder_embed.shape[1]
    enc_heads = HEADS_ENC // 4
    dec_heads = HEADS_DEC // 4

    patch_rows = patch_embed.shape[0] // 2
    half_enc, quarter_dec = width_enc // 2, width_dec // 4
    norm_share, norm_room = norm_params.shape[0], rows_enc * LANES
    place = jnp.stack([x, c])
    enc_in_blocks = encoder_in.transpose(1, 0, 2)
    first_blob = pack_first(place, enc_in_blocks, encoder_out, patch_embed, norm_params.reshape(-1, LANES))
    second_blob, third_blob = pack_rest(
        after(place, first_blob),
        enc_in_blocks,
        encoder_out,
        decoder_in.transpose(1, 0, 2),
        decoder_out.transpose(0, 2, 1),
        decoder_embed,
        pixel_head,
    )
    widths = (
        (half_enc, LANES, 3 * part_enc, part_enc),
        (4 * part_enc, 4 * part_enc, quarter_dec),
        (3 * part_dec, 4 * part_dec, part_dec, 4 * part_dec, pixel_head.shape[1]),
    )

    buf_rows = data_size * -(-(slot_total * vis_count) // data_size)
    alive = row_dest[:, 0] < buf_rows
    use_own = pick(alive, x)
    half_step = lax.axis_size("z") // 2

    def shown_of(visible_row):
        return jnp.any(one_hot(visible_row, tokens), axis=0).astype(FLOAT_TYPE)

    away = slot_total - 1 - x
    visible_moved = shift(pick(visible, away), "z", half_step)
    visible_row = jnp.where(use_own, pick(visible, x), visible_moved)

    seen, packs = [], []

    def pick_slots(mark):
        start = after(x, mark)
        own_slot, away_slot = pick(pixels, start), pick(pixels, slot_total - 1 - start)
        packs.extend((start, own_slot, away_slot))

        def seen_of(slot, rows):
            return low(product("vt,tp->vp", low(one_hot(pick(visible, slot), tokens)), rows))

        sent = halves_of(seen_of(away, away_slot), c)
        seen_away = both(shift(sent, "z", half_step), "c", c, 1)
        seen.append(jnp.where(use_own, seen_of(x, own_slot), seen_away))
        return sent

    def move_pack(marks):
        start, own_slot, away_slot = packs

        def pixels_of(slot, rows):
            place = after(c, marks[1])
            half = pix_width // 2
            cols = [halves_of(rows[:, first : first + half], place) for first in (0, half)]
            return jnp.concatenate(cols + [low(pick(valid, slot))], 1)

        seen.append(pixels_of(start, own_slot))
        away_pack = pixels_of(slot_total - 1 - start, away_slot)
        return shift(after(away_pack, marks[3]), "z", half_step)

    (first_all, second_all, third_all), marks, pack_moved = spread_all(
        (first_blob, second_blob, third_blob), widths, visible_moved, pick_slots, move_pack
    )
    seen_rows, own_pack = seen

    patch_all, norm_all, enc_qkv, enc_proj = first_all
    enc_up, enc_down, embed_all = second_all
    dec_qkv, dec_up, dec_proj, dec_down, head_all = third_all
    patch_all = patch_all.reshape(2, data_size, patch_rows, half_enc).transpose(1, 0, 2, 3)
    patch_all = patch_all.reshape(pix_width, half_enc)
    embed_other = swap(embed_all)
    embed_even = jnp.where(c == 0, embed_all, embed_other)
    embed_odd = jnp.where(c == 0, embed_other, embed_all)
    full_embed = jnp.concatenate([embed_even[0], embed_odd[0], embed_even[1], embed_odd[1]], 1)
    norm_full = norm_all[0].reshape(data_size, norm_room)[:, :norm_share].reshape(-1)
    norm_full = norm_full.astype(FLOAT_TYPE)
    enc_gains = norm_full[: 6 * width_enc].reshape(6, width_enc)
    dec_gains = norm_full[6 * width_enc : 6 * width_enc + 6 * width_dec].reshape(6, width_dec)
    mask_token = norm_full[6 * width_enc + 6 * width_dec : 6 * width_enc + 7 * width_dec]

    chosen = low(one_hot(visible_row, tokens))
    hidden_row = (1.0 - shown_of(visible_row))[:, None]

    visible_late = after(visible, marks[2])
    counted = jnp.stack([1.0 - shown_of(visible_late[slot]) for slot in range(slot_total)])
    counted = counted * alive.astype(FLOAT_TYPE)[:, None]
    valid_count = jnp.sum(counted[:, :, None] * valid.astype(FLOAT_TYPE))
    valid_count = valid_count * (pix_width // patch_positions)

    enc_stream = both(product("lp,pd->ld", seen_rows, patch_all), "c", c, 1)
    enc_stream = enc_stream + angles_of(visible_row, width_enc)
    partial, enc_triple, enc_mixture, enc_log = attn_fwd(
        enc_stream, enc_gains, enc_qkv, enc_proj, enc_heads
    )
    enc_middle, partial = mlp_fwd(enc_stream, partial, swap(partial), enc_gains, enc_up, enc_down)
    enc_last, enc_normed, dec_stream = between(
        enc_middle,
        partial,
        swap(partial),
        enc_gains,
        full_embed,
        chosen,
        hidden_row,
        mask_token[None],
        places_of(tokens, width_dec),
    )

    partial, dec_triple, dec_mixture, dec_log = attn_fwd(
        dec_stream, dec_gains, dec_qkv, dec_proj, dec_heads
    )
    dec_middle, partial = mlp_fwd(dec_stream, partial, swap(partial), dec_gains, dec_up, dec_down)

    pixel_pack = jnp.where(use_own, own_pack, after(pack_moved, dec_triple))
    pixel_cols = pixel_pack[:, : pix_width // 2].astype(FLOAT_TYPE)
    valid_cols = pixel_pack[:, pix_width // 2 :].astype(FLOAT_TYPE)
    half_mean = jnp.mean(pixel_cols, -1, keepdims=True)
    half_square = jnp.sum((pixel_cols - half_mean) ** 2, -1, keepdims=True)
    half_both = jnp.concatenate([half_mean, half_square], 1)
    other_both = swap(half_both)
    mean = 0.5 * (half_both[:, :1] + other_both[:, :1])
    gap = half_both[:, :1] - other_both[:, :1]
    variance = (half_both[:, 1:] + other_both[:, 1:]) / pix_width + 0.25 * gap * gap
    target = (pixel_cols - mean) * lax.rsqrt(variance + EPS_PIX)
    half_positions = patch_positions // 2
    front = jnp.where(c == 0, valid_cols[:, :half_positions], valid_cols[:, half_positions:])
    back = jnp.where(c == 0, valid_cols[:, half_positions:], valid_cols[:, :half_positions])
    part_mask = jnp.concatenate([front, back, front], 1) * hidden_row
    goal = jnp.stack([target[:, : pix_width // 4], target[:, pix_width // 4 :]])
    dec_last, dec_normed, pred_low, partial, loss_part = head_loss(
        dec_middle,
        partial,
        swap(partial),
        dec_gains,
        head_all,
        goal,
        part_mask,
    )

    stream_grad, grad_low, normed_low, hidden_low, upward_low, partial, dec_norms_three = mlp_back(
        (partial, swap(partial)), dec_last, dec_middle, dec_gains, dec_up, dec_down
    )
    dec_tail = Collect(
        share([(normed_low, upward_low), (grad_low, hidden_low), (dec_normed, pred_low)], rows_dec)
    )
    stream_grad, grad_low, normed_low, triple_grad, partial, dec_norms_two = attn_back(
        stream_grad,
        partial,
        swap(partial),
        dec_middle,
        dec_stream,
        (dec_triple, dec_log),
        dec_gains,
        dec_qkv,
        dec_proj,
        dec_heads,
    )
    normed_low = after(normed_low, *dec_tail.second(triple_grad))
    dec_attn = Collect(
        share([(normed_low, triple_grad), (grad_low, dec_mixture)], rows_dec), *dec_tail.late
    )
    embed_mine, normed_grad, mask_grad, dec_norms_one = decoder_end(
        stream_grad,
        partial,
        swap(partial),
        dec_stream,
        dec_gains,
        chosen,
        hidden_row,
        full_embed,
        c[None],
    )

    stream_grad, grad_low, normed_low, hidden_low, upward_low, partial, enc_norms_three = mlp_back(
        (after(normed_grad, *dec_attn.second(), *dec_tail.third()),), enc_last, enc_middle, enc_gains, enc_up, enc_down
    )
    enc_tail = Collect(
        share([(normed_low, upward_low), (grad_low, hidden_low), (enc_normed, embed_mine)], rows_enc),
        *dec_attn.late,
    )
    other_partial = after(swap(partial), *dec_attn.third(), *dec_tail.moved)
    stream_grad, grad_low, normed_low, triple_grad, partial, enc_norms_two = attn_back(
        stream_grad,
        partial,
        other_partial,
        enc_middle,
        enc_stream,
        (enc_triple, enc_log),
        enc_gains,
        enc_qkv,
        enc_proj,
        enc_heads,
    )
    enc_tail_late = enc_tail.second(triple_grad)
    normed_low = after(normed_low, *enc_tail_late)
    enc_attn = Collect(
        share([(normed_low, triple_grad), (grad_low, enc_mixture)], rows_enc), *enc_tail.late
    )
    other_partial = after(swap(partial), *enc_tail_late, *dec_attn.moved)
    patch_right, norm_grads = encoder_end(
        stream_grad,
        partial,
        other_partial,
        enc_stream,
        enc_gains,
        c[None],
        (enc_norms_two, enc_norms_three, dec_norms_one, dec_norms_two, dec_norms_three),
        mask_grad,
    )
    norm_half = norm_share // 2
    enc_attn_late = enc_attn.second()
    enc_first = Collect(
        share(
            [],
            rows_enc,
            (seen_rows, patch_right),
            norm_grads,
        ),
        *enc_attn_late,
    )

    enc_tail_sent = enc_tail.third()
    enc_attn_sent = enc_attn.third(*enc_tail_sent)
    enc_first_late = enc_first.second(*enc_tail.moved)
    early_sums, embed_sum, square = sum_early(
        [
            group.terms(*enc_attn_sent, *enc_first_late)
            for group in (dec_attn, dec_tail, enc_tail)
        ],
        quarter_dec,
    )
    enc_first_sent = enc_first.third()
    late_sum, exchanged, totals = sum_late(
        enc_attn.terms(*enc_first_sent), enc_first.terms(), embed_sum, square, loss_part, valid_count, half_enc
    )
    exchanged = [
        exchanged,
        swap(exchanged, "c"),
        swap(exchanged, "x"),
        lax.ppermute(exchanged, ("x", "c"), ACROSS),
    ]
    norm_cuts = [
        part[:, half_enc : half_enc + LANES].reshape(-1)[:norm_half]
        for part in (exchanged[0], exchanged[2])
    ]
    norm_sum = jnp.where(x == 0, jnp.concatenate(norm_cuts), jnp.concatenate(norm_cuts[::-1]))
    totals = total_over(totals, ("c", "x", "y"))
    totals, *exchanged = lax.optimization_barrier((totals, *exchanged))
    totals = total_over(totals, ("z",))
    scalars, updated = adam_all(
        jnp.stack([x, c]), totals, masters, moments, seconds, [*early_sums, late_sum], exchanged, norm_sum
    )
    return (scalars[0, 0], scalars[0, 1], scalars[0, 2], *updated)


def solution(mesh):
    data, model = mesh.shape["dp"], mesh.shape["mp"]
    inner = Mesh(mesh.devices.reshape(data // 2, 2, model // 2, 2), ("z", "y", "x", "c"))
    data_axes, model_axes = ("z", "y"), ("x", "c")
    rows = P(data_axes)
    into = P(data_axes, None, model_axes)
    out_of = P(None, model_axes, data_axes)
    head = P(data_axes, model_axes)
    weights = (into, out_of, into, out_of, rows, rows, head, rows)
    triples = tuple(spec for spec in weights for _ in range(3))
    return jax.shard_map(
        on_device,
        mesh=inner,
        in_specs=(rows, rows, rows, rows) + triples,
        out_specs=(P(), P(), P()) + triples,
        check_vma=False,
    )
```
